32 devices in a mesh: dp: 8 (over y, x, core), blk: 4 (over z).
Axes of the slice: x: 2, y: 2, z: 4, core: 2. Of those that a mesh axis runs over, the one named last changes fastest.
Arguments:
- token_ids: int32 [16384], P(('dp', 'blk')), may hold values from 0 to 831
- segment_ids: int32 [16384], P(('dp', 'blk')), may hold values from 0 to 3, as said below
- timesteps: int32 [16384], P(('dp', 'blk')), may hold values from 0 to 1999, as said below
- noise: float32 [16384, 16], P(('dp', 'blk')), may hold values from -6 to 6
- table: float32 [832, 16], P('dp')
- up_weight: bfloat16 [16, 768], replicated, may hold values from -1.5 to 1.5
- up_bias: float32 [768], replicated, may hold values from -1.75 to 1.75
- norm1_gain: float32 [768], replicated, may hold values from 0.5 to 1.5
- norm1_shift: float32 [768], replicated, may hold values from -1.75 to 1.75
- qkv_weight: bfloat16 [768, 2304], replicated, may hold values from -0.21875 to 0.21875
- query_bias: float32 [768], replicated, may hold values from -1.75 to 1.75
- value_bias: float32 [768], replicated, may hold values from -1.75 to 1.75
- out_weight: bfloat16 [768, 768], replicated, may hold values from -0.875 to 0.875
- out_bias: float32 [768], replicated, may hold values from -1.75 to 1.75
- norm2_gain: float32 [768], replicated, may hold values from 0.5 to 1.5
- norm2_shift: float32 [768], replicated, may hold values from -1.75 to 1.75
- ffn_in_weight: bfloat16 [768, 3072], replicated, may hold values from -0.21875 to 0.21875
- ffn_in_bias: float32 [3072], replicated, may hold values from -1.75 to 1.75
- ffn_out_weight: bfloat16 [3072, 768], replicated, may hold values from -0.109375 to 0.109375
- ffn_out_bias: float32 [768], replicated, may hold values from -1.75 to 1.75
- cotangent: float32 [16384, 768], P(('dp', 'blk')), may hold values from -6 to 6
Outputs:
- block_out: float32 [16384, 768], P(('dp', 'blk'))
- noise_grad: float32 [16384, 16], P(('dp', 'blk'))
- table_grad: float32 [832, 16], P('dp')
- up_weight_grad: float32 [16, 768], replicated
- up_bias_grad: float32 [768], replicated
- norm1_gain_grad: float32 [768], replicated
- norm1_shift_grad: float32 [768], replicated
- qkv_weight_grad: float32 [768, 2304], P(('dp', 'blk'))
- query_bias_grad: float32 [768], replicated
- value_bias_grad: float32 [768], replicated
- out_weight_grad: float32 [768, 768], P(('dp', 'blk'))
- out_bias_grad: float32 [768], replicated
- norm2_gain_grad: float32 [768], replicated
- norm2_shift_grad: float32 [768], replicated
- ffn_in_weight_grad: float32 [768, 3072], P(('dp', 'blk'))
- ffn_in_bias_grad: float32 [3072], replicated
- ffn_out_weight_grad: float32 [3072, 768], P(('dp', 'blk'))
- ffn_out_bias_grad: float32 [768], replicated
- mean_norm: float32 [], replicated
The draws below stay inside these ranges and needn't reach their ends.
Inputs may be any that keep to these rules, and one draw needn't show every extreme that they name: `segment_ids`: documents are numbered from 0 within each group of 2048 tokens (one index of dp) and lie end to end in the group's order, one to four of them a group, each a multiple of 64 tokens long. `timesteps`: equal for all tokens of one document.
All inputs are finite; a program needn't handle non-finite values.
Results may differ from the reference program's by a relative error of at most 0.017.
Values may be sent and summed in bfloat16 or wider, within the bound.
A program may use at most 192 MiB of HBM per device.

```python
import math
import jax
import jax.numpy as jnp
import numpy as np
from jax import lax

D = 768
HEADS = 12
HEAD_DIM = 64
FF = 3072
EMB = 16
VOCAB = 832
TSTEPS = 2000
SHORT = 64
GROUP = 2048
TOKENS = 16384
N_DP = 8


def doc_layout(key):
    base_key = jax.random.fold_in(key, 11)
    counts = jax.random.randint(jax.random.fold_in(base_key, 1), (N_DP,), 1, 5)
    chosen = jax.random.randint(jax.random.fold_in(base_key, 3), (), 0, N_DP)
    group_index = jnp.arange(N_DP, dtype=jnp.int32)
    counts = jnp.where(group_index == chosen, 1, counts)
    counts = jnp.where(group_index == (chosen + 1) % N_DP, 4, counts).astype(jnp.int32)
    candidates = (jnp.arange(1, GROUP // SHORT, dtype=jnp.int32) * SHORT).astype(jnp.int32)
    group_keys = jax.random.split(jax.random.fold_in(base_key, 5), N_DP)

    def one_group(group_key, count):
        order = jax.random.permutation(group_key, candidates)
        cuts = order[:3]
        valid = jnp.arange(3, dtype=jnp.int32) < count - 1
        place = jnp.arange(GROUP, dtype=jnp.int32)
        passed = valid[None, :] & (cuts[None, :] <= place[:, None])
        return jnp.sum(passed.astype(jnp.int32), axis=1).astype(jnp.int32)
    segments = jax.vmap(one_group)(group_keys, counts)
    return (segments.astype(jnp.int32), chosen)


def draw_segment_ids(key, part):
    segments, chosen = doc_layout(key)
    return segments.reshape(TOKENS)


def draw_timesteps(key, part):
    segments, chosen = doc_layout(key)
    key = jax.random.fold_in(key, 5)
    doc_count = 4
    doc_steps = jax.random.randint(key, (N_DP, doc_count), 0, TSTEPS)
    group_index = jnp.arange(N_DP, dtype=jnp.int32)[:, None]
    doc_index = jnp.arange(doc_count, dtype=jnp.int32)[None, :]
    first_doc = doc_index == 0
    doc_steps = jnp.where(first_doc & (group_index == chosen), TSTEPS - 1, doc_steps)
    doc_steps = jnp.where(first_doc & (group_index == (chosen + 1) % N_DP), 0, doc_steps)
    steps = jnp.take_along_axis(doc_steps, segments, axis=1)
    return steps.astype(jnp.int32).reshape(TOKENS)


def draw_table(key, part):
    key = jax.random.fold_in(key, 7)
    rising = 1.0 + 2.0 * jnp.arange(VOCAB, dtype=jnp.float32) / (VOCAB - 1)
    values = jax.random.truncated_normal(jax.random.fold_in(key, 1), -4.0, 4.0, (VOCAB, EMB), jnp.float32)
    return (values * rising[:, None]).astype(jnp.float32)


def touch_ends(values, rng, smallest, largest):
    spot = [jax.random.randint(jax.random.fold_in(rng, axis), (), 0, length) for axis, length in enumerate(values.shape)]
    longest = values.shape.index(max(values.shape))
    next_to = spot[:longest] + [(spot[longest] + 1) % values.shape[longest]] + spot[longest + 1:]
    return values.at[tuple(spot)].set(smallest).at[tuple(next_to)].set(largest)


def level_of(stream_key, extent, cuts, smallest, high):
    def one(position, blocks):
        heights = jax.random.uniform(jax.random.fold_in(jax.random.fold_in(stream_key, 6), position), (blocks,), jnp.float32, smallest / len(cuts), high / len(cuts))
        return jnp.repeat(jnp.exp(heights), extent[position] // blocks).reshape((-1,) + (1,) * (len(extent) - position - 1))

    factor_of = one(*cuts[0])
    for cut in cuts[1:]:
        factor_of = factor_of * one(*cut)
    return factor_of


def rank_bounds(number_of, slope):
    weights = [(1 << 20) // math.isqrt(grade ** slope) + 1 for grade in range(1, number_of + 1)]
    scale = 1 + sum(weights) // (1 << 30)
    return np.cumsum(np.array([max(1, weight // scale) for weight in weights]))


def ranked(stream_key, extent, count, lean):
    listing = rank_bounds(count, lean)
    lot = jax.random.randint(jax.random.fold_in(stream_key, 1), extent, 0, int(listing[count - 1]))
    standing = jnp.searchsorted(jnp.asarray(listing, jnp.int32), lot, side="right")
    return jax.random.permutation(jax.random.fold_in(stream_key, 2), count)[standing].astype(jnp.int32)


def normal_values(rng, shape, deviation, reach, cuts=(), kind=jnp.bfloat16):
    factor_of = level_of(rng, shape, cuts, -0.22, 0.18) if cuts else 1.0
    entries = jax.random.normal(rng, shape, jnp.float32) * deviation * factor_of
    return jnp.minimum(jnp.maximum(entries, -reach), reach).astype(kind)


def setup_inputs(seed: int = 0) -> dict:
    seeds = jax.random.split(jax.random.key(seed), 22)
    token_ids = touch_ends(ranked(seeds[0], (TOKENS,), VOCAB, 2), jax.random.fold_in(seeds[0], 3), 0, VOCAB - 1).astype(jnp.int32)
    segment_ids = draw_segment_ids(jax.random.fold_in(seeds[21], 71), 0)
    timesteps = draw_timesteps(jax.random.fold_in(seeds[21], 71), 0)
    noise = normal_values(seeds[3], (TOKENS, EMB), 1.0, 6.0, ((0, 32),), jnp.float32)
    table = draw_table(jax.random.fold_in(seeds[21], 71), 0)
    up_weight = normal_values(seeds[5], (EMB, D), EMB ** -0.5, 1.5)
    up_bias = normal_values(seeds[6], (D,), 0.3, 1.75, (), jnp.float32)
    norm1_gain = jnp.clip(1.0 + 0.1 * jax.random.normal(seeds[7], (D,), jnp.float32), 0.5, 1.5)
    norm1_shift = normal_values(seeds[8], (D,), 0.3, 1.75, (), jnp.float32)
    qkv_weight = normal_values(seeds[9], (D, 3 * D), D ** -0.5, 0.21875)
    query_bias = normal_values(seeds[10], (D,), 0.3, 1.75, (), jnp.float32)
    value_bias = normal_values(seeds[11], (D,), 0.3, 1.75, (), jnp.float32)
    out_weight = normal_values(seeds[12], (D, D), (D // 16) ** -0.5, 0.875)
    out_bias = normal_values(seeds[13], (D,), 0.3, 1.75, (), jnp.float32)
    norm2_gain = jnp.clip(1.0 + 0.1 * jax.random.normal(seeds[14], (D,), jnp.float32), 0.5, 1.5)
    norm2_shift = normal_values(seeds[15], (D,), 0.3, 1.75, (), jnp.float32)
    ffn_in_weight = normal_values(seeds[16], (D, FF), D ** -0.5, 0.21875)
    ffn_in_bias = normal_values(seeds[17], (FF,), 0.3, 1.75, (), jnp.float32)
    ffn_out_weight = normal_values(seeds[18], (FF, D), FF ** -0.5, 0.109375)
    ffn_out_bias = normal_values(seeds[19], (D,), 0.3, 1.75, (), jnp.float32)
    cotangent = normal_values(seeds[20], (TOKENS, D), 1.0, 6.0, ((0, 32),), jnp.float32)
    return dict(token_ids=token_ids, segment_ids=segment_ids, timesteps=timesteps, noise=noise, table=table, up_weight=up_weight, up_bias=up_bias, norm1_gain=norm1_gain, norm1_shift=norm1_shift, qkv_weight=qkv_weight, query_bias=query_bias, value_bias=value_bias, out_weight=out_weight, out_bias=out_bias, norm2_gain=norm2_gain, norm2_shift=norm2_shift, ffn_in_weight=ffn_in_weight, ffn_in_bias=ffn_in_bias, ffn_out_weight=ffn_out_weight, ffn_out_bias=ffn_out_bias, cotangent=cotangent)


@jax.custom_vjp
def low(v):
    return lax.optimization_barrier(v.astype(jnp.bfloat16)).astype(jnp.float32)

@jax.custom_vjp
def low_back(v):
    return v

def low_keep(v):
    return (low(v), None)

def low_pass(kept, grad):
    return (grad,)

def back_keep(v):
    return (v, None)

def back_low(kept, grad):
    return (low(grad),)
low.defvjp(low_keep, low_pass)
low_back.defvjp(back_keep, back_low)
highest = lax.Precision.HIGHEST

def product(left, right):
    return jnp.dot(left, right, precision=highest, preferred_element_type=jnp.float32)

def layer_norm(inputs, norm_gain, norm_shift):
    center = lax.optimization_barrier(jnp.mean(inputs, axis=-1, keepdims=True))
    centered = inputs - center
    spread = lax.optimization_barrier(jnp.mean(centered * centered, axis=-1, keepdims=True))
    return centered * lax.rsqrt(spread + 1e-05) * norm_gain + norm_shift

def sinusoid(steps_float, width):
    half_width = width // 2
    frequency = jnp.exp(-math.log(10000.0) * jnp.arange(half_width, dtype=jnp.float32) / half_width)
    angles = steps_float[:, None] * frequency[None, :]
    return jnp.concatenate([jnp.sin(angles), jnp.cos(angles)], axis=-1)

def group_attention(pieces):
    queries, keys, values, segments = pieces
    block_rows = math.gcd(GROUP, 512)
    count = GROUP // block_rows

    def block_attention(item):
        query_part, segment_part = item
        scores = jnp.einsum('qhd,khd->hqk', query_part, keys, precision=highest) * HEAD_DIM ** (-0.5)
        scores = low_back(scores)
        allowed = segment_part[None, :, None] == segments[None, None, :]
        scores = jnp.where(allowed, scores, -1e+30)
        probs = low(jax.nn.softmax(scores, axis=-1))
        return jnp.einsum('hqk,khd->qhd', probs, values, precision=highest)
    result = lax.map(jax.checkpoint(block_attention), (queries.reshape(count, block_rows, HEADS, HEAD_DIM), segments.reshape(count, block_rows)))
    return result.reshape(GROUP, HEADS, HEAD_DIM)

def reference(token_ids, segment_ids, timesteps, noise, table, up_weight, up_bias, norm1_gain, norm1_shift, qkv_weight, query_bias, value_bias, out_weight, out_bias, norm2_gain, norm2_shift, ffn_in_weight, ffn_in_bias, ffn_out_weight, ffn_out_bias, cotangent):
    steps_float = timesteps.astype(jnp.float32)
    alpha_bar = 1.0 - jnp.sqrt(steps_float / TSTEPS + 0.0001)
    signal_scale = jnp.sqrt(alpha_bar)[:, None]
    noise_scale = jnp.sqrt(1.0 - alpha_bar)[:, None]
    time_embed = sinusoid(steps_float, D)
    group_segments = segment_ids.reshape(N_DP, GROUP)

    def forward(params):
        noise_in, table_in, up_w, up_b, gain_one, shift_one, qkv_w, query_b, value_b, out_w, out_b, gain_two, shift_two, inner_w, inner_b, outer_w, outer_b = params
        row_norm = jnp.sqrt(lax.optimization_barrier(jnp.sum(table_in * table_in, axis=-1)) + 1.0)
        norm_value = jnp.mean(row_norm)
        embedded = table_in[token_ids] / norm_value
        mixed = low(signal_scale * embedded + noise_scale * noise_in)
        hidden0 = low_back(product(mixed, up_w) + up_b + time_embed)
        normed = low(layer_norm(hidden0, gain_one, shift_one))
        middle_zero = jnp.zeros((D,), jnp.float32)
        qkv = product(normed, qkv_w) + jnp.concatenate([query_b, middle_zero, value_b])
        qkv = low_back(low(qkv))
        queries = qkv[:, :D].reshape(N_DP, GROUP, HEADS, HEAD_DIM)
        keys = qkv[:, D:2 * D].reshape(N_DP, GROUP, HEADS, HEAD_DIM)
        values = qkv[:, 2 * D:].reshape(N_DP, GROUP, HEADS, HEAD_DIM)
        attended = lax.map(group_attention, (queries, keys, values, group_segments)).reshape(TOKENS, D)
        attended = low_back(low(attended))
        hidden1 = hidden0 + low_back(product(attended, out_w) + out_b)
        normed2 = low(layer_norm(hidden1, gain_two, shift_two))
        inner = low_back(product(normed2, inner_w) + inner_b)
        active = low(jax.nn.gelu(inner))
        result = hidden1 + low_back(product(active, outer_w) + outer_b)
        return (result, norm_value)
    params = (noise, table, up_weight.astype(jnp.float32), up_bias, norm1_gain, norm1_shift, qkv_weight.astype(jnp.float32), query_bias, value_bias, out_weight.astype(jnp.float32), out_bias, norm2_gain, norm2_shift, ffn_in_weight.astype(jnp.float32), ffn_in_bias, ffn_out_weight.astype(jnp.float32), ffn_out_bias)
    (block_out, mean_norm), pullback = jax.vjp(forward, params)
    grads = pullback((cotangent, jnp.zeros((), jnp.float32)))[0]
    noise_grad, table_grad, up_weight_grad, up_bias_grad, norm1_gain_grad, norm1_shift_grad, qkv_weight_grad, query_bias_grad, value_bias_grad, out_weight_grad, out_bias_grad, norm2_gain_grad, norm2_shift_grad, ffn_in_weight_grad, ffn_in_bias_grad, ffn_out_weight_grad, ffn_out_bias_grad = grads
    return (block_out, noise_grad, table_grad, up_weight_grad, up_bias_grad, norm1_gain_grad, norm1_shift_grad, qkv_weight_grad, query_bias_grad, value_bias_grad, out_weight_grad, out_bias_grad, norm2_gain_grad, norm2_shift_grad, ffn_in_weight_grad, ffn_in_bias_grad, ffn_out_weight_grad, ffn_out_bias_grad, mean_norm)
```

```python
import functools
import math

import jax
import jax.numpy as jnp
from jax import lax
from jax.experimental import pallas as pl
from jax.experimental.pallas import tpu as pltpu
from jax.sharding import PartitionSpec as P

D = 768
HEADS = 12
HEAD_DIM = 64
FF = 3072
EMB = 16
TSTEPS = 2000
DOCS = 4
PAIR = 2 * HEAD_DIM
SLOT = 256
EXT = 192
BIG = 1e30
SCALE = HEAD_DIM**-0.5
MIB = 2**20
MESH = pl.DeviceIdType.MESH
VMEM = pltpu.VMEM
f32 = jnp.float32
bf16 = jnp.bfloat16

NN = (((1,), (0,)), ((), ()))
NT = (((1,), (1,)), ((), ()))
TN = (((0,), (0,)), ((), ()))
TT = (((0,), (1,)), ((), ()))


def dot(left, right, dims=NN):
    return lax.dot_general(left, right, dims, preferred_element_type=f32)


def split3(x):
    high = x.astype(bf16)
    rest = x - high.astype(f32)
    middle = rest.astype(bf16)
    low = (rest - middle.astype(f32)).astype(bf16)
    return high.astype(f32), middle.astype(f32), low.astype(f32)


def column_sum(x):
    return jnp.sum(x, axis=0, keepdims=True)


def row_mean(x):
    return jnp.mean(x, axis=-1, keepdims=True)


def norm_parts(x):
    centered = x - row_mean(x)
    inverse = lax.rsqrt(row_mean(centered * centered) + 1e-05)
    return centered * inverse, inverse


def norm_pull(grad, unit, inverse, gain):
    scaled = grad * gain
    return inverse * (scaled - row_mean(scaled) - unit * row_mean(scaled * unit))


def onehot8(row):
    return (lax.broadcasted_iota(jnp.int32, (8, row.shape[1]), 0) == row.astype(jnp.int32)).astype(f32)


def id_matrix(rows, row):
    return (lax.broadcasted_iota(jnp.int32, (rows, row.shape[1]), 0) == row.astype(jnp.int32)).astype(f32).astype(bf16)


def params(**kw):
    return pltpu.CompilerParams(vmem_limit_bytes=60 * MIB, **kw)


def whole(shape):
    return pl.BlockSpec(shape, lambda *_: (0,) * len(shape))


def sync(peers):
    barrier = pltpu.get_barrier_semaphore()
    for peer in peers:
        pl.semaphore_signal(barrier, inc=1, device_id=peer, device_id_type=MESH)
    pl.semaphore_wait(barrier, len(peers))


def remote(src, dst, send, recv, peer):
    return pltpu.make_async_remote_copy(
        src_ref=src, dst_ref=dst, send_sem=send, recv_sem=recv, device_id=peer, device_id_type=MESH
    )


def gather_kernel(dp_n, blk_n, mine_ref, table_ref, tok_ref, tab_ref, send, recv):
    dp = lax.axis_index("dp")
    z = lax.axis_index("blk")
    dp_peers = [(lax.rem(dp + k, dp_n), z) for k in range(1, dp_n)]
    z_peers = [(dp, lax.rem(z + k, blk_n)) for k in range(1, blk_n)]
    sync(z_peers + dp_peers)
    copies = []
    for k, peer in enumerate(z_peers):
        copies.append(remote(mine_ref, tok_ref.at[z], send.at[k], recv.at[k], peer))
    for k, peer in enumerate(dp_peers):
        n = len(z_peers) + k
        copies.append(remote(table_ref, tab_ref.at[dp], send.at[n], recv.at[n], peer))
    for c in copies:
        c.start()
    tok_ref[z] = mine_ref[...]
    tab_ref[dp] = table_ref[...]
    for c in copies:
        c.wait()


def gather(mine, table, dp_n, blk_n):
    count = dp_n + blk_n - 2
    vmem = pl.BlockSpec(memory_space=VMEM)
    return pl.pallas_call(
        functools.partial(gather_kernel, dp_n, blk_n),
        in_specs=[vmem, vmem],
        out_specs=[vmem, vmem],
        out_shape=[
            jax.ShapeDtypeStruct((blk_n,) + mine.shape, f32),
            jax.ShapeDtypeStruct((dp_n,) + table.shape, f32),
        ],
        scratch_shapes=[pltpu.SemaphoreType.DMA((count,)), pltpu.SemaphoreType.DMA((count,))],
        compiler_params=params(collective_id=0, has_side_effects=True),
        name="gather",
    )(mine, table)


class Scatter:
    def __init__(self, grad, columns, by_x, acc, first, second, third, send, recv, local):
        self.grad, self.columns, self.by_x = grad, columns, by_x
        self.acc, self.first, self.second, self.third = acc, first, second, third
        self.send, self.recv, self.local = send, recv, local
        self.dp = lax.axis_index("dp")
        self.z = lax.axis_index("blk")
        self.core = lax.rem(self.dp, 2)
        self.x = lax.rem(lax.div(self.dp, 2), 2)
        self.y = lax.div(self.dp, 4)

    def flip(self, bit, step):
        return (self.dp + step * (1 - 2 * bit), self.z)

    def core_copies(self):
        src = self.grad.at[:, :, 1 - self.core, :, self.columns]
        own = self.grad.at[:, :, self.core, :, self.columns]
        return (
            remote(src, self.first, self.send.at[0], self.recv.at[0], self.flip(self.core, 1)),
            pltpu.make_async_copy(own, self.acc, self.local),
        )

    def wide(self):
        if self.by_x:
            src, peer = self.acc.at[:, 1 - self.x], self.flip(self.x, 2)
        else:
            src, peer = self.acc.at[1 - self.y], self.flip(self.y, 4)
        return remote(src, self.second, self.send.at[1], self.recv.at[1], peer)

    def narrow(self):
        if self.by_x:
            src, peer = self.acc.at[1 - self.y, self.x], self.flip(self.y, 4)
        else:
            src, peer = self.acc.at[self.y, 1 - self.x], self.flip(self.x, 2)
        return remote(src, self.third, self.send.at[2], self.recv.at[2], peer)

    def start(self):
        for c in self.core_copies():
            c.start()

    def core_to_wide(self):
        for c in self.core_copies():
            c.wait()
        for y in range(2):
            for x in range(2):
                self.acc[y, x] = (self.acc[y, x].astype(f32) + self.first[y, x].astype(f32)).astype(bf16)
        self.wide().start()

    def wide_to_narrow(self):
        self.wide().wait()
        for n in range(2):
            at = (n, self.x) if self.by_x else (self.y, n)
            self.acc[at] = (self.acc[at].astype(f32) + self.second[n].astype(f32)).astype(bf16)
        self.narrow().start()

    def narrow_sum(self):
        self.narrow().wait()
        return self.acc[self.y, self.x].astype(f32) + self.third[...].astype(f32)


def scatter_scratch(rows, columns):
    return [
        VMEM((2, 2, rows, columns), bf16),
        VMEM((2, 2, rows, columns), bf16),
        VMEM((2, rows, columns), bf16),
        VMEM((rows, columns), bf16),
        pltpu.SemaphoreType.DMA((3,)),
        pltpu.SemaphoreType.DMA((3,)),
        pltpu.SemaphoreType.DMA,
    ]


class LineScatter:
    def __init__(self, base, out, half, first, rest, second, send, recv):
        self.base, self.out = base, out
        self.half, self.first, self.rest, self.second = half, first, rest, second
        self.send, self.recv = send, recv
        self.low = lax.rem(base.z, 2)
        self.high = lax.div(base.z, 2)

    def near(self):
        peer = (self.base.dp, self.base.z + 1 - 2 * self.low)
        return remote(self.half.at[1 - self.low], self.first, self.send.at[0], self.recv.at[0], peer)

    def far(self):
        peer = (self.base.dp, self.base.z + 2 - 4 * self.high)
        return remote(self.rest.at[1 - self.high], self.second, self.send.at[1], self.recv.at[1], peer)

    def start(self):
        total = self.base.narrow_sum()
        q = total.shape[0] // 4
        for low in range(2):
            self.half[low, :q] = total[low * q : (low + 1) * q].astype(bf16)
            self.half[low, q:] = total[(2 + low) * q : (3 + low) * q].astype(bf16)
        self.near().start()

    def near_to_far(self):
        self.near().wait()
        q = self.rest.shape[1]
        total = self.half[self.low].astype(f32) + self.first[...].astype(f32)
        self.rest[0] = total[:q]
        self.rest[1] = total[q:]
        self.far().start()

    def finish(self):
        self.far().wait()
        self.out[:, self.base.columns] = self.rest[self.high] + self.second[...]


def line_scratch(rows, columns):
    return [
        VMEM((2, rows // 2, columns), bf16),
        VMEM((rows // 2, columns), bf16),
        VMEM((2, rows // 4, columns), f32),
        VMEM((rows // 4, columns), f32),
        pltpu.SemaphoreType.DMA((2,)),
        pltpu.SemaphoreType.DMA((2,)),
    ]


UNITS = (
    (0, 0, 384, True),
    (0, 384, 384, False),
    (1, 0, 768, True),
    (1, 768, 768, False),
    (1, 1536, 768, True),
    (1, 2304, 768, False),
    (2, 0, 384, True),
    (2, 384, 384, False),
)
UNIT_ROWS = (384, 96, 96)


def embed_kernel(
    local_rows,
    z_ref,
    tok_ref,
    tab_ref,
    up_w_ref,
    vec_ref,
    w_ref,
    own_w_ref,
    own_b_ref,
    k_ref,
    vt_ref,
    own_ref,
    normed_ref,
    lhs_ref,
    sc_ref,
    qt_ref,
    h0_ref,
    rhs_ref,
    mean_ref,
    tab3,
    vcol,
):
    i = pl.program_id(0)
    dp_n, _, vp = tab_ref.shape
    blocks, _, rows = tok_ref.shape

    @pl.when(i == 0)
    def _():
        table = jnp.concatenate([tab_ref[j] for j in range(dp_n)], axis=1)
        squares = jnp.sum(table * table, axis=0, keepdims=True)
        lane = lax.broadcasted_iota(jnp.int32, squares.shape, 1)
        norms = jnp.where(lane % vp < local_rows, jnp.sqrt(squares + 1.0), 0.0)
        mean_ref[...] = jnp.broadcast_to(jnp.sum(norms, axis=1, keepdims=True) / (local_rows * dp_n), (8, 128))
        tab3[...] = jnp.concatenate(split3(table), axis=0).astype(bf16)
        segments = tok_ref[:, 17, :]
        steps = tok_ref[:, 18, :]
        sub = lax.broadcasted_iota(jnp.int32, (8, 1), 0)
        time = jnp.zeros((8, 1), f32)
        for s in range(DOCS):
            own = jnp.max(jnp.where(segments == float(s), steps, 0.0), axis=(0, 1), keepdims=True)
            time = jnp.where(sub == s, own, time)
        lane = lax.broadcasted_iota(jnp.int32, (8, D), 1)
        half = D // 2
        index = jnp.where(lane < half, lane, lane - half).astype(f32)
        angle = time * jnp.exp(index * (-math.log(10000.0) / half))
        wave = jnp.where(lane < half, jnp.sin(angle), jnp.cos(angle)) + vec_ref[0:1, :]
        parts = split3(wave)
        rhs_ref[...] = jnp.concatenate([up_w_ref[...].astype(f32), *parts, jnp.zeros((8, D), f32)], axis=0).astype(bf16)
        bias = jnp.concatenate([vec_ref[3:5, :], jnp.zeros((6, D), f32)], axis=0)
        vcol[...] = jnp.transpose(bias)

    tok = tok_ref[i]
    ids = tok[16:17, :]
    picked3 = dot(tab3[...], id_matrix(dp_n * vp, ids))
    picked = picked3[:16] + picked3[16:32] + picked3[32:48]
    mean = mean_ref[0:1, 0:1]
    alpha_bar = 1.0 - jnp.sqrt(tok[18:19, :] / TSTEPS + 0.0001)
    signal = jnp.sqrt(alpha_bar)
    noise_scale = jnp.sqrt(1.0 - alpha_bar)
    mixed = signal * (picked / mean) + noise_scale * tok[:16]
    seg = onehot8(tok[17:18, :])
    lhs = jnp.concatenate([mixed, seg, seg, seg, jnp.zeros((8, rows), f32)], axis=0).astype(bf16)
    lhs_ref[0] = lhs
    sc_ref[0] = jnp.concatenate([picked, signal, noise_scale, jnp.zeros((6, rows), f32)], axis=0)
    hidden0 = dot(lhs, rhs_ref[...], TN)
    unit, _ = norm_parts(hidden0)
    normed = (unit * vec_ref[1:2, :] + vec_ref[2:3, :]).astype(bf16)
    normed_ref[...] = normed
    k_ref[...] = dot(normed, w_ref[:, D : 2 * D]).astype(bf16)
    vt_ref[...] = (dot(w_ref[:, 2 * D :], normed, TT) + vcol[:, 1:2]).astype(bf16)
    own = dot(normed, own_w_ref[...]) + own_b_ref[...]
    own_ref[:, :SLOT] = (own[:, :SLOT] * SCALE).astype(bf16)
    own_ref[:, SLOT:] = own[:, SLOT:].astype(bf16)

    @pl.when(i == z_ref[0])
    def _():
        h0_ref[...] = hidden0
        q = (dot(w_ref[:, :D], normed, TT) + vcol[:, 0:1]).astype(bf16)
        qt_ref[...] = (q.astype(f32) * SCALE).astype(bf16)


def embed(z, tok, tab, up_w, vec, w, own_w, own_b, local_rows):
    blocks, _, rows = tok.shape
    group = blocks * rows
    vocab = tab.shape[0] * tab.shape[2]
    spec = pltpu.PrefetchScalarGridSpec(
        num_scalar_prefetch=1,
        grid=(blocks,),
        in_specs=[whole(x.shape) for x in (tok, tab, up_w, vec, w, own_w, own_b)],
        out_specs=[
            pl.BlockSpec((rows, D), lambda i, z: (i, 0)),
            pl.BlockSpec((D, rows), lambda i, z: (0, i)),
            pl.BlockSpec((rows, 3 * SLOT), lambda i, z: (i, 0)),
            pl.BlockSpec((rows, D), lambda i, z: (i, 0)),
            pl.BlockSpec((1, 48, rows), lambda i, z: (i, 0, 0)),
            pl.BlockSpec((1, 24, rows), lambda i, z: (i, 0, 0)),
            whole((D, rows)),
            whole((rows, D)),
            whole((48, D)),
            whole((8, 128)),
        ],
        scratch_shapes=[VMEM((48, vocab), bf16), VMEM((D, 8), f32)],
    )
    return pl.pallas_call(
        functools.partial(embed_kernel, local_rows),
        grid_spec=spec,
        out_shape=[
            jax.ShapeDtypeStruct((group, D), bf16),
            jax.ShapeDtypeStruct((D, group), bf16),
            jax.ShapeDtypeStruct((group, 3 * SLOT), bf16),
            jax.ShapeDtypeStruct((group, D), bf16),
            jax.ShapeDtypeStruct((blocks, 48, rows), bf16),
            jax.ShapeDtypeStruct((blocks, 24, rows), f32),
            jax.ShapeDtypeStruct((D, rows), bf16),
            jax.ShapeDtypeStruct((rows, D), f32),
            jax.ShapeDtypeStruct((48, D), bf16),
            jax.ShapeDtypeStruct((8, 128), f32),
        ],
        compiler_params=params(),
        name="embed",
    )(z, tok, tab, up_w, vec, w, own_w, own_b)


ROOT = math.sqrt(2.0 / math.pi)


def layer_kernel(
    per,
    tok_ref,
    mine_ref,
    k_ref,
    vt_ref,
    qt_ref,
    h0_ref,
    cot_ref,
    vec_ref,
    b1_ref,
    wo_ref,
    w1_ref,
    w2_ref,
    out_ref,
    h1g_ref,
    msg_ref,
    dwo_ref,
    dw1_ref,
    dw2_ref,
    small_ref,
    kext,
    qext,
    att,
    lse,
    wo,
    wo_slots,
    w1,
    w2,
    sems,
):
    p = pl.program_id(0)
    last = pl.num_programs(0) - 1
    blocks, _, rows = tok_ref.shape
    copies = [
        pltpu.make_async_copy(wo_ref, wo, sems.at[0]),
        pltpu.make_async_copy(w1_ref, w1, sems.at[1]),
        pltpu.make_async_copy(w2_ref, w2, sems.at[2]),
    ]

    @pl.when(p == 0)
    def _():
        for c in copies:
            c.start()
        for b in range(blocks):
            seg = jnp.concatenate([onehot8(tok_ref[b, 17:18, :]), jnp.zeros((120, rows), f32)], axis=0)
            kext[b * rows : (b + 1) * rows, :] = jnp.transpose(seg).astype(bf16)
        seg = onehot8(mine_ref[17:18, :])
        sub = lax.broadcasted_iota(jnp.int32, seg.shape, 0)
        barred = jnp.where(sub < DOCS, -BIG * (1.0 - seg), 0.0)
        qext[...] = jnp.concatenate([barred, jnp.zeros((120, rows), f32)], axis=0).astype(bf16)

    keys = jnp.concatenate([k_ref[...], kext[...]], axis=1)
    zeros = jnp.zeros((HEAD_DIM, rows), bf16)
    ones = jnp.ones((HEAD_DIM, blocks * rows), bf16)
    results = []
    for h in range(2):
        q = qt_ref[h * HEAD_DIM : (h + 1) * HEAD_DIM, :]
        v = vt_ref[h * HEAD_DIM : (h + 1) * HEAD_DIM, :]
        queries = jnp.concatenate([q, zeros, qext[...]] if h == 0 else [zeros, q, qext[...]], axis=0)
        scores = dot(keys, queries)
        top = jnp.max(scores, axis=0, keepdims=True)
        weights = jnp.exp(scores - top).astype(bf16)
        total = dot(jnp.concatenate([v, ones], axis=0), weights)
        results.append(total[:HEAD_DIM] / total[HEAD_DIM:])
        lse[pl.ds(2 * p + h, 1), :] = top + jnp.log(total[HEAD_DIM : HEAD_DIM + 1])
    att[pl.ds(pl.multiple_of(p * PAIR, PAIR), PAIR), :] = jnp.concatenate(results, axis=0)

    @pl.when(p == last)
    def _():
        for c in copies:
            c.wait()
        attended = att[...].astype(bf16)
        hidden1 = h0_ref[...] + dot(attended, wo[...], TN) + vec_ref[0:1, :]
        unit, inverse = norm_parts(hidden1)
        normed2 = (unit * vec_ref[1:2, :] + vec_ref[2:3, :]).astype(bf16)
        cot = cot_ref[...]
        out_grad = cot.astype(bf16)
        block_out = hidden1 + vec_ref[3:4, :]
        norm_grad = jnp.zeros_like(hidden1)
        inner_sums = []
        for c in range(FF // D):
            cols = slice(c * D, (c + 1) * D)
            x = dot(normed2, w1[:, cols]) + b1_ref[c : c + 1, :]
            square = x * x
            t = jnp.tanh(x * (ROOT + (ROOT * 0.044715) * square))
            half = 0.5 * (1.0 + t)
            active = (x * half).astype(bf16)
            slope = half + (0.5 * x) * (1.0 - t * t) * (ROOT + (3.0 * ROOT * 0.044715) * square)
            block_out = block_out + dot(active, w2[cols, :])
            inner_grad = (dot(out_grad, w2[cols, :], NT) * slope).astype(bf16)
            dw2_ref[cols, :] = dot(active, out_grad, TN).astype(bf16)
            dw1_ref[:, cols] = dot(normed2, inner_grad, TN).astype(bf16)
            norm_grad = norm_grad + dot(inner_grad, w1[:, cols], NT)
            inner_sums.append(column_sum(inner_grad.astype(f32)))
        out_ref[...] = block_out
        hidden1_grad = cot + norm_pull(norm_grad, unit, inverse, vec_ref[1:2, :])
        h1g_ref[...] = hidden1_grad
        branch = hidden1_grad.astype(bf16)
        dwo_ref[...] = dot(attended, branch).astype(bf16)
        small_ref[...] = jnp.concatenate(
            [
                column_sum(branch.astype(f32)),
                column_sum(norm_grad * unit),
                column_sum(norm_grad),
                column_sum(out_grad.astype(f32)),
                *inner_sums,
            ],
            axis=0,
        )
        seg = onehot8(mine_ref[17:18, :])
        back = dot(wo[...], branch, NT).astype(bf16).astype(f32)
        product = back * att[...]
        for j in range(blocks):
            heads = [h for h in range(per * j, per * (j + 1)) if h < HEADS]
            wo_slots[...] = jnp.zeros_like(wo_slots)
            size = len(heads) * HEAD_DIM
            rows_ext = [jnp.zeros((HEAD_DIM, rows), f32), jnp.where(
                lax.broadcasted_iota(jnp.int32, (8, rows), 0) < DOCS, -BIG * (1.0 - seg), 0.0
            )[:DOCS]]
            lse_parts = []
            delta_parts = []
            for n in range(3):
                h = per * j + n
                if n < per and h < HEADS:
                    delta = column_sum(product[h * HEAD_DIM : (h + 1) * HEAD_DIM])
                    lse_parts += split3(-lse[h : h + 1, :])
                    delta_parts += split3(-delta)
                else:
                    lse_parts += [jnp.zeros((1, rows), f32)] * 3
                    delta_parts += [jnp.zeros((1, rows), f32)] * 3
            used = DOCS + 18
            rows_ext = rows_ext + lse_parts + delta_parts + [jnp.zeros((HEAD_DIM - used, rows), f32)]
            ext = jnp.transpose(jnp.concatenate(rows_ext, axis=0))
            if size:
                wo_slots[:size, :] = wo[heads[0] * HEAD_DIM : heads[0] * HEAD_DIM + size, :]
            grads = dot(branch, wo_slots[...], NT)
            msg_ref[j, :, :PAIR] = grads[:, :PAIR].astype(bf16)
            msg_ref[j, :, PAIR:] = (grads[:, PAIR:] + ext).astype(bf16)


def layer(tok, mine, k, vt, qt, h0, cot, vec, b1, wo, w1, w2, per):
    blocks, _, rows = tok.shape
    group = blocks * rows
    any_spec = pl.BlockSpec(memory_space=pl.ANY)
    return pl.pallas_call(
        functools.partial(layer_kernel, per),
        grid=(HEADS // 2,),
        in_specs=[
            whole(tok.shape),
            whole(mine.shape),
            pl.BlockSpec((group, PAIR), lambda p: (0, p)),
            pl.BlockSpec((PAIR, group), lambda p: (p, 0)),
            pl.BlockSpec((PAIR, rows), lambda p: (p, 0)),
            whole(h0.shape),
            whole(cot.shape),
            whole(vec.shape),
            whole(b1.shape),
            any_spec,
            any_spec,
            any_spec,
        ],
        out_specs=[
            whole((rows, D)),
            whole((rows, D)),
            whole((blocks, rows, SLOT)),
            whole((D, D)),
            whole((D, FF)),
            whole((FF, D)),
            whole((8, D)),
        ],
        out_shape=[
            jax.ShapeDtypeStruct((rows, D), f32),
            jax.ShapeDtypeStruct((rows, D), f32),
            jax.ShapeDtypeStruct((blocks, rows, SLOT), bf16),
            jax.ShapeDtypeStruct((D, D), bf16),
            jax.ShapeDtypeStruct((D, FF), bf16),
            jax.ShapeDtypeStruct((FF, D), bf16),
            jax.ShapeDtypeStruct((8, D), f32),
        ],
        scratch_shapes=[
            VMEM((group, PAIR), bf16),
            VMEM((PAIR, rows), bf16),
            VMEM((D, rows), f32),
            VMEM((16, rows), f32),
            VMEM((D, D), bf16),
            VMEM((SLOT, D), bf16),
            VMEM((D, FF), bf16),
            VMEM((FF, D), bf16),
            pltpu.SemaphoreType.DMA((3,)),
        ],
        compiler_params=params(),
        name="layer",
    )(tok, mine, k, vt, qt, h0, cot, vec, b1, wo, w1, w2)


def back_prepare(per, tok_ref, own_ref, kt, vt, ksel):
    blocks, _, rows = tok_ref.shape
    for b in range(blocks):
        place = slice(b * rows, (b + 1) * rows)
        seg = onehot8(tok_ref[b, 17:18, :])
        sub = lax.broadcasted_iota(jnp.int32, (HEAD_DIM, rows), 0)
        seg64 = jnp.concatenate([seg, jnp.zeros((HEAD_DIM - 8, rows), f32)], axis=0)
        kb = own_ref[place, SLOT : 2 * SLOT]
        kt_b = jnp.transpose(kb.astype(f32))
        vt_b = jnp.transpose(own_ref[place, 2 * SLOT :].astype(f32))
        lane = lax.broadcasted_iota(jnp.int32, kb.shape, 1)
        row = lax.broadcasted_iota(jnp.int32, kt_b.shape, 0)
        for h in range(per):
            inside = (row >= h * HEAD_DIM) & (row < (h + 1) * HEAD_DIM)
            first = DOCS + 3 * h
            k_ext = jnp.where((sub >= first) & (sub < first + 3), 1.0, jnp.where(sub < DOCS, seg64, 0.0))
            first = DOCS + 9 + 3 * h
            v_ext = jnp.where((sub >= first) & (sub < first + 3), 1.0, 0.0)
            kt[h, :, place] = jnp.concatenate([jnp.where(inside, kt_b, 0.0)[:EXT], k_ext], axis=0).astype(bf16)
            vt[h, :, place] = jnp.concatenate([jnp.where(inside, vt_b, 0.0)[:EXT], v_ext], axis=0).astype(bf16)
            mine = (lane >= h * HEAD_DIM) & (lane < (h + 1) * HEAD_DIM)
            ksel[h, place, :] = jnp.where(mine, kb.astype(f32), 0.0).astype(bf16)


def back_block(per, q, msg, kt, vt, ksel, dkt, dvt):
    lane = lax.broadcasted_iota(jnp.int32, q.shape, 1)
    queries = jnp.where(lane < EXT, q.astype(f32), msg.astype(f32)).astype(bf16)
    q_t = jnp.transpose(q.astype(f32)).astype(bf16)
    m_t = jnp.transpose(msg.astype(f32)).astype(bf16)
    dq = jnp.zeros(q.shape, f32)
    for h in range(per):
        head = slice(h * HEAD_DIM, (h + 1) * HEAD_DIM)
        probs = jnp.exp(dot(queries, kt[h]))
        score_grad = (probs * dot(msg, vt[h])).astype(bf16)
        dvt[head, :] += dot(m_t[head], probs.astype(bf16))
        dkt[head, :] += dot(q_t[head], score_grad)
        dq = dq + dot(score_grad, ksel[h])
    return (dq * SCALE).astype(bf16)


def back_kernel(per, tok_ref, own_ref, msg_ref, grad_ref, kt, vt, ksel, dkt, dvt):
    blocks, _, rows = tok_ref.shape
    back_prepare(per, tok_ref, own_ref, kt, vt, ksel)
    dkt[...] = jnp.zeros_like(dkt)
    dvt[...] = jnp.zeros_like(dvt)

    def step(b, carry):
        place = pl.ds(pl.multiple_of(b * rows, rows), rows)
        grad_ref[place, :SLOT] = back_block(per, own_ref[place, :SLOT], msg_ref[b], kt, vt, ksel, dkt, dvt)
        return carry

    lax.fori_loop(0, blocks, step, 0)
    for b in range(blocks):
        place = slice(b * rows, (b + 1) * rows)
        grad_ref[place, SLOT : 2 * SLOT] = jnp.transpose(dkt[:, place]).astype(bf16)
        grad_ref[place, 2 * SLOT :] = jnp.transpose(dvt[:, place]).astype(bf16)


def back(tok, own, msg, per):
    group = own.shape[0]
    return pl.pallas_call(
        functools.partial(back_kernel, per),
        in_specs=[pl.BlockSpec(memory_space=VMEM)] * 3,
        out_specs=pl.BlockSpec(memory_space=VMEM),
        out_shape=jax.ShapeDtypeStruct(own.shape, bf16),
        scratch_shapes=[
            VMEM((per, SLOT, group), bf16),
            VMEM((per, SLOT, group), bf16),
            VMEM((per, group, SLOT), bf16),
            VMEM((SLOT, group), f32),
            VMEM((SLOT, group), f32),
        ],
        compiler_params=params(),
        name="attention_back",
    )(tok, own, msg)


def back_scatter_kernel(
    per, plan, tok_ref, own_ref, msg_ref, dw2_ref, dw1_ref, dwo_ref, grad_ref, dw2_out, dw1_out, dwo_out,
    kt, vt, ksel, dkt, dvt, msgs, msg_send, msg_recv, *scratch
):
    blocks, _, rows = tok_ref.shape
    dp = lax.axis_index("dp")
    z = lax.axis_index("blk")
    grads = (dw2_ref, dw1_ref, dwo_ref)
    outs = (dw2_out, dw1_out, dwo_out)
    units = []
    for n, (which, first, size, by_x) in enumerate(UNITS):
        part = scratch[13 * n : 13 * (n + 1)]
        base = Scatter(grads[which], pl.ds(first, size), by_x, *part[:7])
        units.append((base, LineScatter(base, outs[which], *part[7:])))
    core, x, y = units[0][0].core, units[0][0].x, units[0][0].y

    def z_peer(k):
        low, high = lax.rem(z, 2), lax.div(z, 2)
        return (low + (k % 2) * (1 - 2 * low)) + 2 * (high + (k // 2) * (1 - 2 * high))

    base = units[0][0]
    sync([base.flip(core, 1), base.flip(x, 2), base.flip(y, 4)] + [(dp, z_peer(k)) for k in range(1, blocks)])

    def message(k):
        return remote(msg_ref.at[z_peer(k)], msgs.at[k], msg_send.at[k], msg_recv.at[k], (dp, z_peer(k)))

    for k in (1, 2, 3):
        message(k).start()

    def run(step):
        kind, n = step
        base, line = units[n]
        if kind == 0:
            base.start()
        elif kind == 1:
            base.core_to_wide()
        elif kind == 2:
            base.wide_to_narrow()
        elif kind == 3:
            line.start()
        elif kind == 4:
            line.near_to_far()
        else:
            line.finish()

    for step in plan[0]:
        run(step)
    back_prepare(per, tok_ref, own_ref, kt, vt, ksel)
    dkt[...] = jnp.zeros_like(dkt)
    dvt[...] = jnp.zeros_like(dvt)
    msgs[0] = msg_ref[z]
    for step in plan[1]:
        run(step)

    def body(b, carry):
        low, high = lax.rem(z, 2), lax.div(z, 2)
        b_low, b_high = lax.rem(b, 2), lax.div(b, 2)
        other = (low + b_low * (1 - 2 * low)) + 2 * (high + b_high * (1 - 2 * high))
        for k in range(1, blocks):

            @pl.when(b == k)
            def _():
                message(k).wait()

        for k in range(blocks):
            if plan[2 + k]:

                @pl.when(b == k)
                def _():
                    for step in plan[2 + k]:
                        run(step)

        place = pl.ds(pl.multiple_of(other * rows, rows), rows)
        grad_ref[place, :SLOT] = back_block(per, own_ref[place, :SLOT], msgs[b], kt, vt, ksel, dkt, dvt)
        return carry

    lax.fori_loop(0, blocks, body, 0)
    for step in plan[6]:
        run(step)
    for b in range(blocks):
        place = slice(b * rows, (b + 1) * rows)
        grad_ref[place, SLOT : 2 * SLOT] = jnp.transpose(dkt[:, place]).astype(bf16)
        grad_ref[place, 2 * SLOT :] = jnp.transpose(dvt[:, place]).astype(bf16)
    for step in plan[7]:
        run(step)


ALL = range(8)
PLAN = (
    [(0, n) for n in ALL],
    [(1, n) for n in (0, 1)],
    [(1, n) for n in range(2, 8)],
    [],
    [(2, 0), (2, 1)],
    [(2, 2), (2, 3), (3, 0), (3, 1)],
    [(2, 4), (2, 5), (4, 0), (4, 1), (3, 2), (3, 3), (2, 6), (2, 7)],
    [(3, 4), (3, 5), (5, 0), (5, 1), (4, 2), (4, 3), (3, 6), (3, 7), (4, 4), (4, 5), (4, 6), (4, 7)]
    + [(5, n) for n in range(2, 8)],
)


def back_scatter(tok, own, msg, dw2, dw1, dwo, per):
    blocks, rows = msg.shape[:2]
    group = own.shape[0]
    vmem = pl.BlockSpec(memory_space=VMEM)
    hbm = pl.BlockSpec(memory_space=pl.ANY)
    scratch = []
    for which, _, size, _ in UNITS:
        scratch += scatter_scratch(UNIT_ROWS[which], size) + line_scratch(UNIT_ROWS[which], size)
    return pl.pallas_call(
        functools.partial(back_scatter_kernel, per, PLAN),
        in_specs=[vmem] * 3 + [hbm] * 3,
        out_specs=[vmem] * 4,
        out_shape=[
            jax.ShapeDtypeStruct(own.shape, bf16),
            jax.ShapeDtypeStruct((96, D), f32),
            jax.ShapeDtypeStruct((24, FF), f32),
            jax.ShapeDtypeStruct((24, D), f32),
        ],
        scratch_shapes=[
            VMEM((per, SLOT, group), bf16),
            VMEM((per, SLOT, group), bf16),
            VMEM((per, group, SLOT), bf16),
            VMEM((SLOT, group), f32),
            VMEM((SLOT, group), f32),
            VMEM((blocks, rows, SLOT), bf16),
            pltpu.SemaphoreType.DMA((blocks,)),
            pltpu.SemaphoreType.DMA((blocks,)),
            *scratch,
        ],
        compiler_params=params(collective_id=1, has_side_effects=True),
        name="attention_back_scatter",
    )(
        tok,
        own,
        msg,
        dw2.reshape(2, 2, 2, 384, D),
        dw1.reshape(2, 2, 2, 96, FF),
        dwo.reshape(2, 2, 2, 96, D),
    )


def final_kernel(
    z_ref, tok_ref, grad_ref, normed_ref, lhs_ref, sc_ref, rhs_ref, h1g_ref, up_w_ref, vec_ref, own_w_ref, mean_ref,
    dw_ref, noise_ref, table_ref, small_ref, acc,
):
    i = pl.program_id(0)
    last = pl.num_programs(0) - 1
    vocab = table_ref.shape[1]
    mean = mean_ref[0:1, 0:1]

    @pl.when(i == 0)
    def _():
        acc[...] = jnp.zeros_like(acc)
        small_ref[...] = jnp.zeros_like(small_ref)
        table_ref[...] = jnp.zeros_like(table_ref)

    grad = grad_ref[...]
    hidden0 = dot(lhs_ref[0], rhs_ref[...], TN)
    unit, inverse = norm_parts(hidden0)
    norm_grad = dot(grad, own_w_ref[...], NT)
    acc[...] += dot(normed_ref[...], grad, TN)
    own = (z_ref[0] == i).astype(f32)
    h0_grad = (norm_pull(norm_grad, unit, inverse, vec_ref[1:2, :]) + own * h1g_ref[...]).astype(bf16)
    mixed_grad = dot(up_w_ref[...], h0_grad, NT)
    sc = sc_ref[0]
    noise_ref[0] = sc[17:18] * mixed_grad
    embedded_grad = sc[16:17] * mixed_grad
    picked = sc[:16]
    norm_term = -jnp.sum(embedded_grad * picked, axis=(0, 1), keepdims=True) / (mean * mean)
    ids = tok_ref[i][16:17, :]
    table3 = dot(jnp.concatenate(split3(embedded_grad / mean), axis=0).astype(bf16), id_matrix(vocab, ids), NT)
    table_ref[...] += table3[:16] + table3[16:32] + table3[32:48]
    gradf = grad.astype(f32)
    small_ref[...] += jnp.concatenate(
        [
            dot(lhs_ref[0, :16, :], h0_grad),
            column_sum(h0_grad.astype(f32)),
            column_sum(norm_grad * unit),
            column_sum(norm_grad),
            column_sum(gradf),
            jnp.broadcast_to(norm_term, (1, D)),
            jnp.zeros((3, D), f32),
        ],
        axis=0,
    )

    @pl.when(i == last)
    def _():
        dw_ref[...] = acc[...].astype(bf16)


def final(z, tok, grad, normed, lhs, sc, rhs, h1g, up_w, vec, own_w, mean, vocab):
    blocks, _, rows = tok.shape
    spec = pltpu.PrefetchScalarGridSpec(
        num_scalar_prefetch=1,
        grid=(blocks,),
        in_specs=[
            whole(tok.shape),
            pl.BlockSpec((rows, 3 * SLOT), lambda i, z: (i, 0)),
            pl.BlockSpec((rows, D), lambda i, z: (i, 0)),
            pl.BlockSpec((1, 48, rows), lambda i, z: (i, 0, 0)),
            pl.BlockSpec((1, 24, rows), lambda i, z: (i, 0, 0)),
            whole(rhs.shape),
            whole(h1g.shape),
            whole(up_w.shape),
            whole(vec.shape),
            whole(own_w.shape),
            whole(mean.shape),
        ],
        out_specs=[
            whole((D, 3 * SLOT)),
            pl.BlockSpec((1, 16, rows), lambda i, z: (i, 0, 0)),
            whole((16, vocab)),
            whole((24, D)),
        ],
        scratch_shapes=[VMEM((D, 3 * SLOT), f32)],
    )
    return pl.pallas_call(
        final_kernel,
        grid_spec=spec,
        out_shape=[
            jax.ShapeDtypeStruct((D, 3 * SLOT), bf16),
            jax.ShapeDtypeStruct((blocks, 16, rows), f32),
            jax.ShapeDtypeStruct((16, vocab), f32),
            jax.ShapeDtypeStruct((24, D), f32),
        ],
        compiler_params=params(),
        name="embed_back",
    )(z, tok, grad, normed, lhs, sc, rhs, h1g, up_w, vec, own_w, mean)


def tail_kernel(
    dw_ref, small_ref, noise_ref, dw_out, small_out, table_out, noise_out,
    parts, mine, lines, sums, dw_parts, dw_mine, noise_parts, sends, recvs, *scratch
):
    dp = lax.axis_index("dp")
    z = lax.axis_index("blk")
    dp_n, blk_n = parts.shape[0], lines.shape[0]
    half = D // 2
    units = [
        Scatter(dw_ref, pl.ds(0, half), True, *scratch[:7]),
        Scatter(dw_ref, pl.ds(half, half), False, *scratch[7:]),
    ]
    dp_to = [(lax.rem(dp + k, dp_n), z) for k in range(1, dp_n)]
    z_to = [(dp, lax.rem(z + k, blk_n)) for k in range(1, blk_n)]
    sync(dp_to + z_to)
    nd, nz = dp_n - 1, blk_n - 1

    def spread(src, dst, peers, first):
        return [
            remote(src(p), dst, sends.at[first + k], recvs.at[first + k], p) for k, p in enumerate(peers)
        ]

    for u in units:
        u.start()
    one = spread(lambda p: small_ref.at[p[0]], parts.at[dp], dp_to, 0)
    four = spread(lambda p: noise_ref.at[p[1]], noise_parts.at[z], z_to, 2 * nd + nz)
    for c in one + four:
        c.start()
    parts[dp] = small_ref[dp]
    noise_parts[z] = noise_ref[z]
    for u in units:
        u.core_to_wide()
    for c in one:
        c.wait()
    total = parts[0]
    for k in range(1, dp_n):
        total = total + parts[k]
    mine[...] = total
    lines[z] = total
    two = spread(lambda p: mine, lines.at[z], z_to, nd)
    for c in two:
        c.start()
    for u in units:
        u.wide_to_narrow()
    for c in two:
        c.wait()
    total = lines[0]
    for k in range(1, blk_n):
        total = total + lines[k]
    table_out[...] = total[:, half:]
    sums[...] = total[:, :half]
    small_out[dp] = total[:, :half]
    three = spread(lambda p: sums, small_out.at[dp], dp_to, nd + nz)
    for c in three:
        c.start()
    for u in units:
        total = u.narrow_sum()
        q = total.shape[0] // blk_n
        for k in range(blk_n):
            dw_parts[k, :, u.columns] = total[k * q : (k + 1) * q]
    five = spread(lambda p: dw_parts.at[p[1]], dw_out.at[z], z_to, 2 * nd + 2 * nz)
    for c in five:
        c.start()
    dw_out[z] = dw_parts[z]
    for c in four:
        c.wait()
    total = noise_parts[0]
    for k in range(1, blk_n):
        total = total + noise_parts[k]
    noise_out[...] = total
    for c in three + five:
        c.wait()


def tail(dw, small, noise, dp_n, blk_n):
    rows = noise.shape[2]
    share = D // (dp_n * blk_n)
    vmem = pl.BlockSpec(memory_space=VMEM)
    width = small.shape[2]
    count = 2 * (dp_n - 1) + 3 * (blk_n - 1)
    half = D // 2
    return pl.pallas_call(
        tail_kernel,
        in_specs=[vmem] * 3,
        out_specs=[vmem] * 4,
        out_shape=[
            jax.ShapeDtypeStruct((blk_n, share, 3 * SLOT), f32),
            jax.ShapeDtypeStruct((dp_n, 8, half), f32),
            jax.ShapeDtypeStruct((8, width - half), f32),
            jax.ShapeDtypeStruct((16, rows), f32),
        ],
        scratch_shapes=[
            VMEM((dp_n, 8, width), f32),
            VMEM((8, width), f32),
            VMEM((blk_n, 8, width), f32),
            VMEM((8, half), f32),
            VMEM((blk_n, share, 3 * SLOT), f32),
            VMEM((8, 128), f32),
            VMEM((blk_n, 16, rows), f32),
            pltpu.SemaphoreType.DMA((count,)),
            pltpu.SemaphoreType.DMA((count,)),
            *(scatter_scratch(D // dp_n, half) * 2),
        ],
        compiler_params=params(collective_id=2, has_side_effects=True),
        name="tail",
    )(dw.reshape(2, 2, 2, D // dp_n, 3 * SLOT), small, noise)


def shards(
    dp_n,
    blk_n,
    token_ids,
    segment_ids,
    timesteps,
    noise,
    table,
    up_weight,
    up_bias,
    norm1_gain,
    norm1_shift,
    qkv_weight,
    query_bias,
    value_bias,
    out_weight,
    out_bias,
    norm2_gain,
    norm2_shift,
    ffn_in_weight,
    ffn_in_bias,
    ffn_out_weight,
    ffn_out_bias,
    cotangent,
):
    rows = token_ids.shape[0]
    local_rows = table.shape[0]
    vp = -(-local_rows // 128) * 128
    per = -(-HEADS // blk_n)
    width = per * HEAD_DIM
    z = lax.axis_index("blk")
    z1 = z.reshape(1).astype(jnp.int32)

    slots = (token_ids // local_rows) * vp + token_ids % local_rows
    scalars = jnp.stack([slots, segment_ids, timesteps]).astype(f32)
    mine = jnp.concatenate([noise.T, scalars, jnp.zeros((5, rows), f32)], axis=0)
    tab_mine = jnp.pad(table.T, ((0, 0), (0, vp - local_rows)))
    near = dp_n == 8 and blk_n == 4
    if near:
        tok, tab = gather(mine, tab_mine, dp_n, blk_n)
    else:
        tok = lax.all_gather(mine, "blk")
        tab = lax.all_gather(tab_mine, "dp")

    padded = blk_n * width
    split = jnp.pad(qkv_weight.reshape(D, 3, D), ((0, 0), (0, 0), (0, padded - D)))
    own_w = lax.dynamic_slice(split, (0, 0, z * width), (D, 3, width))
    own_w = jnp.pad(own_w, ((0, 0), (0, 0), (0, SLOT - width))).reshape(D, 3 * SLOT)
    bias = jnp.pad(jnp.stack([query_bias, jnp.zeros((D,), f32), value_bias]), ((0, 0), (0, padded - D)))
    own_b = lax.dynamic_slice(bias, (0, z * width), (3, width))
    own_b = jnp.pad(own_b, ((0, 0), (0, SLOT - width))).reshape(1, 3 * SLOT)
    vec1 = jnp.stack([up_bias, norm1_gain, norm1_shift, query_bias, value_bias])
    k, vt, own, normed, lhs, sc, qt, h0, rhs, mean = embed(
        z1, tok, tab, up_weight, vec1, qkv_weight, own_w, own_b, local_rows
    )
    vec2 = jnp.stack([out_bias, norm2_gain, norm2_shift, ffn_out_bias])
    b1 = ffn_in_bias.reshape(FF // D, D)
    block_out, h1g, msg, dwo, dw1, dw2, small1 = layer(
        tok, mine, k, vt, qt, h0, cotangent, vec2, b1, out_weight, ffn_in_weight, ffn_out_weight, per
    )
    if near:
        grad, dw2, dw1, dwo = back_scatter(tok, own, msg, dw2, dw1, dwo, per)
    else:
        msg = lax.all_to_all(msg, "blk", 0, 0)
        grad = back(tok, own, msg, per)
    dw, noise_part, table_part, small2 = final(
        z1, tok, grad, normed, lhs, sc, rhs, h1g, up_weight, vec1, own_w, mean, dp_n * vp
    )
    share = D // (dp_n * blk_n)
    if near:
        place = (jnp.arange(blk_n) == z).astype(f32)[:, None]
        flat = jnp.concatenate([small1, small2[:19], small2[20:21], place * small2[19:20]], axis=0)
        flat = jnp.concatenate([flat[:, : D // 2], flat[:, D // 2 :]], axis=0).reshape(dp_n, 8, D // 2)
        table_part = table_part.reshape(2, 8, dp_n, vp).transpose(2, 1, 0, 3).reshape(dp_n, 8, 2 * vp)
        dw, flat, table_total, noise_grad = tail(dw, jnp.concatenate([flat, table_part], axis=2), noise_part, dp_n, blk_n)
        noise_grad = noise_grad.T
        flat = flat.reshape(-1, D // 2)
        flat = jnp.concatenate([flat[:32], flat[32:]], axis=1)
        small1, small2 = flat[:8], flat[8:28]
        norm_grad = flat[27, 0]
        own_sums = flat[28:32].reshape(blk_n, 3, SLOT)[:, :, :width].transpose(1, 0, 2).reshape(3, padded)
        table_grad = table_total.reshape(8, 2, vp).transpose(1, 0, 2).reshape(16, vp)
    else:
        noise_grad = lax.psum_scatter(noise_part, "blk", scatter_dimension=0, tiled=False).T
        own_sums = small2[19].reshape(3, SLOT)[:, :width]
        own_sums = lax.dynamic_update_slice(jnp.zeros((3, padded), f32), own_sums, (0, z * width))[:, :D]
        small2, table_total, small1, own_sums = lax.psum((small2, table_part, small1, own_sums), ("dp", "blk"))
        scatter = functools.partial(lax.psum_scatter, axis_name=("dp", "blk"), scatter_dimension=0, tiled=True)
        dwo, dw1, dw2 = scatter(dwo), scatter(dw1), scatter(dw2)
        dw = lax.psum_scatter(dw, "dp", scatter_dimension=0, tiled=True)
        dw = lax.all_to_all(dw.reshape(blk_n, share, 3 * SLOT), "blk", 0, 0)
        norm_grad = small2[20, 0]
        table_grad = lax.dynamic_slice(table_total, (0, lax.axis_index("dp") * vp), (16, vp))
    dw = dw.reshape(blk_n, share, 3, SLOT)[..., :width].transpose(1, 2, 0, 3).reshape(share, 3, padded)[..., :D]
    qkv_weight_grad = dw.reshape(share, 3 * D).astype(f32)
    mean_norm = mean[0, 0]
    table_grad = table_grad[:, :local_rows].T
    norms = jnp.sqrt(jnp.sum(table * table, axis=-1, keepdims=True) + 1.0)
    table_grad = table_grad + norm_grad * table / (dp_n * local_rows * norms)
    return (
        block_out,
        noise_grad,
        table_grad,
        small2[:16],
        small2[16],
        small2[17],
        small2[18],
        qkv_weight_grad,
        own_sums[0],
        own_sums[2],
        dwo.astype(f32),
        small1[0],
        small1[1],
        small1[2],
        dw1.astype(f32),
        small1[4:8].reshape(FF),
        dw2.astype(f32),
        small1[3],
        mean_norm,
    )


def solution(mesh):
    rows = P(("dp", "blk"))
    wide = P(("dp", "blk"), None)
    in_specs = (rows, rows, rows, wide, P("dp", None)) + (P(),) * 15 + (wide,)
    out_specs = (
        (wide, wide, P("dp", None))
        + (P(),) * 4
        + (wide, P(), P(), wide, P(), P(), P(), wide, P(), wide, P(), P())
    )
    body = functools.partial(shards, mesh.shape["dp"], mesh.shape["blk"])
    return jax.shard_map(body, mesh=mesh, in_specs=in_specs, out_specs=out_specs, check_vma=False)
```

```python
import functools
import math

import jax
import jax.numpy as jnp
from jax import lax
from jax.experimental import pallas as pl
from jax.experimental.pallas import tpu as pltpu
from jax.sharding import PartitionSpec as P

D = 768
HEADS = 12
HEAD_DIM = 64
FF = 3072
EMB = 16
TSTEPS = 2000
DOCS = 4
PAIR = 2 * HEAD_DIM
SLOT = 256
EXT = 192
BIG = 1e30
SCALE = HEAD_DIM**-0.5
MIB = 2**20
MESH = pl.DeviceIdType.MESH
VMEM = pltpu.VMEM
f32 = jnp.float32
bf16 = jnp.bfloat16

NN = (((1,), (0,)), ((), ()))
NT = (((1,), (1,)), ((), ()))
TN = (((0,), (0,)), ((), ()))
TT = (((0,), (1,)), ((), ()))


def dot(left, right, dims=NN):
    return lax.dot_general(left, right, dims, preferred_element_type=f32)


def split3(x):
    high = x.astype(bf16)
    rest = x - high.astype(f32)
    middle = rest.astype(bf16)
    low = (rest - middle.astype(f32)).astype(bf16)
    return high.astype(f32), middle.astype(f32), low.astype(f32)


def column_sum(x):
    return jnp.sum(x, axis=0, keepdims=True)


def row_mean(x):
    return jnp.mean(x, axis=-1, keepdims=True)


def norm_parts(x):
    centered = x - row_mean(x)
    inverse = lax.rsqrt(row_mean(centered * centered) + 1e-05)
    return centered * inverse, inverse


def norm_pull(grad, unit, inverse, gain):
    scaled = grad * gain
    return inverse * (scaled - row_mean(scaled) - unit * row_mean(scaled * unit))


def onehot8(row):
    return (lax.broadcasted_iota(jnp.int32, (8, row.shape[1]), 0) == row.astype(jnp.int32)).astype(f32)


def id_matrix(rows, row):
    return (lax.broadcasted_iota(jnp.int32, (rows, row.shape[1]), 0) == row.astype(jnp.int32)).astype(f32).astype(bf16)


def params(**kw):
    return pltpu.CompilerParams(vmem_limit_bytes=60 * MIB, **kw)


def whole(shape):
    return pl.BlockSpec(shape, lambda *_: (0,) * len(shape))


def sync(peers):
    barrier = pltpu.get_barrier_semaphore()
    for peer in peers:
        pl.semaphore_signal(barrier, inc=1, device_id=peer, device_id_type=MESH)
    pl.semaphore_wait(barrier, len(peers))


def remote(src, dst, send, recv, peer):
    return pltpu.make_async_remote_copy(
        src_ref=src, dst_ref=dst, send_sem=send, recv_sem=recv, device_id=peer, device_id_type=MESH
    )


def gather_kernel(dp_n, blk_n, mine_ref, table_ref, tok_ref, tab_ref, send, recv):
    dp = lax.axis_index("dp")
    z = lax.axis_index("blk")
    dp_peers = [(lax.rem(dp + k, dp_n), z) for k in range(1, dp_n)]
    z_peers = [(dp, lax.rem(z + k, blk_n)) for k in range(1, blk_n)]
    sync(z_peers + dp_peers)
    copies = []
    for k, peer in enumerate(z_peers):
        copies.append(remote(mine_ref, tok_ref.at[z], send.at[k], recv.at[k], peer))
    for k, peer in enumerate(dp_peers):
        n = len(z_peers) + k
        copies.append(remote(table_ref, tab_ref.at[dp], send.at[n], recv.at[n], peer))
    for c in copies:
        c.start()
    tok_ref[z] = mine_ref[...]
    tab_ref[dp] = table_ref[...]
    for c in copies:
        c.wait()


def gather(mine, table, dp_n, blk_n):
    count = dp_n + blk_n - 2
    vmem = pl.BlockSpec(memory_space=VMEM)
    return pl.pallas_call(
        functools.partial(gather_kernel, dp_n, blk_n),
        in_specs=[vmem, vmem],
        out_specs=[vmem, vmem],
        out_shape=[
            jax.ShapeDtypeStruct((blk_n,) + mine.shape, f32),
            jax.ShapeDtypeStruct((dp_n,) + table.shape, f32),
        ],
        scratch_shapes=[pltpu.SemaphoreType.DMA((count,)), pltpu.SemaphoreType.DMA((count,))],
        compiler_params=params(collective_id=0, has_side_effects=True),
        name="gather",
    )(mine, table)


class Scatter:
    def __init__(self, grad, columns, by_x, first, second, third, send, recv, chunks=None):
        self.grad, self.columns, self.by_x = grad, columns, by_x
        self.first, self.second, self.third = first, second, third
        self.send, self.recv, self.chunks = send, recv, chunks
        self.dp = lax.axis_index("dp")
        self.z = lax.axis_index("blk")
        self.core = lax.rem(self.dp, 2)
        self.x = lax.rem(lax.div(self.dp, 2), 2)
        self.y = lax.div(self.dp, 4)

    def flip(self, bit, step):
        return (self.dp + step * (1 - 2 * bit), self.z)

    def own(self, y, x):
        return self.grad[y, x, self.core, :, self.columns].astype(f32)

    def core_copy(self):
        src = self.grad.at[:, :, 1 - self.core, :, self.columns]
        return remote(src, self.first, self.send.at[0], self.recv.at[0], self.flip(self.core, 1))

    def wide(self):
        if self.by_x:
            src, peer = self.grad.at[:, 1 - self.x, self.core, :, self.columns], self.flip(self.x, 2)
        else:
            src, peer = self.grad.at[1 - self.y, :, self.core, :, self.columns], self.flip(self.y, 4)
        return remote(src, self.second, self.send.at[1], self.recv.at[1], peer)

    def narrow(self):
        if self.by_x:
            src, peer = self.grad.at[1 - self.y, self.x, self.core, :, self.columns], self.flip(self.y, 4)
        else:
            src, peer = self.grad.at[self.y, 1 - self.x, self.core, :, self.columns], self.flip(self.x, 2)
        return remote(src, self.third, self.send.at[2], self.recv.at[2], peer)

    def start(self):
        self.core_copy().start()

    def core_to_wide(self):
        if self.chunks is None:
            self.core_copy().wait()
        elif self.by_x:
            for c in self.chunks:
                c().wait()
        for y in range(2):
            for x in range(2):
                if self.chunks is None:
                    other = self.first[y, x]
                else:
                    other = self.first[y, x, :, self.columns]
                self.grad[y, x, self.core, :, self.columns] = (self.own(y, x) + other.astype(f32)).astype(bf16)
        self.wide().start()

    def wide_to_narrow(self):
        self.wide().wait()
        for n in range(2):
            y, x = (n, self.x) if self.by_x else (self.y, n)
            total = self.own(y, x) + self.second[n].astype(f32)
            self.grad[y, x, self.core, :, self.columns] = total.astype(bf16)
        self.narrow().start()

    def narrow_sum(self):
        self.narrow().wait()
        return self.own(self.y, self.x) + self.third[...].astype(f32)


def scatter_scratch(rows, columns, first=True):
    return ([VMEM((2, 2, rows, columns), bf16)] if first else []) + [
        VMEM((2, rows, columns), bf16),
        VMEM((rows, columns), bf16),
        pltpu.SemaphoreType.DMA((3,)),
        pltpu.SemaphoreType.DMA((3,)),
    ]


class LineScatter:
    def __init__(self, base, out, half, first, rest, second, send, recv):
        self.base, self.out = base, out
        self.half, self.first, self.rest, self.second = half, first, rest, second
        self.send, self.recv = send, recv
        self.low = lax.rem(base.z, 2)
        self.high = lax.div(base.z, 2)

    def near(self):
        peer = (self.base.dp, self.base.z + 1 - 2 * self.low)
        return remote(self.half.at[1 - self.low], self.first, self.send.at[0], self.recv.at[0], peer)

    def far(self):
        peer = (self.base.dp, self.base.z + 2 - 4 * self.high)
        return remote(self.rest.at[1 - self.high], self.second, self.send.at[1], self.recv.at[1], peer)

    def start(self):
        total = self.base.narrow_sum()
        q = total.shape[0] // 4
        for low in range(2):
            self.half[low, :q] = total[low * q : (low + 1) * q].astype(bf16)
            self.half[low, q:] = total[(2 + low) * q : (3 + low) * q].astype(bf16)
        self.near().start()

    def near_to_far(self):
        self.near().wait()
        q = self.rest.shape[1]
        total = self.half[self.low].astype(f32) + self.first[...].astype(f32)
        self.rest[0] = total[:q]
        self.rest[1] = total[q:]
        self.far().start()

    def finish(self):
        self.far().wait()
        self.out[:, self.base.columns] = self.rest[self.high] + self.second[...]


def line_scratch(rows, columns):
    return [
        VMEM((2, rows // 2, columns), bf16),
        VMEM((rows // 2, columns), bf16),
        VMEM((2, rows // 4, columns), f32),
        VMEM((rows // 4, columns), f32),
        pltpu.SemaphoreType.DMA((2,)),
        pltpu.SemaphoreType.DMA((2,)),
    ]


def embed_kernel(
    local_rows,
    z_ref,
    tok_ref,
    tab_ref,
    up_w_ref,
    vec_ref,
    w_ref,
    own_w_ref,
    own_b_ref,
    k_ref,
    vt_ref,
    own_ref,
    normed_ref,
    lhs_ref,
    sc_ref,
    qt_ref,
    h0_ref,
    rhs_ref,
    mean_ref,
    tab3,
    vcol,
):
    i = pl.program_id(0)
    dp_n, _, vp = tab_ref.shape
    blocks, _, rows = tok_ref.shape

    @pl.when(i == 0)
    def _():
        table = jnp.concatenate([tab_ref[j] for j in range(dp_n)], axis=1)
        squares = jnp.sum(table * table, axis=0, keepdims=True)
        lane = lax.broadcasted_iota(jnp.int32, squares.shape, 1)
        norms = jnp.where(lane % vp < local_rows, jnp.sqrt(squares + 1.0), 0.0)
        mean_ref[...] = jnp.broadcast_to(jnp.sum(norms, axis=1, keepdims=True) / (local_rows * dp_n), (8, 128))
        tab3[...] = jnp.concatenate(split3(table), axis=0).astype(bf16)
        segments = tok_ref[:, 17, :]
        steps = tok_ref[:, 18, :]
        sub = lax.broadcasted_iota(jnp.int32, (8, 1), 0)
        time = jnp.zeros((8, 1), f32)
        for s in range(DOCS):
            own = jnp.max(jnp.where(segments == float(s), steps, 0.0), axis=(0, 1), keepdims=True)
            time = jnp.where(sub == s, own, time)
        lane = lax.broadcasted_iota(jnp.int32, (8, D), 1)
        half = D // 2
        index = jnp.where(lane < half, lane, lane - half).astype(f32)
        angle = time * jnp.exp(index * (-math.log(10000.0) / half))
        wave = jnp.where(lane < half, jnp.sin(angle), jnp.cos(angle)) + vec_ref[0:1, :]
        parts = split3(wave)
        rhs_ref[...] = jnp.concatenate([up_w_ref[...].astype(f32), *parts, jnp.zeros((8, D), f32)], axis=0).astype(bf16)
        bias = jnp.concatenate([vec_ref[3:5, :], jnp.zeros((6, D), f32)], axis=0)
        vcol[...] = jnp.transpose(bias)

    tok = tok_ref[i]
    ids = tok[16:17, :]
    picked3 = dot(tab3[...], id_matrix(dp_n * vp, ids))
    picked = picked3[:16] + picked3[16:32] + picked3[32:48]
    mean = mean_ref[0:1, 0:1]
    alpha_bar = 1.0 - jnp.sqrt(tok[18:19, :] / TSTEPS + 0.0001)
    signal = jnp.sqrt(alpha_bar)
    noise_scale = jnp.sqrt(1.0 - alpha_bar)
    mixed = signal * (picked / mean) + noise_scale * tok[:16]
    seg = onehot8(tok[17:18, :])
    lhs = jnp.concatenate([mixed, seg, seg, seg, jnp.zeros((8, rows), f32)], axis=0).astype(bf16)
    lhs_ref[0] = lhs
    sc_ref[0] = jnp.concatenate([picked, signal, noise_scale, jnp.zeros((6, rows), f32)], axis=0)
    hidden0 = dot(lhs, rhs_ref[...], TN)
    unit, _ = norm_parts(hidden0)
    normed = (unit * vec_ref[1:2, :] + vec_ref[2:3, :]).astype(bf16)
    normed_ref[...] = normed
    k_ref[...] = dot(normed, w_ref[:, D : 2 * D]).astype(bf16)
    vt_ref[...] = (dot(w_ref[:, 2 * D :], normed, TT) + vcol[:, 1:2]).astype(bf16)
    own = dot(normed, own_w_ref[...]) + own_b_ref[...]
    own_ref[:, :SLOT] = (own[:, :SLOT] * SCALE).astype(bf16)
    own_ref[:, SLOT:] = own[:, SLOT:].astype(bf16)

    @pl.when(i == z_ref[0])
    def _():
        h0_ref[...] = hidden0
        q = (dot(w_ref[:, :D], normed, TT) + vcol[:, 0:1]).astype(bf16)
        qt_ref[...] = (q.astype(f32) * SCALE).astype(bf16)


def embed(z, tok, tab, up_w, vec, w, own_w, own_b, local_rows):
    blocks, _, rows = tok.shape
    group = blocks * rows
    vocab = tab.shape[0] * tab.shape[2]
    spec = pltpu.PrefetchScalarGridSpec(
        num_scalar_prefetch=1,
        grid=(blocks,),
        in_specs=[whole(x.shape) for x in (tok, tab, up_w, vec, w, own_w, own_b)],
        out_specs=[
            pl.BlockSpec((rows, D), lambda i, z: (i, 0)),
            pl.BlockSpec((D, rows), lambda i, z: (0, i)),
            pl.BlockSpec((rows, 3 * SLOT), lambda i, z: (i, 0)),
            pl.BlockSpec((rows, D), lambda i, z: (i, 0)),
            pl.BlockSpec((1, 48, rows), lambda i, z: (i, 0, 0)),
            pl.BlockSpec((1, 24, rows), lambda i, z: (i, 0, 0)),
            whole((D, rows)),
            whole((rows, D)),
            whole((48, D)),
            whole((8, 128)),
        ],
        scratch_shapes=[VMEM((48, vocab), bf16), VMEM((D, 8), f32)],
    )
    return pl.pallas_call(
        functools.partial(embed_kernel, local_rows),
        grid_spec=spec,
        out_shape=[
            jax.ShapeDtypeStruct((group, D), bf16),
            jax.ShapeDtypeStruct((D, group), bf16),
            jax.ShapeDtypeStruct((group, 3 * SLOT), bf16),
            jax.ShapeDtypeStruct((group, D), bf16),
            jax.ShapeDtypeStruct((blocks, 48, rows), bf16),
            jax.ShapeDtypeStruct((blocks, 24, rows), f32),
            jax.ShapeDtypeStruct((D, rows), bf16),
            jax.ShapeDtypeStruct((rows, D), f32),
            jax.ShapeDtypeStruct((48, D), bf16),
            jax.ShapeDtypeStruct((8, 128), f32),
        ],
        compiler_params=params(),
        name="embed",
    )(z, tok, tab, up_w, vec, w, own_w, own_b)


ROOT = math.sqrt(2.0 / math.pi)


def attend(p, tok_ref, mine_ref, k_ref, vt_ref, qt_ref, att, lse, kext, qext):
    blocks, _, rows = tok_ref.shape

    @pl.when(p == 0)
    def _():
        for b in range(blocks):
            seg = jnp.concatenate([onehot8(tok_ref[b, 17:18, :]), jnp.zeros((120, rows), f32)], axis=0)
            kext[b * rows : (b + 1) * rows, :] = jnp.transpose(seg).astype(bf16)
        seg = onehot8(mine_ref[17:18, :])
        sub = lax.broadcasted_iota(jnp.int32, seg.shape, 0)
        barred = jnp.where(sub < DOCS, -BIG * (1.0 - seg), 0.0)
        qext[...] = jnp.concatenate([barred, jnp.zeros((120, rows), f32)], axis=0).astype(bf16)

    keys = jnp.concatenate([k_ref[...], kext[...]], axis=1)
    zeros = jnp.zeros((HEAD_DIM, rows), bf16)
    ones = jnp.ones((HEAD_DIM, blocks * rows), bf16)
    results = []
    for h in range(2):
        q = qt_ref[h * HEAD_DIM : (h + 1) * HEAD_DIM, :]
        v = vt_ref[h * HEAD_DIM : (h + 1) * HEAD_DIM, :]
        queries = jnp.concatenate([q, zeros, qext[...]] if h == 0 else [zeros, q, qext[...]], axis=0)
        scores = dot(keys, queries)
        top = jnp.max(scores, axis=0, keepdims=True)
        weights = jnp.exp(scores - top).astype(bf16)
        total = dot(jnp.concatenate([v, ones], axis=0), weights)
        results.append(total[:HEAD_DIM] / total[HEAD_DIM:])
        lse[pl.ds(2 * p + h, 1), :] = top + jnp.log(total[HEAD_DIM : HEAD_DIM + 1])
    att[pl.ds(pl.multiple_of(p * PAIR, PAIR), PAIR), :] = jnp.concatenate(results, axis=0)


def attention_kernel(tok_ref, mine_ref, k_ref, vt_ref, qt_ref, att, lse, kext, qext):
    attend(pl.program_id(0), tok_ref, mine_ref, k_ref, vt_ref, qt_ref, att, lse, kext, qext)


def attention(tok, mine, k, vt, qt):
    blocks, _, rows = tok.shape
    group = blocks * rows
    return pl.pallas_call(
        attention_kernel,
        grid=(HEADS // 2,),
        in_specs=[
            whole(tok.shape),
            whole(mine.shape),
            pl.BlockSpec((group, PAIR), lambda p: (0, p)),
            pl.BlockSpec((PAIR, group), lambda p: (p, 0)),
            pl.BlockSpec((PAIR, rows), lambda p: (p, 0)),
        ],
        out_specs=[whole((D, rows)), whole((16, rows))],
        out_shape=[jax.ShapeDtypeStruct((D, rows), f32), jax.ShapeDtypeStruct((16, rows), f32)],
        scratch_shapes=[VMEM((group, PAIR), bf16), VMEM((PAIR, rows), bf16)],
        compiler_params=params(),
        name="attention",
    )(tok, mine, k, vt, qt)


def gelu_parts(x):
    square = x * x
    t = jnp.tanh(x * (ROOT + (ROOT * 0.044715) * square))
    half = 0.5 * (1.0 + t)
    slope = half + (0.5 * x) * (1.0 - t * t) * (ROOT + (3.0 * ROOT * 0.044715) * square)
    return (x * half).astype(bf16), slope


def layer_kernel(
    per,
    tok_ref,
    mine_ref,
    k_ref,
    vt_ref,
    qt_ref,
    h0_ref,
    cot_ref,
    vec_ref,
    b1_ref,
    wo_ref,
    w1_ref,
    w2_ref,
    out_ref,
    h1g_ref,
    msg_ref,
    dwo_ref,
    dw1_ref,
    dw2_ref,
    small_ref,
    kext,
    qext,
    att,
    lse,
    wo,
    wo_slots,
    w1,
    w2,
    sems,
):
    p = pl.program_id(0)
    last = pl.num_programs(0) - 1
    blocks, _, rows = tok_ref.shape
    copies = [
        pltpu.make_async_copy(wo_ref, wo, sems.at[0]),
        pltpu.make_async_copy(w1_ref, w1, sems.at[1]),
        pltpu.make_async_copy(w2_ref, w2, sems.at[2]),
    ]

    @pl.when(p == 0)
    def _():
        for c in copies:
            c.start()

    attend(p, tok_ref, mine_ref, k_ref, vt_ref, qt_ref, att, lse, kext, qext)

    @pl.when(p == last)
    def _():
        for c in copies:
            c.wait()
        attended = att[...].astype(bf16)
        hidden1 = h0_ref[...] + dot(attended, wo[...], TN) + vec_ref[0:1, :]
        unit, inverse = norm_parts(hidden1)
        normed2 = (unit * vec_ref[1:2, :] + vec_ref[2:3, :]).astype(bf16)
        cot = cot_ref[...]
        out_grad = cot.astype(bf16)
        block_out = hidden1 + vec_ref[3:4, :]
        norm_grad = jnp.zeros_like(hidden1)
        inner_sums = []
        for c in range(FF // D):
            cols = slice(c * D, (c + 1) * D)
            x = dot(normed2, w1[:, cols]) + b1_ref[c : c + 1, :]
            active, slope = gelu_parts(x)
            block_out = block_out + dot(active, w2[cols, :])
            inner_grad = (dot(out_grad, w2[cols, :], NT) * slope).astype(bf16)
            dw2_ref[cols, :] = dot(active, out_grad, TN).astype(bf16)
            dw1_ref[:, cols] = dot(normed2, inner_grad, TN).astype(bf16)
            norm_grad = norm_grad + dot(inner_grad, w1[:, cols], NT)
            inner_sums.append(column_sum(inner_grad.astype(f32)))
        out_ref[...] = block_out
        hidden1_grad = cot + norm_pull(norm_grad, unit, inverse, vec_ref[1:2, :])
        h1g_ref[...] = hidden1_grad
        branch = hidden1_grad.astype(bf16)
        dwo_ref[...] = dot(attended, branch).astype(bf16)
        small_ref[...] = jnp.concatenate(
            [
                column_sum(branch.astype(f32)),
                column_sum(norm_grad * unit),
                column_sum(norm_grad),
                column_sum(out_grad.astype(f32)),
                *inner_sums,
            ],
            axis=0,
        )
        seg = onehot8(mine_ref[17:18, :])
        back = dot(wo[...], branch, NT).astype(bf16).astype(f32)
        product = back * att[...]
        for j in range(blocks):
            heads = [h for h in range(per * j, per * (j + 1)) if h < HEADS]
            wo_slots[...] = jnp.zeros_like(wo_slots)
            size = len(heads) * HEAD_DIM
            rows_ext = [jnp.zeros((HEAD_DIM, rows), f32), jnp.where(
                lax.broadcasted_iota(jnp.int32, (8, rows), 0) < DOCS, -BIG * (1.0 - seg), 0.0
            )[:DOCS]]
            lse_parts = []
            delta_parts = []
            for n in range(3):
                h = per * j + n
                if n < per and h < HEADS:
                    delta = column_sum(product[h * HEAD_DIM : (h + 1) * HEAD_DIM])
                    lse_parts += split3(-lse[h : h + 1, :])
                    delta_parts += split3(-delta)
                else:
                    lse_parts += [jnp.zeros((1, rows), f32)] * 3
                    delta_parts += [jnp.zeros((1, rows), f32)] * 3
            used = DOCS + 18
            rows_ext = rows_ext + lse_parts + delta_parts + [jnp.zeros((HEAD_DIM - used, rows), f32)]
            ext = jnp.transpose(jnp.concatenate(rows_ext, axis=0))
            if size:
                wo_slots[:size, :] = wo[heads[0] * HEAD_DIM : heads[0] * HEAD_DIM + size, :]
            grads = dot(branch, wo_slots[...], NT)
            msg_ref[j, :, :PAIR] = grads[:, :PAIR].astype(bf16)
            msg_ref[j, :, PAIR:] = (grads[:, PAIR:] + ext).astype(bf16)


def layer(tok, mine, k, vt, qt, h0, cot, vec, b1, wo, w1, w2, per):
    blocks, _, rows = tok.shape
    group = blocks * rows
    any_spec = pl.BlockSpec(memory_space=pl.ANY)
    return pl.pallas_call(
        functools.partial(layer_kernel, per),
        grid=(HEADS // 2,),
        in_specs=[
            whole(tok.shape),
            whole(mine.shape),
            pl.BlockSpec((group, PAIR), lambda p: (0, p)),
            pl.BlockSpec((PAIR, group), lambda p: (p, 0)),
            pl.BlockSpec((PAIR, rows), lambda p: (p, 0)),
            whole(h0.shape),
            whole(cot.shape),
            whole(vec.shape),
            whole(b1.shape),
            any_spec,
            any_spec,
            any_spec,
        ],
        out_specs=[
            whole((rows, D)),
            whole((rows, D)),
            whole((blocks, rows, SLOT)),
            whole((D, D)),
            whole((D, FF)),
            whole((FF, D)),
            whole((8, D)),
        ],
        out_shape=[
            jax.ShapeDtypeStruct((rows, D), f32),
            jax.ShapeDtypeStruct((rows, D), f32),
            jax.ShapeDtypeStruct((blocks, rows, SLOT), bf16),
            jax.ShapeDtypeStruct((D, D), bf16),
            jax.ShapeDtypeStruct((D, FF), bf16),
            jax.ShapeDtypeStruct((FF, D), bf16),
            jax.ShapeDtypeStruct((8, D), f32),
        ],
        scratch_shapes=[
            VMEM((group, PAIR), bf16),
            VMEM((PAIR, rows), bf16),
            VMEM((D, rows), f32),
            VMEM((16, rows), f32),
            VMEM((D, D), bf16),
            VMEM((SLOT, D), bf16),
            VMEM((D, FF), bf16),
            VMEM((FF, D), bf16),
            pltpu.SemaphoreType.DMA((3,)),
        ],
        compiler_params=params(),
        name="layer",
    )(tok, mine, k, vt, qt, h0, cot, vec, b1, wo, w1, w2)


def back_prepare(tok_ref, own_ref, kt, vt):
    blocks, _, rows = tok_ref.shape
    for b in range(blocks):
        place = slice(b * rows, (b + 1) * rows)
        seg = onehot8(tok_ref[b, 17:18, :])
        seg = jnp.concatenate([seg, jnp.zeros((HEAD_DIM - 8, rows), f32)], axis=0)
        sub = lax.broadcasted_iota(jnp.int32, seg.shape, 0)
        k_ext = jnp.where((sub >= DOCS) & (sub < DOCS + 9), 1.0, jnp.where(sub < DOCS, seg, 0.0))
        v_ext = jnp.where((sub >= DOCS + 9) & (sub < DOCS + 18), 1.0, 0.0)
        kt_b = jnp.transpose(own_ref[place, SLOT : 2 * SLOT].astype(f32))
        vt_b = jnp.transpose(own_ref[place, 2 * SLOT :].astype(f32))
        kt[:, place] = jnp.concatenate([kt_b[:EXT], k_ext], axis=0).astype(bf16)
        vt[:, place] = jnp.concatenate([vt_b[:EXT], v_ext], axis=0).astype(bf16)


def back_block(per, q, msg, keys, kt, vt, dkt, dvt):
    lane = lax.broadcasted_iota(jnp.int32, q.shape, 1)
    m = msg.astype(f32)
    queries = jnp.where(lane < EXT, q.astype(f32), m)
    q_t = jnp.transpose(q.astype(f32)).astype(bf16)
    m_t = jnp.transpose(m).astype(bf16)
    dq = jnp.zeros(q.shape, f32)
    for h in range(per):
        head = slice(h * HEAD_DIM, (h + 1) * HEAD_DIM)
        mine = (lane >= h * HEAD_DIM) & (lane < (h + 1) * HEAD_DIM)
        low = EXT + DOCS + 3 * h
        barred = (lane >= EXT) & (lane < EXT + DOCS)
        use_q = mine | barred | ((lane >= low) & (lane < low + 3))
        use_m = mine | ((lane >= low + 9) & (lane < low + 12))
        probs = jnp.exp(dot(jnp.where(use_q, queries, 0.0).astype(bf16), kt[...]))
        score_grad = (probs * dot(jnp.where(use_m, m, 0.0).astype(bf16), vt[...])).astype(bf16)
        dvt[head, :] += dot(m_t[head], probs.astype(bf16))
        dkt[head, :] += dot(q_t[head], score_grad)
        dq = dq + jnp.where(mine, dot(score_grad, keys), 0.0)
    return (dq * SCALE).astype(bf16)


def back_kernel(per, tok_ref, own_ref, msg_ref, grad_ref, kt, vt, dkt, dvt):
    blocks, _, rows = tok_ref.shape
    back_prepare(tok_ref, own_ref, kt, vt)
    dkt[...] = jnp.zeros_like(dkt)
    dvt[...] = jnp.zeros_like(dvt)

    def step(b, carry):
        place = pl.ds(pl.multiple_of(b * rows, rows), rows)
        keys = own_ref[:, SLOT : 2 * SLOT]
        grad_ref[place, :SLOT] = back_block(per, own_ref[place, :SLOT], msg_ref[b], keys, kt, vt, dkt, dvt)
        return carry

    lax.fori_loop(0, blocks, step, 0)
    for b in range(blocks):
        place = slice(b * rows, (b + 1) * rows)
        grad_ref[place, SLOT : 2 * SLOT] = jnp.transpose(dkt[:, place]).astype(bf16)
        grad_ref[place, 2 * SLOT :] = jnp.transpose(dvt[:, place]).astype(bf16)


def back(tok, own, msg, per):
    group = own.shape[0]
    return pl.pallas_call(
        functools.partial(back_kernel, per),
        in_specs=[pl.BlockSpec(memory_space=VMEM)] * 3,
        out_specs=pl.BlockSpec(memory_space=VMEM),
        out_shape=jax.ShapeDtypeStruct(own.shape, bf16),
        scratch_shapes=[
            VMEM((SLOT, group), bf16),
            VMEM((SLOT, group), bf16),
            VMEM((SLOT, group), f32),
            VMEM((SLOT, group), f32),
        ],
        compiler_params=params(),
        name="attention_back",
    )(tok, own, msg)

def final_kernel(
    z_ref, tok_ref, grad_ref, normed_ref, lhs_ref, sc_ref, rhs_ref, h1g_ref, up_w_ref, vec_ref, own_w_ref, mean_ref,
    dw_ref, noise_ref, table_ref, small_ref, acc,
):
    i = pl.program_id(0)
    last = pl.num_programs(0) - 1
    vocab = table_ref.shape[1]
    mean = mean_ref[0:1, 0:1]

    @pl.when(i == 0)
    def _():
        acc[...] = jnp.zeros_like(acc)
        small_ref[...] = jnp.zeros_like(small_ref)
        table_ref[...] = jnp.zeros_like(table_ref)

    grad = grad_ref[...]
    hidden0 = dot(lhs_ref[0], rhs_ref[...], TN)
    unit, inverse = norm_parts(hidden0)
    norm_grad = dot(grad, own_w_ref[...], NT)
    acc[...] += dot(normed_ref[...], grad, TN)
    own = (z_ref[0] == i).astype(f32)
    h0_grad = (norm_pull(norm_grad, unit, inverse, vec_ref[1:2, :]) + own * h1g_ref[...]).astype(bf16)
    mixed_grad = dot(up_w_ref[...], h0_grad, NT)
    sc = sc_ref[0]
    noise_ref[0] = sc[17:18] * mixed_grad
    embedded_grad = sc[16:17] * mixed_grad
    picked = sc[:16]
    norm_term = -jnp.sum(embedded_grad * picked, axis=(0, 1), keepdims=True) / (mean * mean)
    ids = tok_ref[i][16:17, :]
    table3 = dot(jnp.concatenate(split3(embedded_grad / mean), axis=0).astype(bf16), id_matrix(vocab, ids), NT)
    table_ref[...] += table3[:16] + table3[16:32] + table3[32:48]
    gradf = grad.astype(f32)
    small_ref[...] += jnp.concatenate(
        [
            dot(lhs_ref[0, :16, :], h0_grad),
            column_sum(h0_grad.astype(f32)),
            column_sum(norm_grad * unit),
            column_sum(norm_grad),
            column_sum(gradf),
            jnp.broadcast_to(norm_term, (1, D)),
            jnp.zeros((3, D), f32),
        ],
        axis=0,
    )

    @pl.when(i == last)
    def _():
        dw_ref[...] = acc[...].astype(bf16)


def final(z, tok, grad, normed, lhs, sc, rhs, h1g, up_w, vec, own_w, mean, vocab):
    blocks, _, rows = tok.shape
    spec = pltpu.PrefetchScalarGridSpec(
        num_scalar_prefetch=1,
        grid=(blocks,),
        in_specs=[
            whole(tok.shape),
            pl.BlockSpec((rows, 3 * SLOT), lambda i, z: (i, 0)),
            pl.BlockSpec((rows, D), lambda i, z: (i, 0)),
            pl.BlockSpec((1, 48, rows), lambda i, z: (i, 0, 0)),
            pl.BlockSpec((1, 24, rows), lambda i, z: (i, 0, 0)),
            whole(rhs.shape),
            whole(h1g.shape),
            whole(up_w.shape),
            whole(vec.shape),
            whole(own_w.shape),
            whole(mean.shape),
        ],
        out_specs=[
            whole((D, 3 * SLOT)),
            pl.BlockSpec((1, 16, rows), lambda i, z: (i, 0, 0)),
            whole((16, vocab)),
            whole((24, D)),
        ],
        scratch_shapes=[VMEM((D, 3 * SLOT), f32)],
    )
    return pl.pallas_call(
        final_kernel,
        grid_spec=spec,
        out_shape=[
            jax.ShapeDtypeStruct((D, 3 * SLOT), bf16),
            jax.ShapeDtypeStruct((blocks, 16, rows), f32),
            jax.ShapeDtypeStruct((16, vocab), f32),
            jax.ShapeDtypeStruct((24, D), f32),
        ],
        compiler_params=params(),
        name="embed_back",
    )(z, tok, grad, normed, lhs, sc, rhs, h1g, up_w, vec, own_w, mean)


UNITS = (
    (1, 0, 768, True),
    (1, 768, 768, False),
    (1, 1536, 768, True),
    (1, 2304, 768, False),
    (0, 0, 384, True),
    (0, 384, 384, False),
    (2, 0, 384, True),
    (2, 384, 384, False),
    (3, 0, 384, True),
    (3, 384, 384, False),
)
UNIT_ROWS = (384, 96, 96, 96)
CORE, WIDE, NARROW, NEAR, FAR, DONE = range(6)
PLAN = {
    "chunk0": [(CORE, 0)],
    "chunk1": [(CORE, 1), (WIDE, 0)],
    "chunk2": [(CORE, 2), (WIDE, 1)],
    "chunk3": [(CORE, 3), (WIDE, 2)],
    "sent": [(CORE, 6), (CORE, 7), (WIDE, 3), (WIDE, 4), (WIDE, 5)],
    "prep": [(WIDE, 6), (WIDE, 7), (NARROW, 0), (NARROW, 1)],
    "q0": [],
    "q1": [(NARROW, 2), (NARROW, 3), (NEAR, 0), (NEAR, 1)],
    "q2": [(NARROW, 4), (NARROW, 5), (NEAR, 2), (NEAR, 3), (FAR, 0), (FAR, 1)],
    "q3": [(NARROW, 6), (NARROW, 7), (FAR, 2), (FAR, 3), (DONE, 0), (DONE, 1)],
    "kv": [(NEAR, 4), (NEAR, 5), (DONE, 2), (DONE, 3)],
    "dw": [(CORE, 8), (CORE, 9), (NEAR, 6), (NEAR, 7), (FAR, 4), (FAR, 5)],
    "e0": [(WIDE, 8), (WIDE, 9), (FAR, 6), (FAR, 7)],
    "e1": [(DONE, 4), (DONE, 5)],
    "e2": [(NARROW, 8), (NARROW, 9), (DONE, 6), (DONE, 7)],
    "e3": [],
}


def mega_kernel(
    per,
    plan,
    tok_ref,
    mine_ref,
    lse_ref,
    vec1_ref,
    vec2_ref,
    b1_ref,
    lhs_ref,
    sc_ref,
    rhs_ref,
    mean_ref,
    up_w_ref,
    att_hbm,
    h0_hbm,
    cot_hbm,
    wo_hbm,
    w1_hbm,
    w2_hbm,
    own_hbm,
    normed_hbm,
    own_w_hbm,
    out_hbm,
    dwo_out,
    dw1_out,
    dw2_out,
    dw_out,
    small_out,
    table_out,
    noise_out,
    dw2,
    dw1,
    dwo,
    dwq,
    h1g,
    msg_out,
    msgs,
    small1,
    msg_send,
    msg_recv,
    first2,
    chunk_send,
    chunk_recv,
    send_parts,
    parts,
    mine,
    lines,
    sums,
    dw_parts,
    noise_mine,
    noise_parts,
    sends,
    recvs,
    *scratch,
):
    blocks, _, rows = tok_ref.shape
    dp = lax.axis_index("dp")
    z = lax.axis_index("blk")
    dp_n, blk_n = parts.shape[0], lines.shape[0]
    group = blocks * rows
    half = D // 2
    grads = (dw2, dw1, dwo, dwq)
    outs = (dw2_out, dw1_out, dwo_out)
    scratch = list(scratch)
    units = []
    lines_of = []
    core, x, y = lax.rem(dp, 2), lax.rem(lax.div(dp, 2), 2), lax.div(dp, 4)
    sibling = (dp + 1 - 2 * core, z)

    def chunk_copy(c):
        at = (c // 2, c % 2)
        return remote(dw2.at[at + (1 - core,)], first2.at[at], chunk_send.at[c], chunk_recv.at[c], sibling)

    for which, first, size, by_x in UNITS:
        buffer = first2 if which == 0 else scratch.pop(0)
        rest = [scratch.pop(0) for _ in range(4)]
        chunks = [functools.partial(chunk_copy, c) for c in range(4)] if which == 0 else None
        units.append(Scatter(grads[which], pl.ds(first, size), by_x, buffer, *rest, chunks=chunks))
        if which != 3:
            lines_of.append(LineScatter(units[-1], outs[which], *[scratch.pop(0) for _ in range(6)]))

    def run(slot):
        for kind, n in plan[slot]:
            if kind == CORE:
                units[n].start()
            elif kind == WIDE:
                units[n].core_to_wide()
            elif kind == NARROW:
                units[n].wide_to_narrow()
            elif kind == NEAR:
                lines_of[n].start()
            elif kind == FAR:
                lines_of[n].near_to_far()
            else:
                lines_of[n].finish()

    def z_peer(k):
        low, high = lax.rem(z, 2), lax.div(z, 2)
        return (low + (k % 2) * (1 - 2 * low)) + 2 * (high + (k // 2) * (1 - 2 * high))

    def message(k):
        return remote(msg_out.at[z_peer(k)], msgs.at[k], msg_send.at[k], msg_recv.at[k], (dp, z_peer(k)))

    dp_to = [(lax.rem(dp + k, dp_n), z) for k in range(1, dp_n)]
    z_to = [(dp, lax.rem(z + k, blk_n)) for k in range(1, blk_n)]

    def dense(att_v, h0_v, cot_v, wo, w1, w2, wo_slots, sems):
        moves = [
            pltpu.make_async_copy(src, dst, sems.at[n])
            for n, (src, dst) in enumerate(
                ((wo_hbm, wo), (att_hbm, att_v), (h0_hbm, h0_v), (w1_hbm, w1), (cot_hbm, cot_v), (w2_hbm, w2))
            )
        ]
        for c in moves:
            c.start()
        sync(dp_to + z_to)
        for c in moves[:3]:
            c.wait()
        attended = att_v[...].astype(bf16)
        hidden1 = h0_v[...] + dot(attended, wo[...], TN) + vec2_ref[0:1, :]
        unit, inverse = norm_parts(hidden1)
        normed2 = (unit * vec2_ref[1:2, :] + vec2_ref[2:3, :]).astype(bf16)
        for c in moves[3:]:
            c.wait()
        cot = cot_v[...]
        out_grad = cot.astype(bf16)
        h0_v[...] = hidden1 + vec2_ref[3:4, :]
        h1g[...] = jnp.zeros_like(h1g)
        inner_sums = []
        for c in range(FF // D):
            cols = slice(c * D, (c + 1) * D)
            active, slope = gelu_parts(dot(normed2, w1[:, cols]) + b1_ref[c : c + 1, :])
            h0_v[...] += dot(active, w2[cols, :])
            inner_grad = (dot(out_grad, w2[cols, :], NT) * slope).astype(bf16)
            part = dot(active, out_grad, TN).astype(bf16)
            dw2[c // 2, c % 2, 0] = part[: D // 2]
            dw2[c // 2, c % 2, 1] = part[D // 2 :]
            chunk_copy(c).start()
            part = dot(normed2, inner_grad, TN).astype(bf16)
            for k in range(8):
                dw1[k // 4, k // 2 % 2, k % 2, :, cols] = part[k * 96 : (k + 1) * 96]
            h1g[...] += dot(inner_grad, w1[:, cols], NT)
            inner_sums.append(column_sum(inner_grad.astype(f32)))
            run(("chunk0", "chunk1", "chunk2", "chunk3")[c])
        norm_grad = h1g[...]
        write = pltpu.make_async_copy(h0_v, out_hbm, sems.at[0])
        write.start()
        hidden1_grad = cot + norm_pull(norm_grad, unit, inverse, vec2_ref[1:2, :])
        h1g[...] = hidden1_grad
        branch = hidden1_grad.astype(bf16)
        seg = onehot8(mine_ref[17:18, :])
        sub = lax.broadcasted_iota(jnp.int32, (8, rows), 0)
        barred = jnp.where(sub < DOCS, -BIG * (1.0 - seg), 0.0)[:DOCS]
        product = dot(wo[...], branch, NT).astype(bf16).astype(f32) * att_v[...]
        wo_slots[...] = jnp.zeros_like(wo_slots)
        size = per * HEAD_DIM
        for j in range(blocks):
            lse_parts = []
            delta_parts = []
            for h in range(per * j, per * (j + 1)):
                delta = column_sum(product[h * HEAD_DIM : (h + 1) * HEAD_DIM])
                lse_parts += split3(-lse_ref[h : h + 1, :])
                delta_parts += split3(-delta)
            rest = jnp.zeros((HEAD_DIM - DOCS - 6 * per, rows), f32)
            ext = [jnp.zeros((HEAD_DIM, rows), f32), barred] + lse_parts + delta_parts + [rest]
            ext = jnp.transpose(jnp.concatenate(ext, axis=0))
            wo_slots[:size, :] = wo[j * size : (j + 1) * size, :]
            grads = dot(branch, wo_slots[...], NT)
            msg_out[j, :, :PAIR] = grads[:, :PAIR].astype(bf16)
            msg_out[j, :, PAIR:] = (grads[:, PAIR:] + ext).astype(bf16)
        for k in (1, 2, 3):
            message(k).start()
        part = dot(attended, branch).astype(bf16)
        for k in range(8):
            dwo[k // 4, k // 2 % 2, k % 2] = part[k * 96 : (k + 1) * 96]
        small1[...] = jnp.concatenate(
            [
                column_sum(branch.astype(f32)),
                column_sum(norm_grad * unit),
                column_sum(norm_grad),
                column_sum(out_grad.astype(f32)),
                *inner_sums,
            ],
            axis=0,
        )
        run("sent")
        write.wait()

    pl.run_scoped(
        dense,
        VMEM((D, rows), f32),
        VMEM((rows, D), f32),
        VMEM((rows, D), f32),
        VMEM((D, D), bf16),
        VMEM((D, FF), bf16),
        VMEM((FF, D), bf16),
        VMEM((SLOT, D), bf16),
        pltpu.SemaphoreType.DMA((6,)),
    )

    def backward(grad, own, kt, vt, dkt, dvt, sem):
        load = pltpu.make_async_copy(own_hbm, own, sem)
        load.start()
        dkt[...] = jnp.zeros_like(dkt)
        dvt[...] = jnp.zeros_like(dvt)
        msgs[0] = msg_out[z]
        load.wait()
        back_prepare(tok_ref, own, kt, vt)
        run("prep")

        def body(b, carry):
            low, high = lax.rem(z, 2), lax.div(z, 2)
            b_low, b_high = lax.rem(b, 2), lax.div(b, 2)
            other = (low + b_low * (1 - 2 * low)) + 2 * (high + b_high * (1 - 2 * high))
            for k in range(blocks):
                if k or plan["q0"]:

                    @pl.when(b == k)
                    def _():
                        if k:
                            message(k).wait()
                        run(("q0", "q1", "q2", "q3")[k])

            place = pl.ds(pl.multiple_of(other * rows, rows), rows)
            keys = own[:, SLOT : 2 * SLOT]
            grad[place, :SLOT] = back_block(per, own[place, :SLOT], msgs[b], keys, kt, vt, dkt, dvt)
            return carry

        lax.fori_loop(0, blocks, body, 0)
        for b in range(blocks):
            place = slice(b * rows, (b + 1) * rows)
            grad[place, SLOT : 2 * SLOT] = jnp.transpose(dkt[:, place]).astype(bf16)
            grad[place, 2 * SLOT :] = jnp.transpose(dvt[:, place]).astype(bf16)

    def embedding(grad, normed, own_w, sems):
        loads = [
            pltpu.make_async_copy(normed_hbm, normed, sems.at[0]),
            pltpu.make_async_copy(own_w_hbm, own_w, sems.at[1]),
        ]
        for c in loads:
            c.start()
        run("kv")
        for c in loads:
            c.wait()
        part = dot(normed[...], grad[...], TN).astype(bf16)
        for k in range(8):
            dwq[k // 4, k // 2 % 2, k % 2] = part[k * 96 : (k + 1) * 96]
        run("dw")
        mean = mean_ref[0:1, 0:1]
        small2 = jnp.zeros((24, D), f32)
        vocab = dp_n * 128
        table = jnp.zeros((16, vocab), f32)
        for i in range(blocks):
            place = slice(i * rows, (i + 1) * rows)
            g = grad[place, :]
            hidden0 = dot(lhs_ref[i], rhs_ref[...], TN)
            unit, inverse = norm_parts(hidden0)
            norm_grad = dot(g, own_w[...], NT)
            mine_too = (z == i).astype(f32)
            h0_grad = (norm_pull(norm_grad, unit, inverse, vec1_ref[1:2, :]) + mine_too * h1g[...]).astype(bf16)
            mixed_grad = dot(up_w_ref[...], h0_grad, NT)
            sc = sc_ref[i]
            noise_mine[i] = sc[17:18] * mixed_grad
            embedded_grad = sc[16:17] * mixed_grad
            norm_term = -jnp.sum(embedded_grad * sc[:16], axis=(0, 1), keepdims=True) / (mean * mean)
            table3 = dot(
                jnp.concatenate(split3(embedded_grad / mean), axis=0).astype(bf16),
                id_matrix(vocab, tok_ref[i][16:17, :]),
                NT,
            )
            table = table + (table3[:16] + table3[16:32] + table3[32:48])
            small2 = small2 + jnp.concatenate(
                [
                    dot(lhs_ref[i, :16, :], h0_grad),
                    column_sum(h0_grad.astype(f32)),
                    column_sum(norm_grad * unit),
                    column_sum(norm_grad),
                    jnp.broadcast_to(norm_term, (1, D)),
                    *[(z == j).astype(f32) * column_sum(g.astype(f32)) for j in range(blocks)],
                ],
                axis=0,
            )
            run(("e0", "e1", "e2", "e3")[i])
        flat = jnp.concatenate([small1[...], small2], axis=0)
        for k in range(dp_n):
            n = k % 4
            send_parts[k, :, :half] = flat[8 * n : 8 * n + 8, (k // 4) * half : (k // 4 + 1) * half]
            send_parts[k, :, half : half + 128] = table[:8, k * 128 : (k + 1) * 128]
            send_parts[k, :, half + 128 :] = table[8:, k * 128 : (k + 1) * 128]

    def rest(grad):
        pl.run_scoped(
            functools.partial(backward, grad),
            VMEM((group, 3 * SLOT), bf16),
            VMEM((SLOT, group), bf16),
            VMEM((SLOT, group), bf16),
            VMEM((SLOT, group), f32),
            VMEM((SLOT, group), f32),
            pltpu.SemaphoreType.DMA,
        )
        pl.run_scoped(
            functools.partial(embedding, grad),
            VMEM((group, D), bf16),
            VMEM((D, 3 * SLOT), bf16),
            pltpu.SemaphoreType.DMA((2,)),
        )

    pl.run_scoped(rest, VMEM((group, 3 * SLOT), bf16))

    nd, nz = dp_n - 1, blk_n - 1

    def spread(src, dst, peers, first):
        return [remote(src(p), dst, sends.at[first + k], recvs.at[first + k], p) for k, p in enumerate(peers)]

    one = spread(lambda p: send_parts.at[p[0]], parts.at[dp], dp_to, 0)
    four = spread(lambda p: noise_mine.at[p[1]], noise_parts.at[z], z_to, 2 * nd + nz)
    for c in one + four:
        c.start()
    parts[dp] = send_parts[dp]
    noise_parts[z] = noise_mine[z]
    for u in units[8:]:
        total = u.narrow_sum()
        q = total.shape[0] // blk_n
        for k in range(blk_n):
            dw_parts[k, :, u.columns] = total[k * q : (k + 1) * q]
    five = spread(lambda p: dw_parts.at[p[1]], dw_out.at[z], z_to, 2 * nd + 2 * nz)
    for c in five:
        c.start()
    dw_out[z] = dw_parts[z]
    for c in one:
        c.wait()
    total = parts[0]
    for k in range(1, dp_n):
        total = total + parts[k]
    mine[...] = total
    lines[z] = total
    two = spread(lambda p: mine, lines.at[z], z_to, nd)
    for c in two:
        c.start()
    for c in four:
        c.wait()
    total = noise_parts[0]
    for k in range(1, blk_n):
        total = total + noise_parts[k]
    noise_out[...] = total
    for c in two:
        c.wait()
    total = lines[0]
    for k in range(1, blk_n):
        total = total + lines[k]
    table_out[...] = total[:, half:]
    sums[...] = total[:, :half]
    small_out[dp] = total[:, :half]
    three = spread(lambda p: sums, small_out.at[dp], dp_to, nd + nz)
    for c in three:
        c.start()
    for c in three + five:
        c.wait()


def mega(small, big, dp_n, per):
    tok, mine, att, lse, h0, cot, vec1, vec2, b1, lhs, sc, rhs, mean, up_w = small
    blk_n, _, rows = tok.shape
    group = blk_n * rows
    share = D // (dp_n * blk_n)
    vmem = pl.BlockSpec(memory_space=VMEM)
    hbm = pl.BlockSpec(memory_space=pl.ANY)
    count = 2 * (dp_n - 1) + 3 * (blk_n - 1)
    half = D // 2
    scratch = []
    for which, _, size, _ in UNITS:
        scratch += scatter_scratch(UNIT_ROWS[which], size, which != 0)
        if which != 3:
            scratch += line_scratch(UNIT_ROWS[which], size)
    in_vmem = (tok, mine, lse, vec1, vec2, b1, lhs, sc, rhs, mean, up_w)
    in_hbm = (att, h0, cot) + tuple(big)
    return pl.pallas_call(
        functools.partial(mega_kernel, per, PLAN),
        in_specs=[vmem] * len(in_vmem) + [hbm] * len(in_hbm),
        out_specs=[hbm] + [vmem] * 7,
        out_shape=[
            jax.ShapeDtypeStruct((rows, D), f32),
            jax.ShapeDtypeStruct((share, D), f32),
            jax.ShapeDtypeStruct((share, FF), f32),
            jax.ShapeDtypeStruct((4 * share, D), f32),
            jax.ShapeDtypeStruct((blk_n, share, 3 * SLOT), f32),
            jax.ShapeDtypeStruct((dp_n, 8, half), f32),
            jax.ShapeDtypeStruct((8, 256), f32),
            jax.ShapeDtypeStruct((16, rows), f32),
        ],
        scratch_shapes=[
            VMEM((2, 2, 2, 384, D), bf16),
            VMEM((2, 2, 2, 96, FF), bf16),
            VMEM((2, 2, 2, 96, D), bf16),
            VMEM((2, 2, 2, 96, 3 * SLOT), bf16),
            VMEM((rows, D), f32),
            VMEM((blk_n, rows, SLOT), bf16),
            VMEM((blk_n, rows, SLOT), bf16),
            VMEM((8, D), f32),
            pltpu.SemaphoreType.DMA((blk_n,)),
            pltpu.SemaphoreType.DMA((blk_n,)),
            VMEM((2, 2, 384, D), bf16),
            pltpu.SemaphoreType.DMA((4,)),
            pltpu.SemaphoreType.DMA((4,)),
            VMEM((dp_n, 8, half + 256), f32),
            VMEM((dp_n, 8, half + 256), f32),
            VMEM((8, half + 256), f32),
            VMEM((blk_n, 8, half + 256), f32),
            VMEM((8, half), f32),
            VMEM((blk_n, share, 3 * SLOT), f32),
            VMEM((blk_n, 16, rows), f32),
            VMEM((blk_n, 16, rows), f32),
            pltpu.SemaphoreType.DMA((count,)),
            pltpu.SemaphoreType.DMA((count,)),
            *scratch,
        ],
        compiler_params=pltpu.CompilerParams(
            vmem_limit_bytes=63 * MIB, collective_id=1, has_side_effects=True
        ),
        name="layer_and_sums",
    )(*in_vmem, *in_hbm)


def shards(
    dp_n,
    blk_n,
    token_ids,
    segment_ids,
    timesteps,
    noise,
    table,
    up_weight,
    up_bias,
    norm1_gain,
    norm1_shift,
    qkv_weight,
    query_bias,
    value_bias,
    out_weight,
    out_bias,
    norm2_gain,
    norm2_shift,
    ffn_in_weight,
    ffn_in_bias,
    ffn_out_weight,
    ffn_out_bias,
    cotangent,
):
    rows = token_ids.shape[0]
    local_rows = table.shape[0]
    vp = -(-local_rows // 128) * 128
    per = -(-HEADS // blk_n)
    width = per * HEAD_DIM
    z = lax.axis_index("blk")
    z1 = z.reshape(1).astype(jnp.int32)

    slots = (token_ids // local_rows) * vp + token_ids % local_rows
    scalars = jnp.stack([slots, segment_ids, timesteps]).astype(f32)
    mine = jnp.concatenate([noise.T, scalars, jnp.zeros((5, rows), f32)], axis=0)
    tab_mine = jnp.pad(table.T, ((0, 0), (0, vp - local_rows)))
    near = dp_n == 8 and blk_n == 4
    if near:
        tok, tab = gather(mine, tab_mine, dp_n, blk_n)
    else:
        tok = lax.all_gather(mine, "blk")
        tab = lax.all_gather(tab_mine, "dp")

    padded = blk_n * width
    split = jnp.pad(qkv_weight.reshape(D, 3, D), ((0, 0), (0, 0), (0, padded - D)))
    own_w = lax.dynamic_slice(split, (0, 0, z * width), (D, 3, width))
    own_w = jnp.pad(own_w, ((0, 0), (0, 0), (0, SLOT - width))).reshape(D, 3 * SLOT)
    bias = jnp.pad(jnp.stack([query_bias, jnp.zeros((D,), f32), value_bias]), ((0, 0), (0, padded - D)))
    own_b = lax.dynamic_slice(bias, (0, z * width), (3, width))
    own_b = jnp.pad(own_b, ((0, 0), (0, SLOT - width))).reshape(1, 3 * SLOT)
    vec1 = jnp.stack([up_bias, norm1_gain, norm1_shift, query_bias, value_bias])
    k, vt, own, normed, lhs, sc, qt, h0, rhs, mean = embed(
        z1, tok, tab, up_weight, vec1, qkv_weight, own_w, own_b, local_rows
    )
    vec2 = jnp.stack([out_bias, norm2_gain, norm2_shift, ffn_out_bias])
    b1 = ffn_in_bias.reshape(FF // D, D)
    share = D // (dp_n * blk_n)
    if near:
        att, lse = attention(tok, mine, k, vt, qt)
        block_out, dwo, dw1, dw2, dw, flat, table_total, noise_grad = mega(
            (tok, mine, att, lse, h0, cotangent, vec1, vec2, b1, lhs, sc, rhs, mean, up_weight),
            (out_weight, ffn_in_weight, ffn_out_weight, own, normed, own_w),
            dp_n,
            per,
        )
        noise_grad = noise_grad.T
        flat = flat.reshape(-1, D // 2)
        flat = jnp.concatenate([flat[:32], flat[32:]], axis=1)
        small1, small2 = flat[:8], flat[8:28]
        norm_grad = flat[27, 0]
        own_sums = flat[28:32].reshape(blk_n, 3, SLOT)[:, :, :width].transpose(1, 0, 2).reshape(3, padded)
        table_grad = table_total.reshape(8, 2, vp).transpose(1, 0, 2).reshape(16, vp)
    else:
        block_out, h1g, msg, dwo, dw1, dw2, small1 = layer(
            tok, mine, k, vt, qt, h0, cotangent, vec2, b1, out_weight, ffn_in_weight, ffn_out_weight, per
        )
        msg = lax.all_to_all(msg, "blk", 0, 0)
        grad = back(tok, own, msg, per)
        dw, noise_part, table_part, small2 = final(
            z1, tok, grad, normed, lhs, sc, rhs, h1g, up_weight, vec1, own_w, mean, dp_n * vp
        )
        noise_grad = lax.psum_scatter(noise_part, "blk", scatter_dimension=0, tiled=False).T
        own_sums = small2[19].reshape(3, SLOT)[:, :width]
        own_sums = lax.dynamic_update_slice(jnp.zeros((3, padded), f32), own_sums, (0, z * width))[:, :D]
        small2, table_total, small1, own_sums = lax.psum((small2, table_part, small1, own_sums), ("dp", "blk"))
        scatter = functools.partial(lax.psum_scatter, axis_name=("dp", "blk"), scatter_dimension=0, tiled=True)
        dwo, dw1, dw2 = scatter(dwo), scatter(dw1), scatter(dw2)
        dw = lax.psum_scatter(dw, "dp", scatter_dimension=0, tiled=True)
        dw = lax.all_to_all(dw.reshape(blk_n, share, 3 * SLOT), "blk", 0, 0)
        norm_grad = small2[20, 0]
        table_grad = lax.dynamic_slice(table_total, (0, lax.axis_index("dp") * vp), (16, vp))
    dw = dw.reshape(blk_n, share, 3, SLOT)[..., :width].transpose(1, 2, 0, 3).reshape(share, 3, padded)[..., :D]
    qkv_weight_grad = dw.reshape(share, 3 * D).astype(f32)
    mean_norm = mean[0, 0]
    table_grad = table_grad[:, :local_rows].T
    norms = jnp.sqrt(jnp.sum(table * table, axis=-1, keepdims=True) + 1.0)
    table_grad = table_grad + norm_grad * table / (dp_n * local_rows * norms)
    return (
        block_out,
        noise_grad,
        table_grad,
        small2[:16],
        small2[16],
        small2[17],
        small2[18],
        qkv_weight_grad,
        own_sums[0],
        own_sums[2],
        dwo.astype(f32),
        small1[0],
        small1[1],
        small1[2],
        dw1.astype(f32),
        small1[4:8].reshape(FF),
        dw2.astype(f32),
        small1[3],
        mean_norm,
    )


def solution(mesh):
    rows = P(("dp", "blk"))
    wide = P(("dp", "blk"), None)
    in_specs = (rows, rows, rows, wide, P("dp", None)) + (P(),) * 15 + (wide,)
    out_specs = (
        (wide, wide, P("dp", None))
        + (P(),) * 4
        + (wide, P(), P(), wide, P(), P(), P(), wide, P(), wide, P(), P())
    )
    body = functools.partial(shards, mesh.shape["dp"], mesh.shape["blk"])
    return jax.shard_map(body, mesh=mesh, in_specs=in_specs, out_specs=out_specs, check_vma=False)
```

```python
import functools
import math

import jax
import jax.numpy as jnp
from jax import lax
from jax.experimental import pallas as pl
from jax.experimental.pallas import tpu as pltpu
from jax.sharding import PartitionSpec as P

D = 768
HEADS = 12
HEAD_DIM = 64
FF = 3072
EMB = 16
TSTEPS = 2000
DOCS = 4
PAIR = 2 * HEAD_DIM
SLOT = 256
EXT = 192
BIG = 1e30
SAFE = 64.0
SCALE = HEAD_DIM**-0.5
MIB = 2**20
MESH = pl.DeviceIdType.MESH
VMEM = pltpu.VMEM
f32 = jnp.float32
bf16 = jnp.bfloat16

NN = (((1,), (0,)), ((), ()))
NT = (((1,), (1,)), ((), ()))
TN = (((0,), (0,)), ((), ()))
TT = (((0,), (1,)), ((), ()))


def dot(left, right, dims=NN):
    return lax.dot_general(left, right, dims, preferred_element_type=f32)


def split3(x):
    high = x.astype(bf16)
    rest = x - high.astype(f32)
    middle = rest.astype(bf16)
    low = (rest - middle.astype(f32)).astype(bf16)
    return high.astype(f32), middle.astype(f32), low.astype(f32)


def column_sum(x):
    return jnp.sum(x, axis=0, keepdims=True)


def row_mean(x):
    return jnp.mean(x, axis=-1, keepdims=True)


def norm_parts(x):
    centered = x - row_mean(x)
    inverse = lax.rsqrt(row_mean(centered * centered) + 1e-05)
    return centered * inverse, inverse


def norm_pull(grad, unit, inverse, gain):
    scaled = grad * gain
    return inverse * (scaled - row_mean(scaled) - unit * row_mean(scaled * unit))


def onehot8(row):
    return (lax.broadcasted_iota(jnp.int32, (8, row.shape[1]), 0) == row.astype(jnp.int32)).astype(f32)


def id_matrix(rows, row):
    return (lax.broadcasted_iota(jnp.int32, (rows, row.shape[1]), 0) == row.astype(jnp.int32)).astype(f32).astype(bf16)


def params(**kw):
    return pltpu.CompilerParams(vmem_limit_bytes=60 * MIB, **kw)


def whole(shape):
    return pl.BlockSpec(shape, lambda *_: (0,) * len(shape))


def remote(src, dst, send, recv, peer):
    return pltpu.make_async_remote_copy(
        src_ref=src, dst_ref=dst, send_sem=send, recv_sem=recv, device_id=peer, device_id_type=MESH
    )


def greet(peers):
    barrier = pltpu.get_barrier_semaphore()
    for peer in peers:
        pl.semaphore_signal(barrier, inc=1, device_id=peer, device_id_type=MESH)


def met(peers):
    pl.semaphore_wait(pltpu.get_barrier_semaphore(), len(peers))


def gather_kernel(
    dp_n, blk_n, local_rows, ids_ref, seg_ref, steps_ref, noise_ref, table_ref, tok_ref, tab_ref, mine, own, send, recv
):
    dp = lax.axis_index("dp")
    z = lax.axis_index("blk")
    dp_peers = [(lax.rem(dp + k, dp_n), z) for k in range(1, dp_n)]
    z_peers = [(dp, lax.rem(z + k, blk_n)) for k in range(1, blk_n)]
    greet(z_peers + dp_peers)
    rows = ids_ref.shape[0]
    vp = own.shape[1]
    ids = ids_ref[...].reshape(1, rows).astype(f32)
    mine[...] = jnp.zeros_like(mine)
    mine[:16, :] = noise_ref[...]
    mine[16:17, :] = ids + (vp - local_rows) * jnp.floor((ids + 0.5) / local_rows)
    mine[17:18, :] = seg_ref[...].reshape(1, rows).astype(f32)
    mine[18:19, :] = steps_ref[...].reshape(1, rows).astype(f32)
    own[...] = jnp.zeros_like(own)
    own[:, :local_rows] = table_ref[...]
    met(z_peers + dp_peers)
    copies = []
    for k, peer in enumerate(z_peers):
        copies.append(remote(mine, tok_ref.at[z], send.at[k], recv.at[k], peer))
    for k, peer in enumerate(dp_peers):
        n = len(z_peers) + k
        copies.append(remote(own, tab_ref.at[dp], send.at[n], recv.at[n], peer))
    for c in copies:
        c.start()
    tok_ref[z] = mine[...]
    tab_ref[dp] = own[...]
    for c in copies:
        c.wait()


def gather(ids, segments, steps, noise, table, dp_n, blk_n):
    count = dp_n + blk_n - 2
    rows = ids.shape[0]
    local_rows = table.shape[1]
    vp = -(-local_rows // 128) * 128
    vmem = pl.BlockSpec(memory_space=VMEM)
    return pl.pallas_call(
        functools.partial(gather_kernel, dp_n, blk_n, local_rows),
        in_specs=[vmem] * 5,
        out_specs=[vmem, vmem],
        out_shape=[
            jax.ShapeDtypeStruct((blk_n, 24, rows), f32),
            jax.ShapeDtypeStruct((dp_n, 16, vp), f32),
        ],
        scratch_shapes=[
            VMEM((24, rows), f32),
            VMEM((16, vp), f32),
            pltpu.SemaphoreType.DMA((count,)),
            pltpu.SemaphoreType.DMA((count,)),
        ],
        compiler_params=params(collective_id=0, has_side_effects=True),
        name="gather",
    )(ids, segments, steps, noise, table)


class Scatter:
    def __init__(self, grad, columns, by_x, first, second, third, send, recv, chunks=None):
        self.grad, self.columns, self.by_x = grad, columns, by_x
        self.first, self.second, self.third = first, second, third
        self.send, self.recv, self.chunks = send, recv, chunks
        self.dp = lax.axis_index("dp")
        self.z = lax.axis_index("blk")
        self.core = lax.rem(self.dp, 2)
        self.x = lax.rem(lax.div(self.dp, 2), 2)
        self.y = lax.div(self.dp, 4)

    def flip(self, bit, step):
        return (self.dp + step * (1 - 2 * bit), self.z)

    def own(self, y, x):
        return self.grad[y, x, self.core, :, self.columns].astype(f32)

    def core_copy(self):
        src = self.grad.at[:, :, 1 - self.core, :, self.columns]
        return remote(src, self.first, self.send.at[0], self.recv.at[0], self.flip(self.core, 1))

    def wide(self):
        if self.by_x:
            src, peer = self.grad.at[:, 1 - self.x, self.core, :, self.columns], self.flip(self.x, 2)
        else:
            src, peer = self.grad.at[1 - self.y, :, self.core, :, self.columns], self.flip(self.y, 4)
        return remote(src, self.second, self.send.at[1], self.recv.at[1], peer)

    def narrow(self):
        if self.by_x:
            src, peer = self.grad.at[1 - self.y, self.x, self.core, :, self.columns], self.flip(self.y, 4)
        else:
            src, peer = self.grad.at[self.y, 1 - self.x, self.core, :, self.columns], self.flip(self.x, 2)
        return remote(src, self.third, self.send.at[2], self.recv.at[2], peer)

    def start(self):
        self.core_copy().start()

    def core_to_wide(self):
        if self.chunks is None:
            self.core_copy().wait()
        elif self.by_x:
            for c in self.chunks:
                c().wait()
        for y in range(2):
            for x in range(2):
                if self.chunks is None:
                    other = self.first[y, x]
                else:
                    other = self.first[y, x, :, self.columns]
                self.grad[y, x, self.core, :, self.columns] = (self.own(y, x) + other.astype(f32)).astype(bf16)
        self.wide().start()

    def wide_to_narrow(self):
        self.wide().wait()
        for n in range(2):
            y, x = (n, self.x) if self.by_x else (self.y, n)
            total = self.own(y, x) + self.second[n].astype(f32)
            self.grad[y, x, self.core, :, self.columns] = total.astype(bf16)
        self.narrow().start()

    def narrow_sum(self):
        self.narrow().wait()
        return self.own(self.y, self.x) + self.third[...].astype(f32)


def scatter_scratch(rows, columns, first=True):
    return ([VMEM((2, 2, rows, columns), bf16)] if first else []) + [
        VMEM((2, rows, columns), bf16),
        VMEM((rows, columns), bf16),
        pltpu.SemaphoreType.DMA((3,)),
        pltpu.SemaphoreType.DMA((3,)),
    ]


class LineScatter:
    def __init__(self, bases, out, half, first, rest, kept, second, send, recv):
        self.bases, self.out = bases, out
        self.half, self.first, self.rest, self.kept, self.second = half, first, rest, kept, second
        self.send, self.recv = send, recv
        self.dp, self.z = bases[0].dp, bases[0].z
        self.low = lax.rem(self.z, 2)
        self.high = lax.div(self.z, 2)

    def near(self):
        peer = (self.dp, self.z + 1 - 2 * self.low)
        return remote(self.half.at[1 - self.low], self.first, self.send.at[0], self.recv.at[0], peer)

    def far(self):
        peer = (self.dp, self.z + 2 - 4 * self.high)
        return remote(self.rest, self.second, self.send.at[1], self.recv.at[1], peer)

    def start(self):
        q = self.kept.shape[0] // 2
        totals = [base.narrow_sum().astype(bf16) for base in self.bases]
        for low in range(2):
            for high in range(2):
                for n in range(2):
                    block = 2 * high + low
                    self.half[low, pl.ds((2 * high + n) * q, q), :] = totals[n][block * q : (block + 1) * q]
        self.near().start()

    def near_to_far(self):
        self.near().wait()
        size = self.kept.shape[0]
        mine = pl.ds(pl.multiple_of(self.high * size, size), size)
        other = pl.ds(pl.multiple_of((1 - self.high) * size, size), size)
        self.rest[...] = (self.half[self.low, other, :].astype(f32) + self.first[other, :].astype(f32)).astype(bf16)
        self.far().start()
        self.kept[...] = self.half[self.low, mine, :].astype(f32) + self.first[mine, :].astype(f32)

    def finish(self):
        self.far().wait()
        total = self.kept[...] + self.second[...].astype(f32)
        q = total.shape[0] // 2
        for n in range(2):
            self.out[:, self.bases[n].columns] = total[n * q : (n + 1) * q]


def line_scratch(rows, columns):
    return [
        VMEM((2, rows, columns), bf16),
        VMEM((rows, columns), bf16),
        VMEM((rows // 2, columns), bf16),
        VMEM((rows // 2, columns), f32),
        VMEM((rows // 2, columns), bf16),
        pltpu.SemaphoreType.DMA((2,)),
        pltpu.SemaphoreType.DMA((2,)),
    ]


def row(ref):
    return ref[...].reshape(1, ref.shape[0])


def own_columns(per, z, w_ref, qb_ref, vb_ref, own_w, own_b):
    start = z * (per * HEAD_DIM)
    base = pl.multiple_of(start // 128 * 128, 128)
    line = lax.broadcasted_iota(jnp.int32, (SLOT, SLOT), 0)
    lane = lax.broadcasted_iota(jnp.int32, (SLOT, SLOT), 1)
    move = ((line == lane + (start - base)) & (lane < per * HEAD_DIM)).astype(f32).astype(bf16)
    for n in range(3):
        part = w_ref[:, pl.ds(pl.multiple_of(n * D + base, 128), SLOT)]
        own_w[:, n * SLOT : (n + 1) * SLOT] = dot(part, move).astype(bf16)
    own_b[...] = jnp.zeros_like(own_b)
    for n, ref in ((0, qb_ref), (2, vb_ref)):
        part = jnp.concatenate(split3(jnp.broadcast_to(ref[pl.ds(base, SLOT)].reshape(1, SLOT), (8, SLOT))), axis=0)
        part = dot(part.astype(bf16), move)
        own_b[:, n * SLOT : (n + 1) * SLOT] = part[:8] + part[8:16] + part[16:]


def embed_kernel(
    local_rows,
    per,
    z_ref,
    tok_ref,
    tab_ref,
    up_w_ref,
    up_b_ref,
    gain_ref,
    shift_ref,
    qb_ref,
    vb_ref,
    w_ref,
    *refs,
):
    if per:
        *outs, own_w, tab3, vcol, own_b = refs
        embed_body(local_rows, z_ref, tok_ref, tab_ref, up_w_ref, up_b_ref, gain_ref, shift_ref, qb_ref, vb_ref, w_ref,
                   own_b, own_w, per, *outs, tab3, vcol)
    else:
        embed_body(local_rows, z_ref, tok_ref, tab_ref, up_w_ref, up_b_ref, gain_ref, shift_ref, qb_ref, vb_ref, w_ref,
                   refs[1], refs[0], per, *refs[2:])


def embed_body(
    local_rows,
    z_ref,
    tok_ref,
    tab_ref,
    up_w_ref,
    up_b_ref,
    gain_ref,
    shift_ref,
    qb_ref,
    vb_ref,
    w_ref,
    own_b_ref,
    own_w_ref,
    per,
    k_ref,
    vt_ref,
    own_ref,
    normed_ref,
    lhs_ref,
    sc_ref,
    qt_ref,
    h0_ref,
    rhs_ref,
    mean_ref,
    tab3,
    vcol,
):
    i = pl.program_id(0)
    dp_n, _, vp = tab_ref.shape
    blocks, _, rows = tok_ref.shape

    @pl.when(i == 0)
    def _():
        if per:
            own_columns(per, z_ref[0], w_ref, qb_ref, vb_ref, own_w_ref, own_b_ref)
        table = jnp.concatenate([tab_ref[j] for j in range(dp_n)], axis=1)
        squares = jnp.sum(table * table, axis=0, keepdims=True)
        lane = lax.broadcasted_iota(jnp.int32, squares.shape, 1)
        norms = jnp.where(lane % vp < local_rows, jnp.sqrt(squares + 1.0), 0.0)
        mean_ref[...] = jnp.broadcast_to(jnp.sum(norms, axis=1, keepdims=True) / (local_rows * dp_n), (8, 128))
        tab3[...] = jnp.concatenate(split3(table), axis=0).astype(bf16)
        segments = tok_ref[:, 17, :]
        steps = tok_ref[:, 18, :]
        sub = lax.broadcasted_iota(jnp.int32, (8, 1), 0)
        time = jnp.zeros((8, 1), f32)
        for s in range(DOCS):
            own = jnp.max(jnp.where(segments == float(s), steps, 0.0), axis=(0, 1), keepdims=True)
            time = jnp.where(sub == s, own, time)
        lane = lax.broadcasted_iota(jnp.int32, (8, D), 1)
        half = D // 2
        index = jnp.where(lane < half, lane, lane - half).astype(f32)
        angle = time * jnp.exp(index * (-math.log(10000.0) / half))
        wave = jnp.where(lane < half, jnp.sin(angle), jnp.cos(angle)) + row(up_b_ref)
        parts = split3(wave)
        rhs_ref[...] = jnp.concatenate([up_w_ref[...].astype(f32), *parts, jnp.zeros((8, D), f32)], axis=0).astype(bf16)
        bias = jnp.concatenate([row(qb_ref), row(vb_ref), jnp.zeros((6, D), f32)], axis=0)
        vcol[...] = jnp.transpose(bias)

    tok = tok_ref[i]
    ids = tok[16:17, :]
    picked3 = dot(tab3[...], id_matrix(dp_n * vp, ids))
    picked = picked3[:16] + picked3[16:32] + picked3[32:48]
    mean = mean_ref[0:1, 0:1]
    alpha_bar = 1.0 - jnp.sqrt(tok[18:19, :] / TSTEPS + 0.0001)
    signal = jnp.sqrt(alpha_bar)
    noise_scale = jnp.sqrt(1.0 - alpha_bar)
    mixed = signal * (picked / mean) + noise_scale * tok[:16]
    seg = onehot8(tok[17:18, :])
    lhs = jnp.concatenate([mixed, seg, seg, seg, jnp.zeros((8, rows), f32)], axis=0).astype(bf16)
    lhs_ref[0] = lhs
    sc_ref[0] = jnp.concatenate([picked, signal, noise_scale, jnp.zeros((6, rows), f32)], axis=0)
    hidden0 = dot(lhs, rhs_ref[...], TN)
    unit, _ = norm_parts(hidden0)
    normed = (unit * row(gain_ref) + row(shift_ref)).astype(bf16)
    normed_ref[...] = normed
    k_ref[...] = dot(normed, w_ref[:, D : 2 * D]).astype(bf16)
    vt_ref[...] = (dot(w_ref[:, 2 * D :], normed, TT) + vcol[:, 1:2]).astype(bf16)
    own = dot(normed, own_w_ref[...]) + own_b_ref[0:1, :]
    own_ref[:, :SLOT] = (own[:, :SLOT] * SCALE).astype(bf16)
    own_ref[:, SLOT:] = own[:, SLOT:].astype(bf16)

    @pl.when(i == z_ref[0])
    def _():
        h0_ref[...] = hidden0
        q = (dot(w_ref[:, :D], normed, TT) + vcol[:, 0:1]).astype(bf16)
        qt_ref[...] = (q.astype(f32) * SCALE).astype(bf16)


def embed(z, tok, tab, up_w, vectors, w, local_rows, per, own_w=None, own_b=None):
    blocks, _, rows = tok.shape
    group = blocks * rows
    vocab = tab.shape[0] * tab.shape[2]
    operands = (tok, tab, up_w, *vectors, w) + (() if per else (own_w, own_b))
    own_out = [whole((D, 3 * SLOT))] if per else []
    spec = pltpu.PrefetchScalarGridSpec(
        num_scalar_prefetch=1,
        grid=(blocks,),
        in_specs=[whole(x.shape) for x in operands],
        out_specs=[
            pl.BlockSpec((rows, D), lambda i, z: (i, 0)),
            pl.BlockSpec((D, rows), lambda i, z: (0, i)),
            pl.BlockSpec((rows, 3 * SLOT), lambda i, z: (i, 0)),
            pl.BlockSpec((rows, D), lambda i, z: (i, 0)),
            pl.BlockSpec((1, 48, rows), lambda i, z: (i, 0, 0)),
            pl.BlockSpec((1, 24, rows), lambda i, z: (i, 0, 0)),
            whole((D, rows)),
            whole((rows, D)),
            whole((48, D)),
            whole((8, 128)),
        ]
        + own_out,
        scratch_shapes=[VMEM((48, vocab), bf16), VMEM((D, 8), f32)] + ([VMEM((8, 3 * SLOT), f32)] if per else []),
    )
    return pl.pallas_call(
        functools.partial(embed_kernel, local_rows, per),
        grid_spec=spec,
        out_shape=[
            jax.ShapeDtypeStruct((group, D), bf16),
            jax.ShapeDtypeStruct((D, group), bf16),
            jax.ShapeDtypeStruct((group, 3 * SLOT), bf16),
            jax.ShapeDtypeStruct((group, D), bf16),
            jax.ShapeDtypeStruct((blocks, 48, rows), bf16),
            jax.ShapeDtypeStruct((blocks, 24, rows), f32),
            jax.ShapeDtypeStruct((D, rows), bf16),
            jax.ShapeDtypeStruct((rows, D), f32),
            jax.ShapeDtypeStruct((48, D), bf16),
            jax.ShapeDtypeStruct((8, 128), f32),
        ]
        + ([jax.ShapeDtypeStruct((D, 3 * SLOT), bf16)] if per else []),
        compiler_params=params(),
        name="embed",
    )(z, *operands)


ROOT = math.sqrt(2.0 / math.pi)


def attend(p, tok_ref, mine_ref, k_ref, vt_ref, qt_ref, att, lse, kext, qext):
    blocks, _, rows = tok_ref.shape

    @pl.when(p == 0)
    def _():
        for b in range(blocks):
            seg = jnp.concatenate([onehot8(tok_ref[b, 17:18, :]), jnp.zeros((120, rows), f32)], axis=0)
            kext[b * rows : (b + 1) * rows, :] = jnp.transpose(seg).astype(bf16)
        seg = onehot8(mine_ref[17:18, :])
        sub = lax.broadcasted_iota(jnp.int32, seg.shape, 0)
        barred = jnp.where(sub < DOCS, -BIG * (1.0 - seg), 0.0)
        qext[...] = jnp.concatenate([barred, jnp.zeros((120, rows), f32)], axis=0).astype(bf16)

    k = k_ref[...]
    keys = jnp.concatenate([k, kext[...]], axis=1)
    zeros = jnp.zeros((HEAD_DIM, rows), bf16)
    ones = jnp.ones((HEAD_DIM, blocks * rows), bf16)
    largest = jnp.max(jnp.abs(k), axis=0, keepdims=True).astype(f32)
    bound = jnp.max(dot(jnp.broadcast_to(largest, (8, PAIR)).astype(bf16), jnp.abs(qt_ref[...])))

    def heads(shifted):
        results = []
        for h in range(2):
            q = qt_ref[h * HEAD_DIM : (h + 1) * HEAD_DIM, :]
            v = vt_ref[h * HEAD_DIM : (h + 1) * HEAD_DIM, :]
            queries = jnp.concatenate([q, zeros, qext[...]] if h == 0 else [zeros, q, qext[...]], axis=0)
            scores = dot(keys, queries)
            if shifted:
                top = jnp.max(scores, axis=0, keepdims=True)
                scores = scores - top
            total = dot(jnp.concatenate([v, ones], axis=0), jnp.exp(scores).astype(bf16))
            results.append(total[:HEAD_DIM] / total[HEAD_DIM:])
            log_sum = jnp.log(total[HEAD_DIM : HEAD_DIM + 1])
            lse[pl.ds(2 * p + h, 1), :] = log_sum + top if shifted else log_sum
        att[pl.ds(pl.multiple_of(p * PAIR, PAIR), PAIR), :] = jnp.concatenate(results, axis=0)

    safe = bound < SAFE
    pl.when(safe)(lambda: heads(False))
    pl.when(jnp.logical_not(safe))(lambda: heads(True))


def attention_kernel(z_ref, tok_ref, k_ref, vt_ref, qt_ref, att, lse, kext, qext):
    attend(pl.program_id(0), tok_ref, tok_ref.at[z_ref[0]], k_ref, vt_ref, qt_ref, att, lse, kext, qext)


def attention(z, tok, k, vt, qt):
    blocks, _, rows = tok.shape
    group = blocks * rows
    spec = pltpu.PrefetchScalarGridSpec(
        num_scalar_prefetch=1,
        grid=(HEADS // 2,),
        in_specs=[
            whole(tok.shape),
            pl.BlockSpec((group, PAIR), lambda p, z: (0, p)),
            pl.BlockSpec((PAIR, group), lambda p, z: (p, 0)),
            pl.BlockSpec((PAIR, rows), lambda p, z: (p, 0)),
        ],
        out_specs=[whole((D, rows)), whole((16, rows))],
        scratch_shapes=[VMEM((group, PAIR), bf16), VMEM((PAIR, rows), bf16)],
    )
    return pl.pallas_call(
        attention_kernel,
        grid_spec=spec,
        out_shape=[jax.ShapeDtypeStruct((D, rows), f32), jax.ShapeDtypeStruct((16, rows), f32)],
        compiler_params=params(),
        name="attention",
    )(z, tok, k, vt, qt)


def gelu_parts(x):
    square = x * x
    t = jnp.tanh(x * (ROOT + (ROOT * 0.044715) * square))
    half = 0.5 * (1.0 + t)
    slope = half + (0.5 * x) * (1.0 - t * t) * (ROOT + (3.0 * ROOT * 0.044715) * square)
    return (x * half).astype(bf16), slope


def layer_kernel(
    per,
    tok_ref,
    mine_ref,
    k_ref,
    vt_ref,
    qt_ref,
    h0_ref,
    cot_ref,
    vec_ref,
    b1_ref,
    wo_ref,
    w1_ref,
    w2_ref,
    out_ref,
    h1g_ref,
    msg_ref,
    dwo_ref,
    dw1_ref,
    dw2_ref,
    small_ref,
    kext,
    qext,
    att,
    lse,
    wo,
    wo_slots,
    w1,
    w2,
    sems,
):
    p = pl.program_id(0)
    last = pl.num_programs(0) - 1
    blocks, _, rows = tok_ref.shape
    copies = [
        pltpu.make_async_copy(wo_ref, wo, sems.at[0]),
        pltpu.make_async_copy(w1_ref, w1, sems.at[1]),
        pltpu.make_async_copy(w2_ref, w2, sems.at[2]),
    ]

    @pl.when(p == 0)
    def _():
        for c in copies:
            c.start()

    attend(p, tok_ref, mine_ref, k_ref, vt_ref, qt_ref, att, lse, kext, qext)

    @pl.when(p == last)
    def _():
        for c in copies:
            c.wait()
        attended = att[...].astype(bf16)
        hidden1 = h0_ref[...] + dot(attended, wo[...], TN) + vec_ref[0:1, :]
        unit, inverse = norm_parts(hidden1)
        normed2 = (unit * vec_ref[1:2, :] + vec_ref[2:3, :]).astype(bf16)
        cot = cot_ref[...]
        out_grad = cot.astype(bf16)
        block_out = hidden1 + vec_ref[3:4, :]
        norm_grad = jnp.zeros_like(hidden1)
        inner_sums = []
        for c in range(FF // D):
            cols = slice(c * D, (c + 1) * D)
            x = dot(normed2, w1[:, cols]) + b1_ref[c : c + 1, :]
            active, slope = gelu_parts(x)
            block_out = block_out + dot(active, w2[cols, :])
            inner_grad = (dot(out_grad, w2[cols, :], NT) * slope).astype(bf16)
            dw2_ref[cols, :] = dot(active, out_grad, TN).astype(bf16)
            dw1_ref[:, cols] = dot(normed2, inner_grad, TN).astype(bf16)
            norm_grad = norm_grad + dot(inner_grad, w1[:, cols], NT)
            inner_sums.append(column_sum(inner_grad.astype(f32)))
        out_ref[...] = block_out
        hidden1_grad = cot + norm_pull(norm_grad, unit, inverse, vec_ref[1:2, :])
        h1g_ref[...] = hidden1_grad
        branch = hidden1_grad.astype(bf16)
        dwo_ref[...] = dot(attended, branch).astype(bf16)
        small_ref[...] = jnp.concatenate(
            [
                column_sum(branch.astype(f32)),
                column_sum(norm_grad * unit),
                column_sum(norm_grad),
                column_sum(out_grad.astype(f32)),
                *inner_sums,
            ],
            axis=0,
        )
        seg = onehot8(mine_ref[17:18, :])
        back = dot(wo[...], branch, NT).astype(bf16).astype(f32)
        product = back * att[...]
        for j in range(blocks):
            heads = [h for h in range(per * j, per * (j + 1)) if h < HEADS]
            wo_slots[...] = jnp.zeros_like(wo_slots)
            size = len(heads) * HEAD_DIM
            rows_ext = [jnp.zeros((HEAD_DIM, rows), f32), jnp.where(
                lax.broadcasted_iota(jnp.int32, (8, rows), 0) < DOCS, -BIG * (1.0 - seg), 0.0
            )[:DOCS]]
            lse_parts = []
            delta_parts = []
            for n in range(3):
                h = per * j + n
                if n < per and h < HEADS:
                    delta = column_sum(product[h * HEAD_DIM : (h + 1) * HEAD_DIM])
                    lse_parts += split3(-lse[h : h + 1, :])
                    delta_parts += split3(-delta)
                else:
                    lse_parts += [jnp.zeros((1, rows), f32)] * 3
                    delta_parts += [jnp.zeros((1, rows), f32)] * 3
            used = DOCS + 18
            rows_ext = rows_ext + lse_parts + delta_parts + [jnp.zeros((HEAD_DIM - used, rows), f32)]
            ext = jnp.transpose(jnp.concatenate(rows_ext, axis=0))
            if size:
                wo_slots[:size, :] = wo[heads[0] * HEAD_DIM : heads[0] * HEAD_DIM + size, :]
            grads = dot(branch, wo_slots[...], NT)
            msg_ref[j, :, :PAIR] = grads[:, :PAIR].astype(bf16)
            msg_ref[j, :, PAIR:] = (grads[:, PAIR:] + ext).astype(bf16)


def layer(tok, mine, k, vt, qt, h0, cot, vec, b1, wo, w1, w2, per):
    blocks, _, rows = tok.shape
    group = blocks * rows
    any_spec = pl.BlockSpec(memory_space=pl.ANY)
    return pl.pallas_call(
        functools.partial(layer_kernel, per),
        grid=(HEADS // 2,),
        in_specs=[
            whole(tok.shape),
            whole(mine.shape),
            pl.BlockSpec((group, PAIR), lambda p: (0, p)),
            pl.BlockSpec((PAIR, group), lambda p: (p, 0)),
            pl.BlockSpec((PAIR, rows), lambda p: (p, 0)),
            whole(h0.shape),
            whole(cot.shape),
            whole(vec.shape),
            whole(b1.shape),
            any_spec,
            any_spec,
            any_spec,
        ],
        out_specs=[
            whole((rows, D)),
            whole((rows, D)),
            whole((blocks, rows, SLOT)),
            whole((D, D)),
            whole((D, FF)),
            whole((FF, D)),
            whole((8, D)),
        ],
        out_shape=[
            jax.ShapeDtypeStruct((rows, D), f32),
            jax.ShapeDtypeStruct((rows, D), f32),
            jax.ShapeDtypeStruct((blocks, rows, SLOT), bf16),
            jax.ShapeDtypeStruct((D, D), bf16),
            jax.ShapeDtypeStruct((D, FF), bf16),
            jax.ShapeDtypeStruct((FF, D), bf16),
            jax.ShapeDtypeStruct((8, D), f32),
        ],
        scratch_shapes=[
            VMEM((group, PAIR), bf16),
            VMEM((PAIR, rows), bf16),
            VMEM((D, rows), f32),
            VMEM((16, rows), f32),
            VMEM((D, D), bf16),
            VMEM((SLOT, D), bf16),
            VMEM((D, FF), bf16),
            VMEM((FF, D), bf16),
            pltpu.SemaphoreType.DMA((3,)),
        ],
        compiler_params=params(),
        name="layer",
    )(tok, mine, k, vt, qt, h0, cot, vec, b1, wo, w1, w2)


def back_prepare(tok_ref, own_ref, kt, vt):
    blocks, _, rows = tok_ref.shape
    for b in range(blocks):
        place = slice(b * rows, (b + 1) * rows)
        seg = onehot8(tok_ref[b, 17:18, :])
        seg = jnp.concatenate([seg, jnp.zeros((HEAD_DIM - 8, rows), f32)], axis=0)
        sub = lax.broadcasted_iota(jnp.int32, seg.shape, 0)
        k_ext = jnp.where((sub >= DOCS) & (sub < DOCS + 9), 1.0, jnp.where(sub < DOCS, seg, 0.0))
        v_ext = jnp.where((sub >= DOCS + 9) & (sub < DOCS + 18), 1.0, 0.0)
        kt_b = jnp.transpose(own_ref[place, SLOT : 2 * SLOT].astype(f32))
        vt_b = jnp.transpose(own_ref[place, 2 * SLOT :].astype(f32))
        kt[:, place] = jnp.concatenate([kt_b[:EXT], k_ext], axis=0).astype(bf16)
        vt[:, place] = jnp.concatenate([vt_b[:EXT], v_ext], axis=0).astype(bf16)


def back_block(per, q, msg, keys, kt, vt, dkt, dvt):
    lane = lax.broadcasted_iota(jnp.int32, q.shape, 1)
    m = msg.astype(f32)
    queries = jnp.where(lane < EXT, q.astype(f32), m)
    q_t = jnp.transpose(q.astype(f32)).astype(bf16)
    m_t = jnp.transpose(m).astype(bf16)
    dq = jnp.zeros(q.shape, f32)
    for h in range(per):
        head = slice(h * HEAD_DIM, (h + 1) * HEAD_DIM)
        mine = (lane >= h * HEAD_DIM) & (lane < (h + 1) * HEAD_DIM)
        low = EXT + DOCS + 3 * h
        barred = (lane >= EXT) & (lane < EXT + DOCS)
        use_q = mine | barred | ((lane >= low) & (lane < low + 3))
        use_m = mine | ((lane >= low + 9) & (lane < low + 12))
        probs = jnp.exp(dot(jnp.where(use_q, queries, 0.0).astype(bf16), kt[...]))
        score_grad = (probs * dot(jnp.where(use_m, m, 0.0).astype(bf16), vt[...])).astype(bf16)
        dvt[head, :] += dot(m_t[head], probs.astype(bf16))
        dkt[head, :] += dot(q_t[head], score_grad)
        dq = dq + jnp.where(mine, dot(score_grad, keys), 0.0)
    return (dq * SCALE).astype(bf16)


def back_kernel(per, tok_ref, own_ref, msg_ref, grad_ref, kt, vt, dkt, dvt):
    blocks, _, rows = tok_ref.shape
    back_prepare(tok_ref, own_ref, kt, vt)
    dkt[...] = jnp.zeros_like(dkt)
    dvt[...] = jnp.zeros_like(dvt)

    def step(b, carry):
        place = pl.ds(pl.multiple_of(b * rows, rows), rows)
        keys = own_ref[:, SLOT : 2 * SLOT]
        grad_ref[place, :SLOT] = back_block(per, own_ref[place, :SLOT], msg_ref[b], keys, kt, vt, dkt, dvt)
        return carry

    lax.fori_loop(0, blocks, step, 0)
    for b in range(blocks):
        place = slice(b * rows, (b + 1) * rows)
        grad_ref[place, SLOT : 2 * SLOT] = jnp.transpose(dkt[:, place]).astype(bf16)
        grad_ref[place, 2 * SLOT :] = jnp.transpose(dvt[:, place]).astype(bf16)


def back(tok, own, msg, per):
    group = own.shape[0]
    return pl.pallas_call(
        functools.partial(back_kernel, per),
        in_specs=[pl.BlockSpec(memory_space=VMEM)] * 3,
        out_specs=pl.BlockSpec(memory_space=VMEM),
        out_shape=jax.ShapeDtypeStruct(own.shape, bf16),
        scratch_shapes=[
            VMEM((SLOT, group), bf16),
            VMEM((SLOT, group), bf16),
            VMEM((SLOT, group), f32),
            VMEM((SLOT, group), f32),
        ],
        compiler_params=params(),
        name="attention_back",
    )(tok, own, msg)

def final_kernel(
    z_ref, tok_ref, grad_ref, normed_ref, lhs_ref, sc_ref, rhs_ref, h1g_ref, up_w_ref, vec_ref, own_w_ref, mean_ref,
    dw_ref, noise_ref, table_ref, small_ref, acc,
):
    i = pl.program_id(0)
    last = pl.num_programs(0) - 1
    vocab = table_ref.shape[1]
    mean = mean_ref[0:1, 0:1]

    @pl.when(i == 0)
    def _():
        acc[...] = jnp.zeros_like(acc)
        small_ref[...] = jnp.zeros_like(small_ref)
        table_ref[...] = jnp.zeros_like(table_ref)

    grad = grad_ref[...]
    hidden0 = dot(lhs_ref[0], rhs_ref[...], TN)
    unit, inverse = norm_parts(hidden0)
    norm_grad = dot(grad, own_w_ref[...], NT)
    acc[...] += dot(normed_ref[...], grad, TN)
    own = (z_ref[0] == i).astype(f32)
    h0_grad = (norm_pull(norm_grad, unit, inverse, vec_ref[1:2, :]) + own * h1g_ref[...]).astype(bf16)
    mixed_grad = dot(up_w_ref[...], h0_grad, NT)
    sc = sc_ref[0]
    noise_ref[0] = sc[17:18] * mixed_grad
    embedded_grad = sc[16:17] * mixed_grad
    picked = sc[:16]
    norm_term = -jnp.sum(embedded_grad * picked, axis=(0, 1), keepdims=True) / (mean * mean)
    ids = tok_ref[i][16:17, :]
    table3 = dot(jnp.concatenate(split3(embedded_grad / mean), axis=0).astype(bf16), id_matrix(vocab, ids), NT)
    table_ref[...] += table3[:16] + table3[16:32] + table3[32:48]
    gradf = grad.astype(f32)
    small_ref[...] += jnp.concatenate(
        [
            dot(lhs_ref[0, :16, :], h0_grad),
            column_sum(h0_grad.astype(f32)),
            column_sum(norm_grad * unit),
            column_sum(norm_grad),
            column_sum(gradf),
            jnp.broadcast_to(norm_term, (1, D)),
            jnp.zeros((3, D), f32),
        ],
        axis=0,
    )

    @pl.when(i == last)
    def _():
        dw_ref[...] = acc[...].astype(bf16)


def final(z, tok, grad, normed, lhs, sc, rhs, h1g, up_w, vec, own_w, mean, vocab):
    blocks, _, rows = tok.shape
    spec = pltpu.PrefetchScalarGridSpec(
        num_scalar_prefetch=1,
        grid=(blocks,),
        in_specs=[
            whole(tok.shape),
            pl.BlockSpec((rows, 3 * SLOT), lambda i, z: (i, 0)),
            pl.BlockSpec((rows, D), lambda i, z: (i, 0)),
            pl.BlockSpec((1, 48, rows), lambda i, z: (i, 0, 0)),
            pl.BlockSpec((1, 24, rows), lambda i, z: (i, 0, 0)),
            whole(rhs.shape),
            whole(h1g.shape),
            whole(up_w.shape),
            whole(vec.shape),
            whole(own_w.shape),
            whole(mean.shape),
        ],
        out_specs=[
            whole((D, 3 * SLOT)),
            pl.BlockSpec((1, 16, rows), lambda i, z: (i, 0, 0)),
            whole((16, vocab)),
            whole((24, D)),
        ],
        scratch_shapes=[VMEM((D, 3 * SLOT), f32)],
    )
    return pl.pallas_call(
        final_kernel,
        grid_spec=spec,
        out_shape=[
            jax.ShapeDtypeStruct((D, 3 * SLOT), bf16),
            jax.ShapeDtypeStruct((blocks, 16, rows), f32),
            jax.ShapeDtypeStruct((16, vocab), f32),
            jax.ShapeDtypeStruct((24, D), f32),
        ],
        compiler_params=params(),
        name="embed_back",
    )(z, tok, grad, normed, lhs, sc, rhs, h1g, up_w, vec, own_w, mean)


UNITS = (
    (1, 0, 768, True),
    (1, 768, 768, False),
    (1, 1536, 768, True),
    (1, 2304, 768, False),
    (0, 0, 384, True),
    (0, 384, 384, False),
    (2, 0, 384, True),
    (2, 384, 384, False),
    (3, 0, 384, True),
    (3, 384, 384, False),
)
UNIT_ROWS = (384, 96, 96, 96)
CORE, WIDE, NARROW, NEAR, FAR, DONE = range(6)
PLAN = {
    "chunk0": [(CORE, 0)],
    "chunk1": [(CORE, 1), (WIDE, 0)],
    "chunk2": [(CORE, 2), (WIDE, 1)],
    "chunk3": [(CORE, 3), (WIDE, 2)],
    "sent": [(CORE, 6), (CORE, 7), (WIDE, 3), (NARROW, 0), (WIDE, 4), (WIDE, 5)],
    "prep": [(WIDE, 6), (WIDE, 7), (NARROW, 1)],
    "q0": [],
    "q1": [(NARROW, 2), (NARROW, 3)],
    "q2": [(NARROW, 4), (NARROW, 6), (NEAR, 0)],
    "q3": [(NARROW, 5), (NARROW, 7), (FAR, 0)],
    "kv": [(NEAR, 1), (DONE, 0), (NEAR, 2)],
    "dw": [(CORE, 8), (CORE, 9), (FAR, 1), (NEAR, 3)],
    "e0": [(WIDE, 8), (WIDE, 9), (FAR, 2), (DONE, 1)],
    "e1": [(FAR, 3)],
    "e2": [(NARROW, 8), (NARROW, 9), (DONE, 2)],
    "e3": [(DONE, 3)],
}


def mega_kernel(
    per,
    plan,
    tok_ref,
    lse_ref,
    gain1_ref,
    out_b_ref,
    gain2_ref,
    shift2_ref,
    outer_b_ref,
    b1_ref,
    lhs_ref,
    sc_ref,
    rhs_ref,
    mean_ref,
    up_w_ref,
    att_hbm,
    h0_hbm,
    cot_hbm,
    wo_hbm,
    w1_hbm,
    w2_hbm,
    own_hbm,
    normed_hbm,
    own_w_hbm,
    out_hbm,
    dwo_out,
    dw1_out,
    dw2_out,
    dw_out,
    small_out,
    table_out,
    noise_out,
    dw2,
    dw1,
    dwo,
    dwq,
    h1g,
    msg_out,
    msgs,
    small1,
    msg_send,
    msg_recv,
    first2,
    chunk_send,
    chunk_recv,
    send_parts,
    parts,
    mine,
    lines,
    sums,
    dw_parts,
    noise_mine,
    noise_parts,
    sends,
    recvs,
    *scratch,
):
    blocks, _, rows = tok_ref.shape
    dp = lax.axis_index("dp")
    z = lax.axis_index("blk")
    dp_n, blk_n = parts.shape[0], lines.shape[0]
    group = blocks * rows
    half = D // 2
    grads = (dw2, dw1, dwo, dwq)
    outs = (dw2_out, dw1_out, dwo_out)
    scratch = list(scratch)
    units = []
    lines_of = []
    core, x, y = lax.rem(dp, 2), lax.rem(lax.div(dp, 2), 2), lax.div(dp, 4)
    sibling = (dp + 1 - 2 * core, z)

    def chunk_copy(c):
        at = (c // 2, c % 2)
        return remote(dw2.at[at + (1 - core,)], first2.at[at], chunk_send.at[c], chunk_recv.at[c], sibling)

    for which, first, size, by_x in UNITS:
        buffer = first2 if which == 0 else scratch.pop(0)
        rest = [scratch.pop(0) for _ in range(4)]
        chunks = [functools.partial(chunk_copy, c) for c in range(4)] if which == 0 else None
        units.append(Scatter(grads[which], pl.ds(first, size), by_x, buffer, *rest, chunks=chunks))
        if which != 3 and not by_x:
            lines_of.append(LineScatter(units[-2:], outs[which], *[scratch.pop(0) for _ in range(7)]))

    def run(slot):
        for kind, n in plan[slot]:
            if kind == CORE:
                units[n].start()
            elif kind == WIDE:
                units[n].core_to_wide()
            elif kind == NARROW:
                units[n].wide_to_narrow()
            elif kind == NEAR:
                lines_of[n].start()
            elif kind == FAR:
                lines_of[n].near_to_far()
            else:
                lines_of[n].finish()

    def z_peer(k):
        low, high = lax.rem(z, 2), lax.div(z, 2)
        return (low + (k % 2) * (1 - 2 * low)) + 2 * (high + (k // 2) * (1 - 2 * high))

    def message(k):
        return remote(msg_out.at[z_peer(k)], msgs.at[k], msg_send.at[k], msg_recv.at[k], (dp, z_peer(k)))

    dp_to = [(lax.rem(dp + k, dp_n), z) for k in range(1, dp_n)]
    z_to = [(dp, lax.rem(z + k, blk_n)) for k in range(1, blk_n)]

    greet(dp_to + z_to)

    def dense(att_v, h0_v, cot_v, wo, w1, w2, wo_slots, sems):
        moves = [
            pltpu.make_async_copy(src, dst, sems.at[n])
            for n, (src, dst) in enumerate(
                ((wo_hbm, wo), (att_hbm, att_v), (h0_hbm, h0_v), (w1_hbm, w1), (cot_hbm, cot_v), (w2_hbm, w2))
            )
        ]
        for c in moves:
            c.start()
        for c in moves[:3]:
            c.wait()
        attended = att_v[...].astype(bf16)
        hidden1 = h0_v[...] + dot(attended, wo[...], TN) + row(out_b_ref)
        unit, inverse = norm_parts(hidden1)
        normed2 = (unit * row(gain2_ref) + row(shift2_ref)).astype(bf16)
        for c in moves[3:]:
            c.wait()
        cot = cot_v[...]
        out_grad = cot.astype(bf16)
        h0_v[...] = hidden1 + row(outer_b_ref)
        h1g[...] = jnp.zeros_like(h1g)
        inner_sums = []
        for c in range(FF // D):
            cols = slice(c * D, (c + 1) * D)
            active, slope = gelu_parts(dot(normed2, w1[:, cols]) + b1_ref[pl.ds(c * D, D)].reshape(1, D))
            h0_v[...] += dot(active, w2[cols, :])
            inner_grad = (dot(out_grad, w2[cols, :], NT) * slope).astype(bf16)
            if c == 0:
                met(dp_to + z_to)
            part = dot(active, out_grad, TN).astype(bf16)
            dw2[c // 2, c % 2, 0] = part[: D // 2]
            dw2[c // 2, c % 2, 1] = part[D // 2 :]
            chunk_copy(c).start()
            part = dot(normed2, inner_grad, TN).astype(bf16)
            for k in range(8):
                dw1[k // 4, k // 2 % 2, k % 2, :, cols] = part[k * 96 : (k + 1) * 96]
            h1g[...] += dot(inner_grad, w1[:, cols], NT)
            inner_sums.append(column_sum(inner_grad.astype(f32)))
            run(("chunk0", "chunk1", "chunk2", "chunk3")[c])
        norm_grad = h1g[...]
        write = pltpu.make_async_copy(h0_v, out_hbm, sems.at[0])
        write.start()
        hidden1_grad = cot + norm_pull(norm_grad, unit, inverse, row(gain2_ref))
        h1g[...] = hidden1_grad
        branch = hidden1_grad.astype(bf16)
        seg = onehot8(tok_ref[z, 17:18, :])
        sub = lax.broadcasted_iota(jnp.int32, (8, rows), 0)
        barred = jnp.where(sub < DOCS, -BIG * (1.0 - seg), 0.0)[:DOCS]
        product = dot(wo[...], branch, NT).astype(bf16).astype(f32) * att_v[...]
        wo_slots[...] = jnp.zeros_like(wo_slots)
        size = per * HEAD_DIM
        for j in range(blocks):
            lse_parts = []
            delta_parts = []
            for h in range(per * j, per * (j + 1)):
                delta = column_sum(product[h * HEAD_DIM : (h + 1) * HEAD_DIM])
                lse_parts += split3(-lse_ref[h : h + 1, :])
                delta_parts += split3(-delta)
            rest = jnp.zeros((HEAD_DIM - DOCS - 6 * per, rows), f32)
            ext = [jnp.zeros((HEAD_DIM, rows), f32), barred] + lse_parts + delta_parts + [rest]
            ext = jnp.transpose(jnp.concatenate(ext, axis=0))
            wo_slots[:size, :] = wo[j * size : (j + 1) * size, :]
            grads = dot(branch, wo_slots[...], NT)
            msg_out[j, :, :PAIR] = grads[:, :PAIR].astype(bf16)
            msg_out[j, :, PAIR:] = (grads[:, PAIR:] + ext).astype(bf16)
        for k in (1, 2, 3):
            message(k).start()
        part = dot(attended, branch).astype(bf16)
        for k in range(8):
            dwo[k // 4, k // 2 % 2, k % 2] = part[k * 96 : (k + 1) * 96]
        small1[...] = jnp.concatenate(
            [
                column_sum(branch.astype(f32)),
                column_sum(norm_grad * unit),
                column_sum(norm_grad),
                column_sum(out_grad.astype(f32)),
                *inner_sums,
            ],
            axis=0,
        )
        run("sent")
        write.wait()

    pl.run_scoped(
        dense,
        VMEM((D, rows), f32),
        VMEM((rows, D), f32),
        VMEM((rows, D), f32),
        VMEM((D, D), bf16),
        VMEM((D, FF), bf16),
        VMEM((FF, D), bf16),
        VMEM((SLOT, D), bf16),
        pltpu.SemaphoreType.DMA((6,)),
    )

    def backward(grad, own, kt, vt, dkt, dvt, sem):
        load = pltpu.make_async_copy(own_hbm, own, sem)
        load.start()
        dkt[...] = jnp.zeros_like(dkt)
        dvt[...] = jnp.zeros_like(dvt)
        msgs[0] = msg_out[z]
        load.wait()
        back_prepare(tok_ref, own, kt, vt)
        run("prep")

        def body(b, carry):
            low, high = lax.rem(z, 2), lax.div(z, 2)
            b_low, b_high = lax.rem(b, 2), lax.div(b, 2)
            other = (low + b_low * (1 - 2 * low)) + 2 * (high + b_high * (1 - 2 * high))
            for k in range(blocks):
                if k or plan["q0"]:

                    @pl.when(b == k)
                    def _():
                        if k:
                            message(k).wait()
                        run(("q0", "q1", "q2", "q3")[k])

            place = pl.ds(pl.multiple_of(other * rows, rows), rows)
            keys = own[:, SLOT : 2 * SLOT]
            grad[place, :SLOT] = back_block(per, own[place, :SLOT], msgs[b], keys, kt, vt, dkt, dvt)
            return carry

        lax.fori_loop(0, blocks, body, 0)
        for b in range(blocks):
            place = slice(b * rows, (b + 1) * rows)
            grad[place, SLOT : 2 * SLOT] = jnp.transpose(dkt[:, place]).astype(bf16)
            grad[place, 2 * SLOT :] = jnp.transpose(dvt[:, place]).astype(bf16)

    def embedding(grad, normed, own_w, sems):
        loads = [
            pltpu.make_async_copy(normed_hbm, normed, sems.at[0]),
            pltpu.make_async_copy(own_w_hbm, own_w, sems.at[1]),
        ]
        for c in loads:
            c.start()
        run("kv")
        for c in loads:
            c.wait()
        part = dot(normed[...], grad[...], TN).astype(bf16)
        for k in range(8):
            dwq[k // 4, k // 2 % 2, k % 2] = part[k * 96 : (k + 1) * 96]
        run("dw")
        mean = mean_ref[0:1, 0:1]
        small2 = jnp.zeros((24, D), f32)
        vocab = dp_n * 128
        table = jnp.zeros((16, vocab), f32)
        for i in range(blocks):
            place = slice(i * rows, (i + 1) * rows)
            g = grad[place, :]
            hidden0 = dot(lhs_ref[i], rhs_ref[...], TN)
            unit, inverse = norm_parts(hidden0)
            norm_grad = dot(g, own_w[...], NT)
            mine_too = (z == i).astype(f32)
            h0_grad = (norm_pull(norm_grad, unit, inverse, row(gain1_ref)) + mine_too * h1g[...]).astype(bf16)
            mixed_grad = dot(up_w_ref[...], h0_grad, NT)
            sc = sc_ref[i]
            noise_mine[i] = sc[17:18] * mixed_grad
            embedded_grad = sc[16:17] * mixed_grad
            norm_term = -jnp.sum(embedded_grad * sc[:16], axis=(0, 1), keepdims=True) / (mean * mean)
            table3 = dot(
                jnp.concatenate(split3(embedded_grad / mean), axis=0).astype(bf16),
                id_matrix(vocab, tok_ref[i][16:17, :]),
                NT,
            )
            table = table + (table3[:16] + table3[16:32] + table3[32:48])
            small2 = small2 + jnp.concatenate(
                [
                    dot(lhs_ref[i, :16, :], h0_grad),
                    column_sum(h0_grad.astype(f32)),
                    column_sum(norm_grad * unit),
                    column_sum(norm_grad),
                    jnp.broadcast_to(norm_term, (1, D)),
                    *[(z == j).astype(f32) * column_sum(g.astype(f32)) for j in range(blocks)],
                ],
                axis=0,
            )
            run(("e0", "e1", "e2", "e3")[i])
        flat = jnp.concatenate([small1[...], small2], axis=0)
        for k in range(dp_n):
            n = k % 4
            send_parts[k, :, :half] = flat[8 * n : 8 * n + 8, (k // 4) * half : (k // 4 + 1) * half]
            send_parts[k, :, half : half + 128] = table[:8, k * 128 : (k + 1) * 128]
            send_parts[k, :, half + 128 :] = table[8:, k * 128 : (k + 1) * 128]

    def rest(grad):
        pl.run_scoped(
            functools.partial(backward, grad),
            VMEM((group, 3 * SLOT), bf16),
            VMEM((SLOT, group), bf16),
            VMEM((SLOT, group), bf16),
            VMEM((SLOT, group), f32),
            VMEM((SLOT, group), f32),
            pltpu.SemaphoreType.DMA,
        )
        pl.run_scoped(
            functools.partial(embedding, grad),
            VMEM((group, D), bf16),
            VMEM((D, 3 * SLOT), bf16),
            pltpu.SemaphoreType.DMA((2,)),
        )

    pl.run_scoped(rest, VMEM((group, 3 * SLOT), bf16))

    nd, nz = dp_n - 1, blk_n - 1

    def spread(src, dst, peers, first):
        return [remote(src(p), dst, sends.at[first + k], recvs.at[first + k], p) for k, p in enumerate(peers)]

    one = spread(lambda p: send_parts.at[p[0]], parts.at[dp], dp_to, 0)
    four = spread(lambda p: noise_mine.at[p[1]], noise_parts.at[z], z_to, 2 * nd + nz)
    for c in one + four:
        c.start()
    parts[dp] = send_parts[dp]
    noise_parts[z] = noise_mine[z]
    for u in units[8:]:
        total = u.narrow_sum()
        q = total.shape[0] // blk_n
        for k in range(blk_n):
            dw_parts[k, :, u.columns] = total[k * q : (k + 1) * q]
    five = spread(lambda p: dw_parts.at[p[1]], dw_out.at[z], z_to, 2 * nd + 2 * nz)
    for c in five:
        c.start()
    dw_out[z] = dw_parts[z]
    for c in one:
        c.wait()
    total = parts[0]
    for k in range(1, dp_n):
        total = total + parts[k]
    mine[...] = total
    lines[z] = total
    two = spread(lambda p: mine, lines.at[z], z_to, nd)
    for c in two:
        c.start()
    for c in four:
        c.wait()
    total = noise_parts[0]
    for k in range(1, blk_n):
        total = total + noise_parts[k]
    noise_out[...] = total
    for c in two:
        c.wait()
    total = lines[0]
    for k in range(1, blk_n):
        total = total + lines[k]
    table_out[...] = total[:, half:]
    sums[...] = total[:, :half]
    small_out[dp] = total[:, :half]
    three = spread(lambda p: sums, small_out.at[dp], dp_to, nd + nz)
    for c in three:
        c.start()
    for c in three + five:
        c.wait()


def mega(small, big, dp_n, per):
    tok, att, lse, h0, cot, vectors, lhs, sc, rhs, mean, up_w = small
    blk_n, _, rows = tok.shape
    group = blk_n * rows
    share = D // (dp_n * blk_n)
    vmem = pl.BlockSpec(memory_space=VMEM)
    hbm = pl.BlockSpec(memory_space=pl.ANY)
    count = 2 * (dp_n - 1) + 3 * (blk_n - 1)
    half = D // 2
    scratch = []
    for which, _, size, by_x in UNITS:
        scratch += scatter_scratch(UNIT_ROWS[which], size, which != 0)
        if which != 3 and not by_x:
            scratch += line_scratch(UNIT_ROWS[which], size)
    in_vmem = (tok, lse, *vectors, lhs, sc, rhs, mean, up_w)
    in_hbm = (att, h0, cot) + tuple(big)
    return pl.pallas_call(
        functools.partial(mega_kernel, per, PLAN),
        in_specs=[vmem] * len(in_vmem) + [hbm] * len(in_hbm),
        out_specs=[hbm] + [vmem] * 7,
        out_shape=[
            jax.ShapeDtypeStruct((rows, D), f32),
            jax.ShapeDtypeStruct((share, D), f32),
            jax.ShapeDtypeStruct((share, FF), f32),
            jax.ShapeDtypeStruct((4 * share, D), f32),
            jax.ShapeDtypeStruct((blk_n, share, 3 * SLOT), f32),
            jax.ShapeDtypeStruct((dp_n, 8, half), f32),
            jax.ShapeDtypeStruct((8, 256), f32),
            jax.ShapeDtypeStruct((16, rows), f32),
        ],
        scratch_shapes=[
            VMEM((2, 2, 2, 384, D), bf16),
            VMEM((2, 2, 2, 96, FF), bf16),
            VMEM((2, 2, 2, 96, D), bf16),
            VMEM((2, 2, 2, 96, 3 * SLOT), bf16),
            VMEM((rows, D), f32),
            VMEM((blk_n, rows, SLOT), bf16),
            VMEM((blk_n, rows, SLOT), bf16),
            VMEM((8, D), f32),
            pltpu.SemaphoreType.DMA((blk_n,)),
            pltpu.SemaphoreType.DMA((blk_n,)),
            VMEM((2, 2, 384, D), bf16),
            pltpu.SemaphoreType.DMA((4,)),
            pltpu.SemaphoreType.DMA((4,)),
            VMEM((dp_n, 8, half + 256), f32),
            VMEM((dp_n, 8, half + 256), f32),
            VMEM((8, half + 256), f32),
            VMEM((blk_n, 8, half + 256), f32),
            VMEM((8, half), f32),
            VMEM((blk_n, share, 3 * SLOT), f32),
            VMEM((blk_n, 16, rows), f32),
            VMEM((blk_n, 16, rows), f32),
            pltpu.SemaphoreType.DMA((count,)),
            pltpu.SemaphoreType.DMA((count,)),
            *scratch,
        ],
        compiler_params=pltpu.CompilerParams(
            vmem_limit_bytes=63 * MIB, collective_id=1, has_side_effects=True
        ),
        name="layer_and_sums",
    )(*in_vmem, *in_hbm)


def finish_kernel(
    per, dwo_ref, dw1_ref, dw2_ref, dw_ref, flat_ref, table_sum_ref, noise_ref, mean_ref, table_ref, block_hbm,
    block_out, noise_out, table_out, up_w_out, up_b_out, gain1_out, shift1_out, qkv_out, qb_out, vb_out, dwo_out,
    out_b_out, gain2_out, shift2_out, dw1_out, b1_out, dw2_out, b2_out, mean_out, buffer, sems,
):
    load = pltpu.make_async_copy(block_hbm, buffer, sems.at[0])
    store = pltpu.make_async_copy(buffer, block_out, sems.at[1])
    load.start()
    blk_n = dw_ref.shape[0]
    vocab = table_ref.shape[1] * flat_ref.shape[0]
    load.wait()
    store.start()
    width = per * HEAD_DIM
    flat = [jnp.concatenate([flat_ref[n], flat_ref[4 + n]], axis=1) for n in range(4)]
    noise_out[...] = noise_ref[...]
    dwo_out[...] = dwo_ref[...]
    dw1_out[...] = dw1_ref[...]
    dw2_out[...] = dw2_ref[...]
    out_b_out[...] = flat[0][0]
    gain2_out[...] = flat[0][1]
    shift2_out[...] = flat[0][2]
    b2_out[...] = flat[0][3]
    for n in range(4):
        b1_out[pl.ds(n * D, D)] = flat[0][4 + n]
    up_w_out[:8, :] = flat[1]
    up_w_out[8:, :] = flat[2]
    up_b_out[...] = flat[3][0]
    gain1_out[...] = flat[3][1]
    shift1_out[...] = flat[3][2]
    for n in range(3):
        parts = [dw_ref[k, :, n * SLOT : n * SLOT + width] for k in range(blk_n)]
        qkv_out[:, n * D : (n + 1) * D] = jnp.concatenate(parts, axis=1)
    for n, out in ((0, qb_out), (2, vb_out)):
        parts = [flat[3][4 + k : 5 + k, n * SLOT : n * SLOT + width] for k in range(blk_n)]
        out[...] = jnp.concatenate(parts, axis=1)[0]
    table = table_ref[...]
    norms = jnp.sqrt(jnp.sum(table * table, axis=0, keepdims=True) + 1.0)
    total = jnp.concatenate([table_sum_ref[:, :128], table_sum_ref[:, 128:]], axis=0)
    table_out[...] = total[:, : table.shape[1]] + flat[3][3:4, :1] * table / (vocab * norms)
    mean_out[...] = mean_ref[0:1, 0:1]
    store.wait()


def finish(per, dwo, dw1, dw2, dw, flat, table_sum, noise, mean, table, block):
    vmem = pl.BlockSpec(memory_space=VMEM)
    hbm = pl.BlockSpec(memory_space=pl.ANY)
    vector = jax.ShapeDtypeStruct((D,), f32)
    share = dwo.shape[0]
    like = lambda x: jax.ShapeDtypeStruct(x.shape, x.dtype)
    shapes = [
        like(block), like(noise), like(table), jax.ShapeDtypeStruct((16, D), f32), vector, vector, vector,
        jax.ShapeDtypeStruct((share, 3 * D), f32), vector, vector, like(dwo), vector, vector, vector, like(dw1),
        jax.ShapeDtypeStruct((FF,), f32), like(dw2), vector, jax.ShapeDtypeStruct((1, 1), f32),
    ]
    return pl.pallas_call(
        functools.partial(finish_kernel, per),
        in_specs=[vmem] * 9 + [hbm],
        out_specs=[hbm] + [vmem] * 18,
        out_shape=shapes,
        scratch_shapes=[VMEM(block.shape, f32), pltpu.SemaphoreType.DMA((2,))],
        compiler_params=params(),
        name="finish",
    )(dwo, dw1, dw2, dw, flat, table_sum, noise, mean, table, block)


def shards(
    dp_n,
    blk_n,
    token_ids,
    segment_ids,
    timesteps,
    noise,
    table,
    up_weight,
    up_bias,
    norm1_gain,
    norm1_shift,
    qkv_weight,
    query_bias,
    value_bias,
    out_weight,
    out_bias,
    norm2_gain,
    norm2_shift,
    ffn_in_weight,
    ffn_in_bias,
    ffn_out_weight,
    ffn_out_bias,
    cotangent,
):
    rows = token_ids.shape[0]
    local_rows = table.shape[0]
    vp = -(-local_rows // 128) * 128
    per = -(-HEADS // blk_n)
    width = per * HEAD_DIM
    z = lax.axis_index("blk")
    z1 = z.reshape(1).astype(jnp.int32)
    vectors = (up_bias, norm1_gain, norm1_shift, query_bias, value_bias)

    if dp_n == 8 and blk_n == 4:
        tok, tab = gather(token_ids, segment_ids, timesteps, noise.T, table.T, dp_n, blk_n)
        k, vt, own, normed, lhs, sc, qt, h0, rhs, mean, own_w = embed(
            z1, tok, tab, up_weight, vectors, qkv_weight, local_rows, per
        )
        att, lse = attention(z1, tok, k, vt, qt)
        vectors = (norm1_gain, out_bias, norm2_gain, norm2_shift, ffn_out_bias, ffn_in_bias)
        block_out, dwo, dw1, dw2, dw, flat, table_sum, noise_sum = mega(
            (tok, att, lse, h0, cotangent, vectors, lhs, sc, rhs, mean, up_weight),
            (out_weight, ffn_in_weight, ffn_out_weight, own, normed, own_w),
            dp_n,
            per,
        )
        outs = list(finish(per, dwo, dw1, dw2, dw, flat, table_sum, noise_sum, mean, table.T, block_out))
        outs[1] = outs[1].T
        outs[2] = outs[2].T
        outs[-1] = outs[-1].reshape(())
        return tuple(outs)

    slots = (token_ids // local_rows) * vp + token_ids % local_rows
    scalars = jnp.stack([slots, segment_ids, timesteps]).astype(f32)
    mine = jnp.concatenate([noise.T, scalars, jnp.zeros((5, rows), f32)], axis=0)
    tok = lax.all_gather(mine, "blk")
    tab = lax.all_gather(jnp.pad(table.T, ((0, 0), (0, vp - local_rows))), "dp")
    padded = blk_n * width
    split = jnp.pad(qkv_weight.reshape(D, 3, D), ((0, 0), (0, 0), (0, padded - D)))
    own_w = lax.dynamic_slice(split, (0, 0, z * width), (D, 3, width))
    own_w = jnp.pad(own_w, ((0, 0), (0, 0), (0, SLOT - width))).reshape(D, 3 * SLOT)
    bias = jnp.pad(jnp.stack([query_bias, jnp.zeros((D,), f32), value_bias]), ((0, 0), (0, padded - D)))
    own_b = lax.dynamic_slice(bias, (0, z * width), (3, width))
    own_b = jnp.pad(own_b, ((0, 0), (0, SLOT - width))).reshape(1, 3 * SLOT)
    k, vt, own, normed, lhs, sc, qt, h0, rhs, mean = embed(
        z1, tok, tab, up_weight, vectors, qkv_weight, local_rows, 0, own_w, own_b
    )
    vec1 = jnp.stack([up_bias, norm1_gain, norm1_shift])
    vec2 = jnp.stack([out_bias, norm2_gain, norm2_shift, ffn_out_bias])
    b1 = ffn_in_bias.reshape(FF // D, D)
    share = D // (dp_n * blk_n)
    block_out, h1g, msg, dwo, dw1, dw2, small1 = layer(
        tok, mine, k, vt, qt, h0, cotangent, vec2, b1, out_weight, ffn_in_weight, ffn_out_weight, per
    )
    msg = lax.all_to_all(msg, "blk", 0, 0)
    grad = back(tok, own, msg, per)
    dw, noise_part, table_part, small2 = final(
        z1, tok, grad, normed, lhs, sc, rhs, h1g, up_weight, vec1, own_w, mean, dp_n * vp
    )
    noise_grad = lax.psum_scatter(noise_part, "blk", scatter_dimension=0, tiled=False).T
    own_sums = small2[19].reshape(3, SLOT)[:, :width]
    own_sums = lax.dynamic_update_slice(jnp.zeros((3, padded), f32), own_sums, (0, z * width))[:, :D]
    small2, table_total, small1, own_sums = lax.psum((small2, table_part, small1, own_sums), ("dp", "blk"))
    scatter = functools.partial(lax.psum_scatter, axis_name=("dp", "blk"), scatter_dimension=0, tiled=True)
    dwo, dw1, dw2 = scatter(dwo), scatter(dw1), scatter(dw2)
    dw = lax.psum_scatter(dw, "dp", scatter_dimension=0, tiled=True)
    dw = lax.all_to_all(dw.reshape(blk_n, share, 3 * SLOT), "blk", 0, 0)
    dw = dw.reshape(blk_n, share, 3, SLOT)[..., :width].transpose(1, 2, 0, 3).reshape(share, 3, padded)[..., :D]
    table_grad = lax.dynamic_slice(table_total, (0, lax.axis_index("dp") * vp), (16, local_rows)).T
    norms = jnp.sqrt(jnp.sum(table * table, axis=-1, keepdims=True) + 1.0)
    table_grad = table_grad + small2[20, 0] * table / (dp_n * local_rows * norms)
    return (
        block_out,
        noise_grad,
        table_grad,
        small2[:16],
        small2[16],
        small2[17],
        small2[18],
        dw.reshape(share, 3 * D).astype(f32),
        own_sums[0],
        own_sums[2],
        dwo.astype(f32),
        small1[0],
        small1[1],
        small1[2],
        dw1.astype(f32),
        small1[4:8].reshape(FF),
        dw2.astype(f32),
        small1[3],
        mean[0, 0],
    )


def solution(mesh):
    rows = P(("dp", "blk"))
    wide = P(("dp", "blk"), None)
    in_specs = (rows, rows, rows, wide, P("dp", None)) + (P(),) * 15 + (wide,)
    out_specs = (
        (wide, wide, P("dp", None))
        + (P(),) * 4
        + (wide, P(), P(), wide, P(), P(), P(), wide, P(), wide, P(), P())
    )
    body = functools.partial(shards, mesh.shape["dp"], mesh.shape["blk"])
    return jax.shard_map(body, mesh=mesh, in_specs=in_specs, out_specs=out_specs, check_vma=False)
```

```python
import functools
import math

import jax
import jax.numpy as jnp
from jax import lax
from jax.experimental import pallas as pl
from jax.experimental.pallas import tpu as pltpu
from jax.sharding import PartitionSpec as P

D = 768
HEADS = 12
HEAD_DIM = 64
FF = 3072
EMB = 16
TSTEPS = 2000
DOCS = 4
PAIR = 2 * HEAD_DIM
SLOT = 256
EXT = 192
BIG = 1e30
SAFE = 64.0
SCALE = HEAD_DIM**-0.5
MIB = 2**20
MESH = pl.DeviceIdType.MESH
VMEM = pltpu.VMEM
f32 = jnp.float32
bf16 = jnp.bfloat16

NN = (((1,), (0,)), ((), ()))
NT = (((1,), (1,)), ((), ()))
TN = (((0,), (0,)), ((), ()))
TT = (((0,), (1,)), ((), ()))


def dot(left, right, dims=NN):
    return lax.dot_general(left, right, dims, preferred_element_type=f32)


def split3(x):
    high = x.astype(bf16)
    rest = x - high.astype(f32)
    middle = rest.astype(bf16)
    low = (rest - middle.astype(f32)).astype(bf16)
    return high.astype(f32), middle.astype(f32), low.astype(f32)


def column_sum(x):
    return jnp.sum(x, axis=0, keepdims=True)


def row_mean(x):
    return jnp.mean(x, axis=-1, keepdims=True)


def norm_parts(x):
    centered = x - row_mean(x)
    inverse = lax.rsqrt(row_mean(centered * centered) + 1e-05)
    return centered * inverse, inverse


def norm_pull(grad, unit, inverse, gain):
    scaled = grad * gain
    return inverse * (scaled - row_mean(scaled) - unit * row_mean(scaled * unit))


def onehot8(row):
    return (lax.broadcasted_iota(jnp.int32, (8, row.shape[1]), 0) == row.astype(jnp.int32)).astype(f32)


def id_matrix(rows, row):
    return (lax.broadcasted_iota(jnp.int32, (rows, row.shape[1]), 0) == row.astype(jnp.int32)).astype(f32).astype(bf16)


def params(**kw):
    return pltpu.CompilerParams(vmem_limit_bytes=60 * MIB, **kw)


def whole(shape):
    return pl.BlockSpec(shape, lambda *_: (0,) * len(shape))


def remote(src, dst, send, recv, peer):
    return pltpu.make_async_remote_copy(
        src_ref=src, dst_ref=dst, send_sem=send, recv_sem=recv, device_id=peer, device_id_type=MESH
    )


def greet(peers):
    barrier = pltpu.get_barrier_semaphore()
    for peer in peers:
        pl.semaphore_signal(barrier, inc=1, device_id=peer, device_id_type=MESH)


def met(peers):
    pl.semaphore_wait(pltpu.get_barrier_semaphore(), len(peers))


def gather_kernel(
    dp_n, blk_n, local_rows, ids_ref, seg_ref, steps_ref, noise_ref, table_ref, tok_ref, tab_ref, mine, own, send, recv
):
    dp = lax.axis_index("dp")
    z = lax.axis_index("blk")
    dp_peers = [(lax.rem(dp + k, dp_n), z) for k in range(1, dp_n)]
    z_peers = [(dp, lax.rem(z + k, blk_n)) for k in range(1, blk_n)]
    greet(z_peers + dp_peers)
    rows = ids_ref.shape[0]
    vp = own.shape[1]
    ids = ids_ref[...].reshape(1, rows).astype(f32)
    mine[...] = jnp.zeros_like(mine)
    mine[:16, :] = noise_ref[...]
    mine[16:17, :] = ids + (vp - local_rows) * jnp.floor((ids + 0.5) / local_rows)
    mine[17:18, :] = seg_ref[...].reshape(1, rows).astype(f32)
    mine[18:19, :] = steps_ref[...].reshape(1, rows).astype(f32)
    own[...] = jnp.zeros_like(own)
    own[:, :local_rows] = table_ref[...]
    met(z_peers + dp_peers)
    copies = []
    for k, peer in enumerate(z_peers):
        copies.append(remote(mine, tok_ref.at[z], send.at[k], recv.at[k], peer))
    for k, peer in enumerate(dp_peers):
        n = len(z_peers) + k
        copies.append(remote(own, tab_ref.at[dp], send.at[n], recv.at[n], peer))
    for c in copies:
        c.start()
    tok_ref[z] = mine[...]
    tab_ref[dp] = own[...]
    for c in copies:
        c.wait()


def gather(ids, segments, steps, noise, table, dp_n, blk_n):
    count = dp_n + blk_n - 2
    rows = ids.shape[0]
    local_rows = table.shape[1]
    vp = -(-local_rows // 128) * 128
    vmem = pl.BlockSpec(memory_space=VMEM)
    return pl.pallas_call(
        functools.partial(gather_kernel, dp_n, blk_n, local_rows),
        in_specs=[vmem] * 5,
        out_specs=[vmem, vmem],
        out_shape=[
            jax.ShapeDtypeStruct((blk_n, 24, rows), f32),
            jax.ShapeDtypeStruct((dp_n, 16, vp), f32),
        ],
        scratch_shapes=[
            VMEM((24, rows), f32),
            VMEM((16, vp), f32),
            pltpu.SemaphoreType.DMA((count,)),
            pltpu.SemaphoreType.DMA((count,)),
        ],
        compiler_params=params(collective_id=0, has_side_effects=True),
        name="gather",
    )(ids, segments, steps, noise, table)


class Scatter:
    def __init__(self, grad, columns, by_x, first, second, third, send, recv, chunks=None):
        self.grad, self.columns, self.by_x = grad, columns, by_x
        self.first, self.second, self.third = first, second, third
        self.send, self.recv, self.chunks = send, recv, chunks
        self.dp = lax.axis_index("dp")
        self.z = lax.axis_index("blk")
        self.core = lax.rem(self.dp, 2)
        self.x = lax.rem(lax.div(self.dp, 2), 2)
        self.y = lax.div(self.dp, 4)

    def flip(self, bit, step):
        return (self.dp + step * (1 - 2 * bit), self.z)

    def own(self, y, x):
        return self.grad[y, x, self.core, :, self.columns].astype(f32)

    def core_copy(self):
        src = self.grad.at[:, :, 1 - self.core, :, self.columns]
        return remote(src, self.first, self.send.at[0], self.recv.at[0], self.flip(self.core, 1))

    def wide(self):
        if self.by_x:
            src, peer = self.grad.at[:, 1 - self.x, self.core, :, self.columns], self.flip(self.x, 2)
        else:
            src, peer = self.grad.at[1 - self.y, :, self.core, :, self.columns], self.flip(self.y, 4)
        return remote(src, self.second, self.send.at[1], self.recv.at[1], peer)

    def narrow(self):
        if self.by_x:
            src, peer = self.grad.at[1 - self.y, self.x, self.core, :, self.columns], self.flip(self.y, 4)
        else:
            src, peer = self.grad.at[self.y, 1 - self.x, self.core, :, self.columns], self.flip(self.x, 2)
        return remote(src, self.third, self.send.at[2], self.recv.at[2], peer)

    def start(self):
        self.core_copy().start()

    def core_to_wide(self):
        if self.chunks is None:
            self.core_copy().wait()
        elif self.by_x:
            for c in self.chunks:
                c().wait()
        def add(k, carry):
            y, x = lax.div(k, 2), lax.rem(k, 2)
            if self.chunks is None:
                other = self.first[y, x]
            else:
                other = self.first[y, x, :, self.columns]
            self.grad[y, x, self.core, :, self.columns] = (self.own(y, x) + other.astype(f32)).astype(bf16)
            return carry

        lax.fori_loop(0, 4, add, 0)
        self.wide().start()

    def wide_to_narrow(self):
        self.wide().wait()
        def add(n, carry):
            y, x = (n, self.x) if self.by_x else (self.y, n)
            total = self.own(y, x) + self.second[n].astype(f32)
            self.grad[y, x, self.core, :, self.columns] = total.astype(bf16)
            return carry

        lax.fori_loop(0, 2, add, 0)
        self.narrow().start()

    def narrow_sum(self):
        self.narrow().wait()
        return (self.own(self.y, self.x) + self.third[...].astype(f32)).astype(bf16)


def scatter_scratch(rows, columns, first=True):
    return ([VMEM((2, 2, rows, columns), bf16)] if first else []) + [
        VMEM((2, rows, columns), bf16),
        VMEM((rows, columns), bf16),
        pltpu.SemaphoreType.DMA((3,)),
        pltpu.SemaphoreType.DMA((3,)),
    ]


class LineScatter:
    def __init__(self, bases, out, half, first, rest, kept, second, send, recv):
        self.bases, self.out = bases, out
        self.half, self.first, self.rest, self.kept, self.second = half, first, rest, kept, second
        self.send, self.recv = send, recv
        self.dp, self.z = bases[0].dp, bases[0].z
        self.low = lax.rem(self.z, 2)
        self.high = lax.div(self.z, 2)

    def near(self):
        peer = (self.dp, self.z + 1 - 2 * self.low)
        return remote(self.half.at[1 - self.low], self.first, self.send.at[0], self.recv.at[0], peer)

    def far(self):
        peer = (self.dp, self.z + 2 - 4 * self.high)
        return remote(self.rest, self.second, self.send.at[1], self.recv.at[1], peer)

    def start(self):
        q = self.kept.shape[0] // 2
        totals = [base.narrow_sum() for base in self.bases]
        for low in range(2):
            for high in range(2):
                for n in range(2):
                    block = 2 * high + low
                    self.half[low, pl.ds((2 * high + n) * q, q), :] = totals[n][block * q : (block + 1) * q]
        self.near().start()

    def near_to_far(self):
        self.near().wait()
        size = self.kept.shape[0]
        mine = pl.ds(pl.multiple_of(self.high * size, size), size)
        other = pl.ds(pl.multiple_of((1 - self.high) * size, size), size)
        self.rest[...] = (self.half[self.low, other, :].astype(f32) + self.first[other, :].astype(f32)).astype(bf16)
        self.far().start()
        self.kept[...] = self.half[self.low, mine, :].astype(f32) + self.first[mine, :].astype(f32)

    def finish(self):
        self.far().wait()
        total = self.kept[...] + self.second[...].astype(f32)
        q = total.shape[0] // 2
        for n in range(2):
            self.out[:, self.bases[n].columns] = total[n * q : (n + 1) * q]


def line_scratch(rows, columns):
    return [
        VMEM((2, rows, columns), bf16),
        VMEM((rows, columns), bf16),
        VMEM((rows // 2, columns), bf16),
        VMEM((rows // 2, columns), f32),
        VMEM((rows // 2, columns), bf16),
        pltpu.SemaphoreType.DMA((2,)),
        pltpu.SemaphoreType.DMA((2,)),
    ]


def row(ref):
    return ref[...].reshape(1, ref.shape[0])


def own_columns(per, z, w_ref, qb_ref, vb_ref, own_w, own_b):
    start = z * (per * HEAD_DIM)
    base = pl.multiple_of(start // 128 * 128, 128)
    line = lax.broadcasted_iota(jnp.int32, (SLOT, SLOT), 0)
    lane = lax.broadcasted_iota(jnp.int32, (SLOT, SLOT), 1)
    move = ((line == lane + (start - base)) & (lane < per * HEAD_DIM)).astype(f32).astype(bf16)
    for n in range(3):
        part = w_ref[:, pl.ds(pl.multiple_of(n * D + base, 128), SLOT)]
        own_w[:, n * SLOT : (n + 1) * SLOT] = dot(part, move).astype(bf16)
    own_b[...] = jnp.zeros_like(own_b)
    for n, ref in ((0, qb_ref), (2, vb_ref)):
        part = jnp.concatenate(split3(jnp.broadcast_to(ref[pl.ds(base, SLOT)].reshape(1, SLOT), (8, SLOT))), axis=0)
        part = dot(part.astype(bf16), move)
        own_b[:, n * SLOT : (n + 1) * SLOT] = part[:8] + part[8:16] + part[16:]


def embed_kernel(local_rows, z_ref, tok_ref, tab_ref, up_w_ref, up_b_ref, gain_ref, shift_ref, qb_ref, vb_ref, w_ref,
                 own_w_ref, own_b_ref, *refs):
    embed_body(local_rows, z_ref, tok_ref, tab_ref, up_w_ref, up_b_ref, gain_ref, shift_ref, qb_ref, vb_ref, w_ref,
               own_b_ref, own_w_ref, 0, *refs)


def embed_body(
    local_rows,
    z_ref,
    tok_ref,
    tab_ref,
    up_w_ref,
    up_b_ref,
    gain_ref,
    shift_ref,
    qb_ref,
    vb_ref,
    w_ref,
    own_b_ref,
    own_w_ref,
    per,
    k_ref,
    vt_ref,
    own_ref,
    normed_ref,
    lhs_ref,
    sc_ref,
    qt_ref,
    h0_ref,
    rhs_ref,
    mean_ref,
    tab3,
    vcol,
):
    i = pl.program_id(0)
    dp_n, _, vp = tab_ref.shape
    blocks, _, rows = tok_ref.shape

    @pl.when(i == 0)
    def _():
        if per:
            own_columns(per, z_ref[0], w_ref, qb_ref, vb_ref, own_w_ref, own_b_ref)
        table = jnp.concatenate([tab_ref[j] for j in range(dp_n)], axis=1)
        squares = jnp.sum(table * table, axis=0, keepdims=True)
        lane = lax.broadcasted_iota(jnp.int32, squares.shape, 1)
        norms = jnp.where(lane % vp < local_rows, jnp.sqrt(squares + 1.0), 0.0)
        mean_ref[...] = jnp.broadcast_to(jnp.sum(norms, axis=1, keepdims=True) / (local_rows * dp_n), (8, 128))
        tab3[...] = jnp.concatenate(split3(table), axis=0).astype(bf16)
        segments = tok_ref[:, 17, :]
        steps = tok_ref[:, 18, :]
        sub = lax.broadcasted_iota(jnp.int32, (8, 1), 0)
        time = jnp.zeros((8, 1), f32)
        for s in range(DOCS):
            own = jnp.max(jnp.where(segments == float(s), steps, 0.0), axis=(0, 1), keepdims=True)
            time = jnp.where(sub == s, own, time)
        lane = lax.broadcasted_iota(jnp.int32, (8, D), 1)
        half = D // 2
        index = jnp.where(lane < half, lane, lane - half).astype(f32)
        angle = time * jnp.exp(index * (-math.log(10000.0) / half))
        wave = jnp.where(lane < half, jnp.sin(angle), jnp.cos(angle)) + row(up_b_ref)
        parts = split3(wave)
        rhs_ref[...] = jnp.concatenate([up_w_ref[...].astype(f32), *parts, jnp.zeros((8, D), f32)], axis=0).astype(bf16)
        bias = jnp.concatenate([row(qb_ref), row(vb_ref), jnp.zeros((6, D), f32)], axis=0)
        vcol[...] = jnp.transpose(bias)

    tok = tok_ref[i]
    ids = tok[16:17, :]
    picked3 = dot(tab3[...], id_matrix(dp_n * vp, ids))
    picked = picked3[:16] + picked3[16:32] + picked3[32:48]
    mean = mean_ref[0:1, 0:1]
    alpha_bar = 1.0 - jnp.sqrt(tok[18:19, :] / TSTEPS + 0.0001)
    signal = jnp.sqrt(alpha_bar)
    noise_scale = jnp.sqrt(1.0 - alpha_bar)
    mixed = signal * (picked / mean) + noise_scale * tok[:16]
    seg = onehot8(tok[17:18, :])
    lhs = jnp.concatenate([mixed, seg, seg, seg, jnp.zeros((8, rows), f32)], axis=0).astype(bf16)
    lhs_ref[0] = lhs
    sc_ref[0] = jnp.concatenate([picked, signal, noise_scale, jnp.zeros((6, rows), f32)], axis=0)
    hidden0 = dot(lhs, rhs_ref[...], TN)
    unit, _ = norm_parts(hidden0)
    normed = (unit * row(gain_ref) + row(shift_ref)).astype(bf16)
    normed_ref[...] = normed
    k_ref[...] = dot(normed, w_ref[:, D : 2 * D]).astype(bf16)
    vt_ref[...] = (dot(w_ref[:, 2 * D :], normed, TT) + vcol[:, 1:2]).astype(bf16)
    own = dot(normed, own_w_ref[...]) + own_b_ref[0:1, :]
    own_ref[:, :SLOT] = (own[:, :SLOT] * SCALE).astype(bf16)
    own_ref[:, SLOT:] = own[:, SLOT:].astype(bf16)

    @pl.when(i == z_ref[0])
    def _():
        h0_ref[...] = hidden0
        q = (dot(w_ref[:, :D], normed, TT) + vcol[:, 0:1]).astype(bf16)
        qt_ref[...] = (q.astype(f32) * SCALE).astype(bf16)


def embed(z, tok, tab, up_w, vectors, w, local_rows, own_w, own_b):
    blocks, _, rows = tok.shape
    group = blocks * rows
    vocab = tab.shape[0] * tab.shape[2]
    operands = (tok, tab, up_w, *vectors, w, own_w, own_b)
    spec = pltpu.PrefetchScalarGridSpec(
        num_scalar_prefetch=1,
        grid=(blocks,),
        in_specs=[whole(x.shape) for x in operands],
        out_specs=[
            pl.BlockSpec((rows, D), lambda i, z: (i, 0)),
            pl.BlockSpec((D, rows), lambda i, z: (0, i)),
            pl.BlockSpec((rows, 3 * SLOT), lambda i, z: (i, 0)),
            pl.BlockSpec((rows, D), lambda i, z: (i, 0)),
            pl.BlockSpec((1, 48, rows), lambda i, z: (i, 0, 0)),
            pl.BlockSpec((1, 24, rows), lambda i, z: (i, 0, 0)),
            whole((D, rows)),
            whole((rows, D)),
            whole((48, D)),
            whole((8, 128)),
        ],
        scratch_shapes=[VMEM((48, vocab), bf16), VMEM((D, 8), f32)],
    )
    return pl.pallas_call(
        functools.partial(embed_kernel, local_rows),
        grid_spec=spec,
        out_shape=[
            jax.ShapeDtypeStruct((group, D), bf16),
            jax.ShapeDtypeStruct((D, group), bf16),
            jax.ShapeDtypeStruct((group, 3 * SLOT), bf16),
            jax.ShapeDtypeStruct((group, D), bf16),
            jax.ShapeDtypeStruct((blocks, 48, rows), bf16),
            jax.ShapeDtypeStruct((blocks, 24, rows), f32),
            jax.ShapeDtypeStruct((D, rows), bf16),
            jax.ShapeDtypeStruct((rows, D), f32),
            jax.ShapeDtypeStruct((48, D), bf16),
            jax.ShapeDtypeStruct((8, 128), f32),
        ],
        compiler_params=params(),
        name="embed",
    )(z, *operands)


ROOT = math.sqrt(2.0 / math.pi)


def attend(p, tok_ref, mine_ref, k_ref, vt_ref, qt_ref, att, lse, kext, qext):
    blocks, _, rows = tok_ref.shape

    @pl.when(p == 0)
    def _():
        for b in range(blocks):
            seg = jnp.concatenate([onehot8(tok_ref[b, 17:18, :]), jnp.zeros((120, rows), f32)], axis=0)
            kext[b * rows : (b + 1) * rows, :] = jnp.transpose(seg).astype(bf16)
        seg = onehot8(mine_ref[17:18, :])
        sub = lax.broadcasted_iota(jnp.int32, seg.shape, 0)
        barred = jnp.where(sub < DOCS, -BIG * (1.0 - seg), 0.0)
        qext[...] = jnp.concatenate([barred, jnp.zeros((120, rows), f32)], axis=0).astype(bf16)

    k = k_ref[...]
    keys = jnp.concatenate([k, kext[...]], axis=1)
    zeros = jnp.zeros((HEAD_DIM, rows), bf16)
    ones = jnp.ones((HEAD_DIM, blocks * rows), bf16)
    largest = jnp.max(jnp.abs(k), axis=0, keepdims=True).astype(f32)
    bound = jnp.max(dot(jnp.broadcast_to(largest, (8, PAIR)).astype(bf16), jnp.abs(qt_ref[...])))

    def heads(shifted):
        results = []
        for h in range(2):
            q = qt_ref[h * HEAD_DIM : (h + 1) * HEAD_DIM, :]
            v = vt_ref[h * HEAD_DIM : (h + 1) * HEAD_DIM, :]
            queries = jnp.concatenate([q, zeros, qext[...]] if h == 0 else [zeros, q, qext[...]], axis=0)
            scores = dot(keys, queries)
            if shifted:
                top = jnp.max(scores, axis=0, keepdims=True)
                scores = scores - top
            total = dot(jnp.concatenate([v, ones], axis=0), jnp.exp(scores).astype(bf16))
            results.append(total[:HEAD_DIM] / total[HEAD_DIM:])
            log_sum = jnp.log(total[HEAD_DIM : HEAD_DIM + 1])
            lse[pl.ds(2 * p + h, 1), :] = log_sum + top if shifted else log_sum
        att[pl.ds(pl.multiple_of(p * PAIR, PAIR), PAIR), :] = jnp.concatenate(results, axis=0)

    safe = bound < SAFE
    pl.when(safe)(lambda: heads(False))
    pl.when(jnp.logical_not(safe))(lambda: heads(True))


def front_kernel(
    local_rows,
    per,
    z_ref,
    tok_ref,
    tab_ref,
    up_w_ref,
    up_b_ref,
    gain_ref,
    shift_ref,
    qb_ref,
    vb_ref,
    w_ref,
    own_ref,
    normed_ref,
    lhs_ref,
    sc_ref,
    h0_ref,
    rhs_ref,
    mean_ref,
    own_w_ref,
    att,
    lse,
    keys,
    values,
    queries,
    tab3,
    vcol,
    own_b,
    kext,
    qext,
):
    i = pl.program_id(0)
    blocks, _, rows = tok_ref.shape

    @pl.when(i < blocks)
    def _():
        place = pl.ds(pl.multiple_of(i * rows, rows), rows)
        embed_body(
            local_rows, z_ref, tok_ref, tab_ref, up_w_ref, up_b_ref, gain_ref, shift_ref, qb_ref, vb_ref, w_ref, own_b,
            own_w_ref, per, keys.at[place, :], values.at[:, place], own_ref, normed_ref, lhs_ref, sc_ref, queries,
            h0_ref, rhs_ref, mean_ref, tab3, vcol,
        )

    @pl.when(i >= blocks)
    def _():
        p = i - blocks
        pair = pl.ds(pl.multiple_of(p * PAIR, PAIR), PAIR)
        mine = tok_ref.at[z_ref[0]]
        attend(p, tok_ref, mine, keys.at[:, pair], values.at[pair, :], queries.at[pair, :], att, lse, kext, qext)


def front(z, tok, tab, up_w, vectors, w, local_rows, per):
    blocks, _, rows = tok.shape
    group = blocks * rows
    vocab = tab.shape[0] * tab.shape[2]
    operands = (tok, tab, up_w, *vectors, w)
    spec = pltpu.PrefetchScalarGridSpec(
        num_scalar_prefetch=1,
        grid=(blocks + HEADS // 2,),
        in_specs=[whole(x.shape) for x in operands],
        out_specs=[
            pl.BlockSpec((rows, 3 * SLOT), lambda i, z: (jnp.minimum(i, blocks - 1), 0)),
            pl.BlockSpec((rows, D), lambda i, z: (jnp.minimum(i, blocks - 1), 0)),
            pl.BlockSpec((1, 48, rows), lambda i, z: (jnp.minimum(i, blocks - 1), 0, 0)),
            pl.BlockSpec((1, 24, rows), lambda i, z: (jnp.minimum(i, blocks - 1), 0, 0)),
            whole((rows, D)),
            whole((48, D)),
            whole((8, 128)),
            whole((D, 3 * SLOT)),
            whole((D, rows)),
            whole((16, rows)),
        ],
        scratch_shapes=[
            VMEM((group, D), bf16),
            VMEM((D, group), bf16),
            VMEM((D, rows), bf16),
            VMEM((48, vocab), bf16),
            VMEM((D, 8), f32),
            VMEM((8, 3 * SLOT), f32),
            VMEM((group, PAIR), bf16),
            VMEM((PAIR, rows), bf16),
        ],
    )
    return pl.pallas_call(
        functools.partial(front_kernel, local_rows, per),
        grid_spec=spec,
        out_shape=[
            jax.ShapeDtypeStruct((group, 3 * SLOT), bf16),
            jax.ShapeDtypeStruct((group, D), bf16),
            jax.ShapeDtypeStruct((blocks, 48, rows), bf16),
            jax.ShapeDtypeStruct((blocks, 24, rows), f32),
            jax.ShapeDtypeStruct((rows, D), f32),
            jax.ShapeDtypeStruct((48, D), bf16),
            jax.ShapeDtypeStruct((8, 128), f32),
            jax.ShapeDtypeStruct((D, 3 * SLOT), bf16),
            jax.ShapeDtypeStruct((D, rows), f32),
            jax.ShapeDtypeStruct((16, rows), f32),
        ],
        compiler_params=params(),
        name="front",
    )(z, *operands)


def gelu_parts(x):
    square = x * x
    t = jnp.tanh(x * (ROOT + (ROOT * 0.044715) * square))
    half = 0.5 * (1.0 + t)
    slope = half + (0.5 * x) * (1.0 - t * t) * (ROOT + (3.0 * ROOT * 0.044715) * square)
    return (x * half).astype(bf16), slope


def layer_kernel(
    per,
    tok_ref,
    mine_ref,
    k_ref,
    vt_ref,
    qt_ref,
    h0_ref,
    cot_ref,
    vec_ref,
    b1_ref,
    wo_ref,
    w1_ref,
    w2_ref,
    out_ref,
    h1g_ref,
    msg_ref,
    dwo_ref,
    dw1_ref,
    dw2_ref,
    small_ref,
    kext,
    qext,
    att,
    lse,
    wo,
    wo_slots,
    w1,
    w2,
    sems,
):
    p = pl.program_id(0)
    last = pl.num_programs(0) - 1
    blocks, _, rows = tok_ref.shape
    copies = [
        pltpu.make_async_copy(wo_ref, wo, sems.at[0]),
        pltpu.make_async_copy(w1_ref, w1, sems.at[1]),
        pltpu.make_async_copy(w2_ref, w2, sems.at[2]),
    ]

    @pl.when(p == 0)
    def _():
        for c in copies:
            c.start()

    attend(p, tok_ref, mine_ref, k_ref, vt_ref, qt_ref, att, lse, kext, qext)

    @pl.when(p == last)
    def _():
        for c in copies:
            c.wait()
        attended = att[...].astype(bf16)
        hidden1 = h0_ref[...] + dot(attended, wo[...], TN) + vec_ref[0:1, :]
        unit, inverse = norm_parts(hidden1)
        normed2 = (unit * vec_ref[1:2, :] + vec_ref[2:3, :]).astype(bf16)
        cot = cot_ref[...]
        out_grad = cot.astype(bf16)
        block_out = hidden1 + vec_ref[3:4, :]
        norm_grad = jnp.zeros_like(hidden1)
        inner_sums = []
        for c in range(FF // D):
            cols = slice(c * D, (c + 1) * D)
            x = dot(normed2, w1[:, cols]) + b1_ref[c : c + 1, :]
            active, slope = gelu_parts(x)
            block_out = block_out + dot(active, w2[cols, :])
            inner_grad = (dot(out_grad, w2[cols, :], NT) * slope).astype(bf16)
            dw2_ref[cols, :] = dot(active, out_grad, TN).astype(bf16)
            dw1_ref[:, cols] = dot(normed2, inner_grad, TN).astype(bf16)
            norm_grad = norm_grad + dot(inner_grad, w1[:, cols], NT)
            inner_sums.append(column_sum(inner_grad.astype(f32)))
        out_ref[...] = block_out
        hidden1_grad = cot + norm_pull(norm_grad, unit, inverse, vec_ref[1:2, :])
        h1g_ref[...] = hidden1_grad
        branch = hidden1_grad.astype(bf16)
        dwo_ref[...] = dot(attended, branch).astype(bf16)
        small_ref[...] = jnp.concatenate(
            [
                column_sum(branch.astype(f32)),
                column_sum(norm_grad * unit),
                column_sum(norm_grad),
                column_sum(out_grad.astype(f32)),
                *inner_sums,
            ],
            axis=0,
        )
        seg = onehot8(mine_ref[17:18, :])
        back = dot(wo[...], branch, NT).astype(bf16).astype(f32)
        product = back * att[...]
        for j in range(blocks):
            heads = [h for h in range(per * j, per * (j + 1)) if h < HEADS]
            wo_slots[...] = jnp.zeros_like(wo_slots)
            size = len(heads) * HEAD_DIM
            rows_ext = [jnp.zeros((HEAD_DIM, rows), f32), jnp.where(
                lax.broadcasted_iota(jnp.int32, (8, rows), 0) < DOCS, -BIG * (1.0 - seg), 0.0
            )[:DOCS]]
            lse_parts = []
            delta_parts = []
            for n in range(3):
                h = per * j + n
                if n < per and h < HEADS:
                    delta = column_sum(product[h * HEAD_DIM : (h + 1) * HEAD_DIM])
                    lse_parts += split3(-lse[h : h + 1, :])
                    delta_parts += split3(-delta)
                else:
                    lse_parts += [jnp.zeros((1, rows), f32)] * 3
                    delta_parts += [jnp.zeros((1, rows), f32)] * 3
            used = DOCS + 18
            rows_ext = rows_ext + lse_parts + delta_parts + [jnp.zeros((HEAD_DIM - used, rows), f32)]
            ext = jnp.transpose(jnp.concatenate(rows_ext, axis=0))
            if size:
                wo_slots[:size, :] = wo[heads[0] * HEAD_DIM : heads[0] * HEAD_DIM + size, :]
            grads = dot(branch, wo_slots[...], NT)
            msg_ref[j, :, :PAIR] = grads[:, :PAIR].astype(bf16)
            msg_ref[j, :, PAIR:] = (grads[:, PAIR:] + ext).astype(bf16)


def layer(tok, mine, k, vt, qt, h0, cot, vec, b1, wo, w1, w2, per):
    blocks, _, rows = tok.shape
    group = blocks * rows
    any_spec = pl.BlockSpec(memory_space=pl.ANY)
    return pl.pallas_call(
        functools.partial(layer_kernel, per),
        grid=(HEADS // 2,),
        in_specs=[
            whole(tok.shape),
            whole(mine.shape),
            pl.BlockSpec((group, PAIR), lambda p: (0, p)),
            pl.BlockSpec((PAIR, group), lambda p: (p, 0)),
            pl.BlockSpec((PAIR, rows), lambda p: (p, 0)),
            whole(h0.shape),
            whole(cot.shape),
            whole(vec.shape),
            whole(b1.shape),
            any_spec,
            any_spec,
            any_spec,
        ],
        out_specs=[
            whole((rows, D)),
            whole((rows, D)),
            whole((blocks, rows, SLOT)),
            whole((D, D)),
            whole((D, FF)),
            whole((FF, D)),
            whole((8, D)),
        ],
        out_shape=[
            jax.ShapeDtypeStruct((rows, D), f32),
            jax.ShapeDtypeStruct((rows, D), f32),
            jax.ShapeDtypeStruct((blocks, rows, SLOT), bf16),
            jax.ShapeDtypeStruct((D, D), bf16),
            jax.ShapeDtypeStruct((D, FF), bf16),
            jax.ShapeDtypeStruct((FF, D), bf16),
            jax.ShapeDtypeStruct((8, D), f32),
        ],
        scratch_shapes=[
            VMEM((group, PAIR), bf16),
            VMEM((PAIR, rows), bf16),
            VMEM((D, rows), f32),
            VMEM((16, rows), f32),
            VMEM((D, D), bf16),
            VMEM((SLOT, D), bf16),
            VMEM((D, FF), bf16),
            VMEM((FF, D), bf16),
            pltpu.SemaphoreType.DMA((3,)),
        ],
        compiler_params=params(),
        name="layer",
    )(tok, mine, k, vt, qt, h0, cot, vec, b1, wo, w1, w2)


def back_prepare(tok_ref, own_ref, kt, vt):
    blocks, _, rows = tok_ref.shape
    for b in range(blocks):
        place = slice(b * rows, (b + 1) * rows)
        seg = onehot8(tok_ref[b, 17:18, :])
        seg = jnp.concatenate([seg, jnp.zeros((HEAD_DIM - 8, rows), f32)], axis=0)
        sub = lax.broadcasted_iota(jnp.int32, seg.shape, 0)
        k_ext = jnp.where((sub >= DOCS) & (sub < DOCS + 9), 1.0, jnp.where(sub < DOCS, seg, 0.0))
        v_ext = jnp.where((sub >= DOCS + 9) & (sub < DOCS + 18), 1.0, 0.0)
        kt_b = jnp.transpose(own_ref[place, SLOT : 2 * SLOT].astype(f32))
        vt_b = jnp.transpose(own_ref[place, 2 * SLOT :].astype(f32))
        kt[:, place] = jnp.concatenate([kt_b[:EXT], k_ext], axis=0).astype(bf16)
        vt[:, place] = jnp.concatenate([vt_b[:EXT], v_ext], axis=0).astype(bf16)


def back_block(per, q, msg, keys, kt, vt, dkt, dvt):
    lane = lax.broadcasted_iota(jnp.int32, q.shape, 1)
    m = msg.astype(f32)
    queries = jnp.where(lane < EXT, q.astype(f32), m)
    q_t = jnp.transpose(q.astype(f32)).astype(bf16)
    m_t = jnp.transpose(m).astype(bf16)
    dq = jnp.zeros(q.shape, f32)
    for h in range(per):
        head = slice(h * HEAD_DIM, (h + 1) * HEAD_DIM)
        mine = (lane >= h * HEAD_DIM) & (lane < (h + 1) * HEAD_DIM)
        low = EXT + DOCS + 3 * h
        barred = (lane >= EXT) & (lane < EXT + DOCS)
        use_q = mine | barred | ((lane >= low) & (lane < low + 3))
        use_m = mine | ((lane >= low + 9) & (lane < low + 12))
        probs = jnp.exp(dot(jnp.where(use_q, queries, 0.0).astype(bf16), kt[...]))
        score_grad = (probs * dot(jnp.where(use_m, m, 0.0).astype(bf16), vt[...])).astype(bf16)
        dvt[head, :] += dot(m_t[head], probs.astype(bf16))
        dkt[head, :] += dot(q_t[head], score_grad)
        dq = dq + jnp.where(mine, dot(score_grad, keys), 0.0)
    return (dq * SCALE).astype(bf16)


def back_kernel(per, tok_ref, own_ref, msg_ref, grad_ref, kt, vt, dkt, dvt):
    blocks, _, rows = tok_ref.shape
    back_prepare(tok_ref, own_ref, kt, vt)
    dkt[...] = jnp.zeros_like(dkt)
    dvt[...] = jnp.zeros_like(dvt)

    def step(b, carry):
        place = pl.ds(pl.multiple_of(b * rows, rows), rows)
        keys = own_ref[:, SLOT : 2 * SLOT]
        grad_ref[place, :SLOT] = back_block(per, own_ref[place, :SLOT], msg_ref[b], keys, kt, vt, dkt, dvt)
        return carry

    lax.fori_loop(0, blocks, step, 0)
    for b in range(blocks):
        place = slice(b * rows, (b + 1) * rows)
        grad_ref[place, SLOT : 2 * SLOT] = jnp.transpose(dkt[:, place]).astype(bf16)
        grad_ref[place, 2 * SLOT :] = jnp.transpose(dvt[:, place]).astype(bf16)


def back(tok, own, msg, per):
    group = own.shape[0]
    return pl.pallas_call(
        functools.partial(back_kernel, per),
        in_specs=[pl.BlockSpec(memory_space=VMEM)] * 3,
        out_specs=pl.BlockSpec(memory_space=VMEM),
        out_shape=jax.ShapeDtypeStruct(own.shape, bf16),
        scratch_shapes=[
            VMEM((SLOT, group), bf16),
            VMEM((SLOT, group), bf16),
            VMEM((SLOT, group), f32),
            VMEM((SLOT, group), f32),
        ],
        compiler_params=params(),
        name="attention_back",
    )(tok, own, msg)

def final_kernel(
    z_ref, tok_ref, grad_ref, normed_ref, lhs_ref, sc_ref, rhs_ref, h1g_ref, up_w_ref, vec_ref, own_w_ref, mean_ref,
    dw_ref, noise_ref, table_ref, small_ref, acc,
):
    i = pl.program_id(0)
    last = pl.num_programs(0) - 1
    vocab = table_ref.shape[1]
    mean = mean_ref[0:1, 0:1]

    @pl.when(i == 0)
    def _():
        acc[...] = jnp.zeros_like(acc)
        small_ref[...] = jnp.zeros_like(small_ref)
        table_ref[...] = jnp.zeros_like(table_ref)

    grad = grad_ref[...]
    hidden0 = dot(lhs_ref[0], rhs_ref[...], TN)
    unit, inverse = norm_parts(hidden0)
    norm_grad = dot(grad, own_w_ref[...], NT)
    acc[...] += dot(normed_ref[...], grad, TN)
    own = (z_ref[0] == i).astype(f32)
    h0_grad = (norm_pull(norm_grad, unit, inverse, vec_ref[1:2, :]) + own * h1g_ref[...]).astype(bf16)
    mixed_grad = dot(up_w_ref[...], h0_grad, NT)
    sc = sc_ref[0]
    noise_ref[0] = sc[17:18] * mixed_grad
    embedded_grad = sc[16:17] * mixed_grad
    picked = sc[:16]
    norm_term = -jnp.sum(embedded_grad * picked, axis=(0, 1), keepdims=True) / (mean * mean)
    ids = tok_ref[i][16:17, :]
    table3 = dot(jnp.concatenate(split3(embedded_grad / mean), axis=0).astype(bf16), id_matrix(vocab, ids), NT)
    table_ref[...] += table3[:16] + table3[16:32] + table3[32:48]
    gradf = grad.astype(f32)
    small_ref[...] += jnp.concatenate(
        [
            dot(lhs_ref[0, :16, :], h0_grad),
            column_sum(h0_grad.astype(f32)),
            column_sum(norm_grad * unit),
            column_sum(norm_grad),
            column_sum(gradf),
            jnp.broadcast_to(norm_term, (1, D)),
            jnp.zeros((3, D), f32),
        ],
        axis=0,
    )

    @pl.when(i == last)
    def _():
        dw_ref[...] = acc[...].astype(bf16)


def final(z, tok, grad, normed, lhs, sc, rhs, h1g, up_w, vec, own_w, mean, vocab):
    blocks, _, rows = tok.shape
    spec = pltpu.PrefetchScalarGridSpec(
        num_scalar_prefetch=1,
        grid=(blocks,),
        in_specs=[
            whole(tok.shape),
            pl.BlockSpec((rows, 3 * SLOT), lambda i, z: (i, 0)),
            pl.BlockSpec((rows, D), lambda i, z: (i, 0)),
            pl.BlockSpec((1, 48, rows), lambda i, z: (i, 0, 0)),
            pl.BlockSpec((1, 24, rows), lambda i, z: (i, 0, 0)),
            whole(rhs.shape),
            whole(h1g.shape),
            whole(up_w.shape),
            whole(vec.shape),
            whole(own_w.shape),
            whole(mean.shape),
        ],
        out_specs=[
            whole((D, 3 * SLOT)),
            pl.BlockSpec((1, 16, rows), lambda i, z: (i, 0, 0)),
            whole((16, vocab)),
            whole((24, D)),
        ],
        scratch_shapes=[VMEM((D, 3 * SLOT), f32)],
    )
    return pl.pallas_call(
        final_kernel,
        grid_spec=spec,
        out_shape=[
            jax.ShapeDtypeStruct((D, 3 * SLOT), bf16),
            jax.ShapeDtypeStruct((blocks, 16, rows), f32),
            jax.ShapeDtypeStruct((16, vocab), f32),
            jax.ShapeDtypeStruct((24, D), f32),
        ],
        compiler_params=params(),
        name="embed_back",
    )(z, tok, grad, normed, lhs, sc, rhs, h1g, up_w, vec, own_w, mean)


UNITS = (
    (1, 0, 768, True),
    (1, 768, 768, False),
    (1, 1536, 768, True),
    (1, 2304, 768, False),
    (0, 0, 384, True),
    (0, 384, 384, False),
    (2, 0, 384, True),
    (2, 384, 384, False),
    (3, 0, 384, True),
    (3, 384, 384, False),
)
UNIT_ROWS = (384, 96, 96, 96)
CORE, WIDE, NARROW, NEAR, FAR, DONE = range(6)
PLAN = {
    "chunk0": [(CORE, 0)],
    "chunk1": [(CORE, 1), (WIDE, 0)],
    "chunk2": [(CORE, 2), (WIDE, 1)],
    "chunk3": [(CORE, 3), (WIDE, 2)],
    "sent": [(CORE, 6), (CORE, 7), (WIDE, 3), (NARROW, 0), (WIDE, 4), (WIDE, 5)],
    "prep": [(WIDE, 6), (WIDE, 7), (NARROW, 1)],
    "q0": [],
    "q1": [(NARROW, 2), (NARROW, 3)],
    "q2": [(NARROW, 4), (NARROW, 6)],
    "q3": [(NARROW, 5), (NARROW, 7), (NEAR, 0)],
    "kv": [(NEAR, 1), (FAR, 0)],
    "dw": [(CORE, 8), (CORE, 9), (NEAR, 2), (NEAR, 3)],
    "e0": [(WIDE, 8), (WIDE, 9), (FAR, 1)],
    "e1": [(FAR, 2), (FAR, 3)],
    "e2": [(NARROW, 8), (NARROW, 9)],
    "e3": [(DONE, 0), (DONE, 1)],
    "end": [(DONE, 2), (DONE, 3)],
}


def mega_kernel(
    per,
    plan,
    tok_ref,
    lse_ref,
    gain1_ref,
    out_b_ref,
    gain2_ref,
    shift2_ref,
    outer_b_ref,
    b1_ref,
    lhs_ref,
    sc_ref,
    rhs_ref,
    mean_ref,
    up_w_ref,
    att_hbm,
    h0_hbm,
    cot_hbm,
    wo_hbm,
    w1_hbm,
    w2_hbm,
    own_hbm,
    normed_hbm,
    own_w_hbm,
    out_hbm,
    dwo_out,
    dw1_out,
    dw2_out,
    dw_out,
    small_out,
    table_out,
    noise_out,
    dw2,
    dw1,
    dwo,
    dwq,
    h1g,
    msg_out,
    msgs,
    small1,
    msg_send,
    msg_recv,
    first2,
    chunk_send,
    chunk_recv,
    send_parts,
    parts,
    mine,
    lines,
    sums,
    dw_parts,
    noise_mine,
    noise_parts,
    sends,
    recvs,
    *scratch,
):
    blocks, _, rows = tok_ref.shape
    dp = lax.axis_index("dp")
    z = lax.axis_index("blk")
    dp_n, blk_n = parts.shape[0], lines.shape[0]
    group = blocks * rows
    half = D // 2
    nd, nz = dp_n - 1, blk_n - 1
    grads = (dw2, dw1, dwo, dwq)
    outs = (dw2_out, dw1_out, dwo_out)
    scratch = list(scratch)
    units = []
    lines_of = []
    core, x, y = lax.rem(dp, 2), lax.rem(lax.div(dp, 2), 2), lax.div(dp, 4)
    sibling = (dp + 1 - 2 * core, z)

    def chunk_copy(c):
        at = (c // 2, c % 2)
        return remote(dw2.at[at + (1 - core,)], first2.at[at], chunk_send.at[c], chunk_recv.at[c], sibling)

    for which, first, size, by_x in UNITS:
        buffer = first2 if which == 0 else scratch.pop(0)
        rest = [scratch.pop(0) for _ in range(4)]
        chunks = [functools.partial(chunk_copy, c) for c in range(4)] if which == 0 else None
        units.append(Scatter(grads[which], pl.ds(first, size), by_x, buffer, *rest, chunks=chunks))
        if which != 3 and not by_x:
            lines_of.append(LineScatter(units[-2:], outs[which], *[scratch.pop(0) for _ in range(7)]))

    def run(slot):
        for kind, n in plan[slot]:
            if kind == CORE:
                units[n].start()
            elif kind == WIDE:
                units[n].core_to_wide()
            elif kind == NARROW:
                units[n].wide_to_narrow()
            elif kind == NEAR:
                lines_of[n].start()
            elif kind == FAR:
                lines_of[n].near_to_far()
            else:
                lines_of[n].finish()

    def z_peer(k):
        low, high = lax.rem(z, 2), lax.div(z, 2)
        return (low + (k % 2) * (1 - 2 * low)) + 2 * (high + (k // 2) * (1 - 2 * high))

    def message(k):
        return remote(msg_out.at[z_peer(k)], msgs.at[k], msg_send.at[k], msg_recv.at[k], (dp, z_peer(k)))

    dp_to = [(lax.rem(dp + k, dp_n), z) for k in range(1, dp_n)]
    z_to = [(dp, lax.rem(z + k, blk_n)) for k in range(1, blk_n)]

    greet(dp_to + z_to)

    def dense(att_v, h0_v, cot_v, wo, w1, w2, wo_slots, sems):
        pairs = [(wo_hbm, wo), (att_hbm, att_v), (h0_hbm, h0_v), (cot_hbm, cot_v)]
        for c in range(FF // D):
            part = pl.ds(c * D, D)
            pairs += [(w1_hbm.at[:, part], w1.at[:, part]), (w2_hbm.at[part], w2.at[part])]
        moves = [pltpu.make_async_copy(src, dst, sems.at[n]) for n, (src, dst) in enumerate(pairs)]
        for c in moves:
            c.start()
        for c in moves[:3]:
            c.wait()
        attended = att_v[...].astype(bf16)
        hidden1 = h0_v[...] + dot(attended, wo[...], TN) + row(out_b_ref)
        unit, inverse = norm_parts(hidden1)
        normed2 = (unit * row(gain2_ref) + row(shift2_ref)).astype(bf16)
        moves[3].wait()
        cot = cot_v[...]
        out_grad = cot.astype(bf16)
        h0_v[...] = hidden1 + row(outer_b_ref)
        h1g[...] = jnp.zeros_like(h1g)
        inner_sums = []
        for c in range(FF // D):
            cols = slice(c * D, (c + 1) * D)
            moves[4 + 2 * c].wait()
            moves[5 + 2 * c].wait()
            active, slope = gelu_parts(dot(normed2, w1[:, cols]) + b1_ref[pl.ds(c * D, D)].reshape(1, D))
            h0_v[...] += dot(active, w2[cols, :])
            inner_grad = (dot(out_grad, w2[cols, :], NT) * slope).astype(bf16)
            if c == 0:
                met(dp_to + z_to)
            part = dot(active, out_grad, TN).astype(bf16)
            dw2[c // 2, c % 2, 0] = part[: D // 2]
            dw2[c // 2, c % 2, 1] = part[D // 2 :]
            chunk_copy(c).start()
            part = dot(normed2, inner_grad, TN).astype(bf16)
            for k in range(8):
                dw1[k // 4, k // 2 % 2, k % 2, :, cols] = part[k * 96 : (k + 1) * 96]
            h1g[...] += dot(inner_grad, w1[:, cols], NT)
            inner_sums.append(column_sum(inner_grad.astype(f32)))
            run(("chunk0", "chunk1", "chunk2", "chunk3")[c])
        norm_grad = h1g[...]
        write = pltpu.make_async_copy(h0_v, out_hbm, sems.at[0])
        write.start()
        hidden1_grad = cot + norm_pull(norm_grad, unit, inverse, row(gain2_ref))
        h1g[...] = hidden1_grad
        branch = hidden1_grad.astype(bf16)
        seg = onehot8(tok_ref[z, 17:18, :])
        sub = lax.broadcasted_iota(jnp.int32, (8, rows), 0)
        barred = jnp.where(sub < DOCS, -BIG * (1.0 - seg), 0.0)[:DOCS]
        product = dot(wo[...], branch, NT).astype(bf16).astype(f32) * att_v[...]
        wo_slots[...] = jnp.zeros_like(wo_slots)
        size = per * HEAD_DIM
        for j in range(blocks):
            lse_parts = []
            delta_parts = []
            for h in range(per * j, per * (j + 1)):
                delta = column_sum(product[h * HEAD_DIM : (h + 1) * HEAD_DIM])
                lse_parts += split3(-lse_ref[h : h + 1, :])
                delta_parts += split3(-delta)
            rest = jnp.zeros((HEAD_DIM - DOCS - 6 * per, rows), f32)
            ext = [jnp.zeros((HEAD_DIM, rows), f32), barred] + lse_parts + delta_parts + [rest]
            ext = jnp.transpose(jnp.concatenate(ext, axis=0))
            wo_slots[:size, :] = wo[j * size : (j + 1) * size, :]
            grads = dot(branch, wo_slots[...], NT)
            msg_out[j, :, :PAIR] = grads[:, :PAIR].astype(bf16)
            msg_out[j, :, PAIR:] = (grads[:, PAIR:] + ext).astype(bf16)
        message(1).start()
        message(2).start()
        part = dot(attended, branch).astype(bf16)
        for k in range(8):
            dwo[k // 4, k // 2 % 2, k % 2] = part[k * 96 : (k + 1) * 96]
        small1[...] = jnp.concatenate(
            [
                column_sum(branch.astype(f32)),
                column_sum(norm_grad * unit),
                column_sum(norm_grad),
                column_sum(out_grad.astype(f32)),
                *inner_sums,
            ],
            axis=0,
        )
        run("sent")
        write.wait()

    pl.run_scoped(
        dense,
        VMEM((D, rows), f32),
        VMEM((rows, D), f32),
        VMEM((rows, D), f32),
        VMEM((D, D), bf16),
        VMEM((D, FF), bf16),
        VMEM((FF, D), bf16),
        VMEM((SLOT, D), bf16),
        pltpu.SemaphoreType.DMA((12,)),
    )

    def backward(grad, own, kt, vt, dkt, dvt, sem):
        load = pltpu.make_async_copy(own_hbm, own, sem)
        load.start()
        dkt[...] = jnp.zeros_like(dkt)
        dvt[...] = jnp.zeros_like(dvt)
        msgs[0] = msg_out[z]
        load.wait()
        back_prepare(tok_ref, own, kt, vt)
        run("prep")

        def body(b, carry):
            low, high = lax.rem(z, 2), lax.div(z, 2)
            b_low, b_high = lax.rem(b, 2), lax.div(b, 2)
            other = (low + b_low * (1 - 2 * low)) + 2 * (high + b_high * (1 - 2 * high))
            for k in range(blocks):
                if k or plan["q0"]:

                    @pl.when(b == k)
                    def _():
                        if k == 1:
                            message(3).start()
                        if k:
                            message(k).wait()
                        run(("q0", "q1", "q2", "q3")[k])

            place = pl.ds(pl.multiple_of(other * rows, rows), rows)
            keys = own[:, SLOT : 2 * SLOT]
            grad[place, :SLOT] = back_block(per, own[place, :SLOT], msgs[b], keys, kt, vt, dkt, dvt)
            return carry

        lax.fori_loop(0, blocks, body, 0)
        for b in range(blocks):
            place = slice(b * rows, (b + 1) * rows)
            grad[place, SLOT : 2 * SLOT] = jnp.transpose(dkt[:, place]).astype(bf16)
            grad[place, 2 * SLOT :] = jnp.transpose(dvt[:, place]).astype(bf16)

    def noise_copy(i):
        k = lax.rem(i - z + blk_n, blk_n) - 1
        k = jnp.maximum(k, 0)
        n = 2 * nd + nz + k
        return remote(noise_mine.at[i], noise_parts.at[z], sends.at[n], recvs.at[n], (dp, i))

    def embedding(grad, normed, own_w, sems):
        loads = [
            pltpu.make_async_copy(normed_hbm, normed, sems.at[0]),
            pltpu.make_async_copy(own_w_hbm, own_w, sems.at[1]),
        ]
        for c in loads:
            c.start()
        run("kv")
        for c in loads:
            c.wait()
        part = dot(normed[...], grad[...], TN).astype(bf16)
        for k in range(8):
            dwq[k // 4, k // 2 % 2, k % 2] = part[k * 96 : (k + 1) * 96]
        run("dw")
        mean = mean_ref[0:1, 0:1]
        small2 = jnp.zeros((24, D), f32)
        vocab = dp_n * 128
        table = jnp.zeros((16, vocab), f32)
        for first in range(0, blocks, 2):
            two = (first, first + 1)
            g = grad[first * rows : (first + 2) * rows, :]
            lhs = jnp.concatenate([lhs_ref[i] for i in two], axis=1)
            hidden0 = dot(lhs, rhs_ref[...], TN)
            unit, inverse = norm_parts(hidden0)
            norm_grad = dot(g, own_w[...], NT)
            later = jnp.concatenate([(z == i).astype(f32) * h1g[...] for i in two], axis=0)
            h0_grad = (norm_pull(norm_grad, unit, inverse, row(gain1_ref)) + later).astype(bf16)
            run(("e0", "e2")[first // 2])
            mixed_grad = dot(up_w_ref[...], h0_grad, NT)
            sc = jnp.concatenate([sc_ref[i] for i in two], axis=1)
            for n, i in enumerate(two):
                noise_mine[i] = (sc[17:18] * mixed_grad)[:, n * rows : (n + 1) * rows].astype(bf16)
                pl.when(z != i)(noise_copy(i).start)
            embedded_grad = sc[16:17] * mixed_grad
            norm_term = -jnp.sum(embedded_grad * sc[:16], axis=(0, 1), keepdims=True) / (mean * mean)
            table3 = dot(
                jnp.concatenate(split3(embedded_grad / mean), axis=0).astype(bf16),
                id_matrix(vocab, jnp.concatenate([tok_ref[i][16:17, :] for i in two], axis=1)),
                NT,
            )
            table = table + (table3[:16] + table3[16:32] + table3[32:48])
            small2 = small2 + jnp.concatenate(
                [
                    dot(lhs[:16, :], h0_grad),
                    column_sum(h0_grad.astype(f32)),
                    column_sum(norm_grad * unit),
                    column_sum(norm_grad),
                    jnp.broadcast_to(norm_term, (1, D)),
                    *[(z == j).astype(f32) * column_sum(g.astype(f32)) for j in range(blocks)],
                ],
                axis=0,
            )
            run(("e1", "e3")[first // 2])
        flat = jnp.concatenate([small1[...], small2], axis=0)
        for k in range(dp_n):
            n = k % 4
            send_parts[k, :, :half] = flat[8 * n : 8 * n + 8, (k // 4) * half : (k // 4 + 1) * half]
            send_parts[k, :, half : half + 128] = table[:8, k * 128 : (k + 1) * 128]
            send_parts[k, :, half + 128 :] = table[8:, k * 128 : (k + 1) * 128]

    def rest(grad):
        pl.run_scoped(
            functools.partial(backward, grad),
            VMEM((group, 3 * SLOT), bf16),
            VMEM((SLOT, group), bf16),
            VMEM((SLOT, group), bf16),
            VMEM((SLOT, group), f32),
            VMEM((SLOT, group), f32),
            pltpu.SemaphoreType.DMA,
        )
        pl.run_scoped(
            functools.partial(embedding, grad),
            VMEM((group, D), bf16),
            VMEM((D, 3 * SLOT), bf16),
            pltpu.SemaphoreType.DMA((2,)),
        )

    pl.run_scoped(rest, VMEM((group, 3 * SLOT), bf16))

    def spread(src, dst, peers, first):
        return [remote(src(p), dst, sends.at[first + k], recvs.at[first + k], p) for k, p in enumerate(peers)]

    one = spread(lambda p: send_parts.at[p[0]], parts.at[dp], dp_to, 0)
    four = spread(lambda p: noise_mine.at[p[1]], noise_parts.at[z], z_to, 2 * nd + nz)
    for c in one:
        c.start()
    parts[dp] = send_parts[dp]
    noise_parts[z] = noise_mine[z]
    dw_parts[...] = jnp.zeros_like(dw_parts)
    for u in units[8:]:
        total = u.narrow_sum()
        q = total.shape[0] // blk_n
        for k in range(blk_n):
            dw_parts[k, :q, u.columns] = total[k * q : (k + 1) * q]
    five = spread(lambda p: dw_parts.at[p[1]], dw_out.at[z], z_to, 2 * nd + 2 * nz)
    for c in five:
        c.start()
    dw_out[z] = dw_parts[z]
    for c in one:
        c.wait()
    total = parts[0]
    for k in range(1, dp_n):
        total = total + parts[k]
    mine[...] = total
    lines[z] = total
    two = spread(lambda p: mine, lines.at[z], z_to, nd)
    for c in two:
        c.start()
    for c in four:
        c.wait()
    total = noise_parts[0].astype(f32)
    for k in range(1, blk_n):
        total = total + noise_parts[k].astype(f32)
    noise_out[...] = total
    for c in two:
        c.wait()
    total = lines[0]
    for k in range(1, blk_n):
        total = total + lines[k]
    table_out[...] = total[:, half:]
    sums[...] = total[:, :half]
    small_out[dp] = total[:, :half]
    three = spread(lambda p: sums, small_out.at[dp], dp_to, nd + nz)
    for c in three:
        c.start()
    run("end")
    for c in three + five:
        c.wait()


def mega(small, big, dp_n, per):
    tok, att, lse, h0, cot, vectors, lhs, sc, rhs, mean, up_w = small
    blk_n, _, rows = tok.shape
    group = blk_n * rows
    share = D // (dp_n * blk_n)
    vmem = pl.BlockSpec(memory_space=VMEM)
    hbm = pl.BlockSpec(memory_space=pl.ANY)
    count = 2 * (dp_n - 1) + 3 * (blk_n - 1)
    half = D // 2
    scratch = []
    for which, _, size, by_x in UNITS:
        scratch += scatter_scratch(UNIT_ROWS[which], size, which != 0)
        if which != 3 and not by_x:
            scratch += line_scratch(UNIT_ROWS[which], size)
    in_vmem = (tok, lse, *vectors, lhs, sc, rhs, mean, up_w)
    in_hbm = (att, h0, cot) + tuple(big)
    return pl.pallas_call(
        functools.partial(mega_kernel, per, PLAN),
        in_specs=[vmem] * len(in_vmem) + [hbm] * len(in_hbm),
        out_specs=[hbm] + [vmem] * 7,
        out_shape=[
            jax.ShapeDtypeStruct((rows, D), f32),
            jax.ShapeDtypeStruct((share, D), f32),
            jax.ShapeDtypeStruct((share, FF), f32),
            jax.ShapeDtypeStruct((4 * share, D), f32),
            jax.ShapeDtypeStruct((blk_n, 32, 3 * SLOT), bf16),
            jax.ShapeDtypeStruct((dp_n, 8, half), f32),
            jax.ShapeDtypeStruct((8, 256), f32),
            jax.ShapeDtypeStruct((16, rows), f32),
        ],
        scratch_shapes=[
            VMEM((2, 2, 2, 384, D), bf16),
            VMEM((2, 2, 2, 96, FF), bf16),
            VMEM((2, 2, 2, 96, D), bf16),
            VMEM((2, 2, 2, 96, 3 * SLOT), bf16),
            VMEM((rows, D), f32),
            VMEM((blk_n, rows, SLOT), bf16),
            VMEM((blk_n, rows, SLOT), bf16),
            VMEM((8, D), f32),
            pltpu.SemaphoreType.DMA((blk_n,)),
            pltpu.SemaphoreType.DMA((blk_n,)),
            VMEM((2, 2, 384, D), bf16),
            pltpu.SemaphoreType.DMA((4,)),
            pltpu.SemaphoreType.DMA((4,)),
            VMEM((dp_n, 8, half + 256), f32),
            VMEM((dp_n, 8, half + 256), f32),
            VMEM((8, half + 256), f32),
            VMEM((blk_n, 8, half + 256), f32),
            VMEM((8, half), f32),
            VMEM((blk_n, 32, 3 * SLOT), bf16),
            VMEM((blk_n, 16, rows), bf16),
            VMEM((blk_n, 16, rows), bf16),
            pltpu.SemaphoreType.DMA((count,)),
            pltpu.SemaphoreType.DMA((count,)),
            *scratch,
        ],
        compiler_params=pltpu.CompilerParams(
            vmem_limit_bytes=63 * MIB, collective_id=1, has_side_effects=True
        ),
        name="layer_and_sums",
    )(*in_vmem, *in_hbm)


def finish_kernel(
    per, dwo_ref, dw1_ref, dw2_ref, dw_ref, flat_ref, table_sum_ref, noise_ref, mean_ref, table_ref, block_hbm,
    block_out, noise_out, table_out, up_w_out, up_b_out, gain1_out, shift1_out, qkv_out, qb_out, vb_out, dwo_out,
    out_b_out, gain2_out, shift2_out, dw1_out, b1_out, dw2_out, b2_out, mean_out, buffer, sems,
):
    load = pltpu.make_async_copy(block_hbm, buffer, sems.at[0])
    store = pltpu.make_async_copy(buffer, block_out, sems.at[1])
    load.start()
    blk_n = dw_ref.shape[0]
    vocab = table_ref.shape[1] * flat_ref.shape[0]
    load.wait()
    store.start()
    width = per * HEAD_DIM
    share = dwo_ref.shape[0]
    flat = [jnp.concatenate([flat_ref[n], flat_ref[4 + n]], axis=1) for n in range(4)]
    noise_out[...] = noise_ref[...]
    dwo_out[...] = dwo_ref[...]
    dw1_out[...] = dw1_ref[...]
    dw2_out[...] = dw2_ref[...]
    out_b_out[...] = flat[0][0]
    gain2_out[...] = flat[0][1]
    shift2_out[...] = flat[0][2]
    b2_out[...] = flat[0][3]
    for n in range(4):
        b1_out[pl.ds(n * D, D)] = flat[0][4 + n]
    up_w_out[:8, :] = flat[1]
    up_w_out[8:, :] = flat[2]
    up_b_out[...] = flat[3][0]
    gain1_out[...] = flat[3][1]
    shift1_out[...] = flat[3][2]
    for n in range(3):
        parts = [dw_ref[k].astype(f32)[:share, n * SLOT : n * SLOT + width] for k in range(blk_n)]
        qkv_out[:, n * D : (n + 1) * D] = jnp.concatenate(parts, axis=1)
    for n, out in ((0, qb_out), (2, vb_out)):
        parts = [flat[3][4 + k : 5 + k, n * SLOT : n * SLOT + width] for k in range(blk_n)]
        out[...] = jnp.concatenate(parts, axis=1)[0]
    table = table_ref[...]
    norms = jnp.sqrt(jnp.sum(table * table, axis=0, keepdims=True) + 1.0)
    total = jnp.concatenate([table_sum_ref[:, :128], table_sum_ref[:, 128:]], axis=0)
    table_out[...] = total[:, : table.shape[1]] + flat[3][3:4, :1] * table / (vocab * norms)
    mean_out[...] = mean_ref[0:1, 0:1]
    store.wait()


def finish(per, dwo, dw1, dw2, dw, flat, table_sum, noise, mean, table, block):
    vmem = pl.BlockSpec(memory_space=VMEM)
    hbm = pl.BlockSpec(memory_space=pl.ANY)
    vector = jax.ShapeDtypeStruct((D,), f32)
    share = dwo.shape[0]
    like = lambda x: jax.ShapeDtypeStruct(x.shape, x.dtype)
    shapes = [
        like(block), like(noise), like(table), jax.ShapeDtypeStruct((16, D), f32), vector, vector, vector,
        jax.ShapeDtypeStruct((share, 3 * D), f32), vector, vector, like(dwo), vector, vector, vector, like(dw1),
        jax.ShapeDtypeStruct((FF,), f32), like(dw2), vector, jax.ShapeDtypeStruct((1, 1), f32),
    ]
    return pl.pallas_call(
        functools.partial(finish_kernel, per),
        in_specs=[vmem] * 9 + [hbm],
        out_specs=[hbm] + [vmem] * 18,
        out_shape=shapes,
        scratch_shapes=[VMEM(block.shape, f32), pltpu.SemaphoreType.DMA((2,))],
        compiler_params=params(),
        name="finish",
    )(dwo, dw1, dw2, dw, flat, table_sum, noise, mean, table, block)


def shards(
    dp_n,
    blk_n,
    token_ids,
    segment_ids,
    timesteps,
    noise,
    table,
    up_weight,
    up_bias,
    norm1_gain,
    norm1_shift,
    qkv_weight,
    query_bias,
    value_bias,
    out_weight,
    out_bias,
    norm2_gain,
    norm2_shift,
    ffn_in_weight,
    ffn_in_bias,
    ffn_out_weight,
    ffn_out_bias,
    cotangent,
):
    rows = token_ids.shape[0]
    local_rows = table.shape[0]
    vp = -(-local_rows // 128) * 128
    per = -(-HEADS // blk_n)
    width = per * HEAD_DIM
    z = lax.axis_index("blk")
    z1 = z.reshape(1).astype(jnp.int32)
    vectors = (up_bias, norm1_gain, norm1_shift, query_bias, value_bias)

    if dp_n == 8 and blk_n == 4:
        tok, tab = gather(token_ids, segment_ids, timesteps, noise.T, table.T, dp_n, blk_n)
        own, normed, lhs, sc, h0, rhs, mean, own_w, att, lse = front(
            z1, tok, tab, up_weight, vectors, qkv_weight, local_rows, per
        )
        vectors = (norm1_gain, out_bias, norm2_gain, norm2_shift, ffn_out_bias, ffn_in_bias)
        block_out, dwo, dw1, dw2, dw, flat, table_sum, noise_sum = mega(
            (tok, att, lse, h0, cotangent, vectors, lhs, sc, rhs, mean, up_weight),
            (out_weight, ffn_in_weight, ffn_out_weight, own, normed, own_w),
            dp_n,
            per,
        )
        outs = list(finish(per, dwo, dw1, dw2, dw, flat, table_sum, noise_sum, mean, table.T, block_out))
        outs[1] = outs[1].T
        outs[2] = outs[2].T
        outs[-1] = outs[-1].reshape(())
        return tuple(outs)

    slots = (token_ids // local_rows) * vp + token_ids % local_rows
    scalars = jnp.stack([slots, segment_ids, timesteps]).astype(f32)
    mine = jnp.concatenate([noise.T, scalars, jnp.zeros((5, rows), f32)], axis=0)
    tok = lax.all_gather(mine, "blk")
    tab = lax.all_gather(jnp.pad(table.T, ((0, 0), (0, vp - local_rows))), "dp")
    padded = blk_n * width
    split = jnp.pad(qkv_weight.reshape(D, 3, D), ((0, 0), (0, 0), (0, padded - D)))
    own_w = lax.dynamic_slice(split, (0, 0, z * width), (D, 3, width))
    own_w = jnp.pad(own_w, ((0, 0), (0, 0), (0, SLOT - width))).reshape(D, 3 * SLOT)
    bias = jnp.pad(jnp.stack([query_bias, jnp.zeros((D,), f32), value_bias]), ((0, 0), (0, padded - D)))
    own_b = lax.dynamic_slice(bias, (0, z * width), (3, width))
    own_b = jnp.pad(own_b, ((0, 0), (0, SLOT - width))).reshape(1, 3 * SLOT)
    k, vt, own, normed, lhs, sc, qt, h0, rhs, mean = embed(
        z1, tok, tab, up_weight, vectors, qkv_weight, local_rows, own_w, own_b
    )
    vec1 = jnp.stack([up_bias, norm1_gain, norm1_shift])
    vec2 = jnp.stack([out_bias, norm2_gain, norm2_shift, ffn_out_bias])
    b1 = ffn_in_bias.reshape(FF // D, D)
    share = D // (dp_n * blk_n)
    block_out, h1g, msg, dwo, dw1, dw2, small1 = layer(
        tok, mine, k, vt, qt, h0, cotangent, vec2, b1, out_weight, ffn_in_weight, ffn_out_weight, per
    )
    msg = lax.all_to_all(msg, "blk", 0, 0)
    grad = back(tok, own, msg, per)
    dw, noise_part, table_part, small2 = final(
        z1, tok, grad, normed, lhs, sc, rhs, h1g, up_weight, vec1, own_w, mean, dp_n * vp
    )
    noise_grad = lax.psum_scatter(noise_part, "blk", scatter_dimension=0, tiled=False).T
    own_sums = small2[19].reshape(3, SLOT)[:, :width]
    own_sums = lax.dynamic_update_slice(jnp.zeros((3, padded), f32), own_sums, (0, z * width))[:, :D]
    small2, table_total, small1, own_sums = lax.psum((small2, table_part, small1, own_sums), ("dp", "blk"))
    scatter = functools.partial(lax.psum_scatter, axis_name=("dp", "blk"), scatter_dimension=0, tiled=True)
    dwo, dw1, dw2 = scatter(dwo), scatter(dw1), scatter(dw2)
    dw = lax.psum_scatter(dw, "dp", scatter_dimension=0, tiled=True)
    dw = lax.all_to_all(dw.reshape(blk_n, share, 3 * SLOT), "blk", 0, 0)
    dw = dw.reshape(blk_n, share, 3, SLOT)[..., :width].transpose(1, 2, 0, 3).reshape(share, 3, padded)[..., :D]
    table_grad = lax.dynamic_slice(table_total, (0, lax.axis_index("dp") * vp), (16, local_rows)).T
    norms = jnp.sqrt(jnp.sum(table * table, axis=-1, keepdims=True) + 1.0)
    table_grad = table_grad + small2[20, 0] * table / (dp_n * local_rows * norms)
    return (
        block_out,
        noise_grad,
        table_grad,
        small2[:16],
        small2[16],
        small2[17],
        small2[18],
        dw.reshape(share, 3 * D).astype(f32),
        own_sums[0],
        own_sums[2],
        dwo.astype(f32),
        small1[0],
        small1[1],
        small1[2],
        dw1.astype(f32),
        small1[4:8].reshape(FF),
        dw2.astype(f32),
        small1[3],
        mean[0, 0],
    )


def solution(mesh):
    rows = P(("dp", "blk"))
    wide = P(("dp", "blk"), None)
    in_specs = (rows, rows, rows, wide, P("dp", None)) + (P(),) * 15 + (wide,)
    out_specs = (
        (wide, wide, P("dp", None))
        + (P(),) * 4
        + (wide, P(), P(), wide, P(), P(), P(), wide, P(), wide, P(), P())
    )
    body = functools.partial(shards, mesh.shape["dp"], mesh.shape["blk"])
    return jax.shard_map(body, mesh=mesh, in_specs=in_specs, out_specs=out_specs, check_vma=False)
```

```python
import functools
import math

import jax
import jax.numpy as jnp
from jax import lax
from jax.experimental import pallas as pl
from jax.experimental.pallas import tpu as pltpu
from jax.sharding import PartitionSpec as P

D = 768
HEADS = 12
HEAD_DIM = 64
FF = 3072
EMB = 16
TSTEPS = 2000
DOCS = 4
PAIR = 2 * HEAD_DIM
SLOT = 256
EXT = 192
BIG = 1e30
SAFE = 64.0
SCALE = HEAD_DIM**-0.5
MIB = 2**20
MESH = pl.DeviceIdType.MESH
VMEM = pltpu.VMEM
f32 = jnp.float32
bf16 = jnp.bfloat16

NN = (((1,), (0,)), ((), ()))
NT = (((1,), (1,)), ((), ()))
TN = (((0,), (0,)), ((), ()))
TT = (((0,), (1,)), ((), ()))


def dot(left, right, dims=NN):
    return lax.dot_general(left, right, dims, preferred_element_type=f32)


def split3(x):
    high = x.astype(bf16)
    rest = x - high.astype(f32)
    middle = rest.astype(bf16)
    low = (rest - middle.astype(f32)).astype(bf16)
    return high.astype(f32), middle.astype(f32), low.astype(f32)


def column_sum(x):
    return jnp.sum(x, axis=0, keepdims=True)


def row_mean(x):
    return jnp.mean(x, axis=-1, keepdims=True)


def norm_parts(x):
    centered = x - row_mean(x)
    inverse = lax.rsqrt(row_mean(centered * centered) + 1e-05)
    return centered * inverse, inverse


def norm_pull(grad, unit, inverse, gain):
    scaled = grad * gain
    return inverse * (scaled - row_mean(scaled) - unit * row_mean(scaled * unit))


def onehot8(row):
    return (lax.broadcasted_iota(jnp.int32, (8, row.shape[1]), 0) == row.astype(jnp.int32)).astype(f32)


def id_matrix(rows, row):
    return (lax.broadcasted_iota(jnp.int32, (rows, row.shape[1]), 0) == row.astype(jnp.int32)).astype(f32).astype(bf16)


def params(**kw):
    return pltpu.CompilerParams(vmem_limit_bytes=60 * MIB, **kw)


def whole(shape):
    return pl.BlockSpec(shape, lambda *_: (0,) * len(shape))


def remote(src, dst, send, recv, peer):
    return pltpu.make_async_remote_copy(
        src_ref=src, dst_ref=dst, send_sem=send, recv_sem=recv, device_id=peer, device_id_type=MESH
    )


def greet(peers):
    barrier = pltpu.get_barrier_semaphore()
    for peer in peers:
        pl.semaphore_signal(barrier, inc=1, device_id=peer, device_id_type=MESH)


def met(peers):
    pl.semaphore_wait(pltpu.get_barrier_semaphore(), len(peers))


def gather_kernel(
    dp_n, blk_n, local_rows, ids_ref, seg_ref, steps_ref, noise_ref, table_ref, tok_ref, tab_ref, mine, own, send, recv
):
    dp = lax.axis_index("dp")
    z = lax.axis_index("blk")
    dp_peers = [(lax.rem(dp + k, dp_n), z) for k in range(1, dp_n)]
    z_peers = [(dp, lax.rem(z + k, blk_n)) for k in range(1, blk_n)]
    greet(z_peers + dp_peers)
    rows = ids_ref.shape[0]
    vp = own.shape[1]
    ids = ids_ref[...].reshape(1, rows).astype(f32)
    mine[...] = jnp.zeros_like(mine)
    mine[:16, :] = noise_ref[...]
    mine[16:17, :] = ids + (vp - local_rows) * jnp.floor((ids + 0.5) / local_rows)
    mine[17:18, :] = seg_ref[...].reshape(1, rows).astype(f32)
    mine[18:19, :] = steps_ref[...].reshape(1, rows).astype(f32)
    own[...] = jnp.zeros_like(own)
    own[:, :local_rows] = table_ref[...]
    met(z_peers + dp_peers)
    copies = []
    for k, peer in enumerate(z_peers):
        copies.append(remote(mine, tok_ref.at[z], send.at[k], recv.at[k], peer))
    for k, peer in enumerate(dp_peers):
        n = len(z_peers) + k
        copies.append(remote(own, tab_ref.at[dp], send.at[n], recv.at[n], peer))
    for c in copies:
        c.start()
    tok_ref[z] = mine[...]
    tab_ref[dp] = own[...]
    for c in copies:
        c.wait()


def gather(ids, segments, steps, noise, table, dp_n, blk_n):
    count = dp_n + blk_n - 2
    rows = ids.shape[0]
    local_rows = table.shape[1]
    vp = -(-local_rows // 128) * 128
    vmem = pl.BlockSpec(memory_space=VMEM)
    return pl.pallas_call(
        functools.partial(gather_kernel, dp_n, blk_n, local_rows),
        in_specs=[vmem] * 5,
        out_specs=[vmem, vmem],
        out_shape=[
            jax.ShapeDtypeStruct((blk_n, 24, rows), f32),
            jax.ShapeDtypeStruct((dp_n, 16, vp), f32),
        ],
        scratch_shapes=[
            VMEM((24, rows), f32),
            VMEM((16, vp), f32),
            pltpu.SemaphoreType.DMA((count,)),
            pltpu.SemaphoreType.DMA((count,)),
        ],
        compiler_params=params(collective_id=0, has_side_effects=True),
        name="gather",
    )(ids, segments, steps, noise, table)


class Scatter:
    def __init__(self, grad, columns, by_x, first, second, third, send, recv, chunks=None):
        self.grad, self.columns, self.by_x = grad, columns, by_x
        self.first, self.second, self.third = first, second, third
        self.send, self.recv, self.chunks = send, recv, chunks
        self.dp = lax.axis_index("dp")
        self.z = lax.axis_index("blk")
        self.core = lax.rem(self.dp, 2)
        self.x = lax.rem(lax.div(self.dp, 2), 2)
        self.y = lax.div(self.dp, 4)

    def flip(self, bit, step):
        return (self.dp + step * (1 - 2 * bit), self.z)

    def pair(self, y, x):
        if self.chunks is None:
            other = self.first[y, x]
        else:
            other = self.first[y, x, :, self.columns]
        return self.grad[y, x, self.core, :, self.columns].astype(f32) + other.astype(f32)

    def put(self, y, x, total):
        self.grad[y, x, self.core, :, self.columns] = total.astype(bf16)

    def core_copy(self):
        src = self.grad.at[:, :, 1 - self.core, :, self.columns]
        return remote(src, self.first, self.send.at[0], self.recv.at[0], self.flip(self.core, 1))

    def wide(self):
        if self.by_x:
            src, peer = self.grad.at[:, 1 - self.x, self.core, :, self.columns], self.flip(self.x, 2)
        else:
            src, peer = self.grad.at[1 - self.y, :, self.core, :, self.columns], self.flip(self.y, 4)
        return remote(src, self.second, self.send.at[1], self.recv.at[1], peer)

    def narrow(self):
        if self.by_x:
            src, peer = self.grad.at[1 - self.y, self.x, self.core, :, self.columns], self.flip(self.y, 4)
        else:
            src, peer = self.grad.at[self.y, 1 - self.x, self.core, :, self.columns], self.flip(self.x, 2)
        return remote(src, self.third, self.send.at[2], self.recv.at[2], peer)

    def start(self):
        self.core_copy().start()

    def core_to_wide(self):
        if self.chunks is None:
            self.core_copy().wait()
        elif self.by_x:
            for c in self.chunks:
                c().wait()
        def add(n, carry):
            y, x = (n, 1 - self.x) if self.by_x else (1 - self.y, n)
            self.put(y, x, self.pair(y, x))
            return carry

        lax.fori_loop(0, 2, add, 0)
        self.wide().start()

    def wide_to_narrow(self):
        self.wide().wait()
        y, x = (1 - self.y, self.x) if self.by_x else (self.y, 1 - self.x)
        self.put(y, x, self.pair(y, x) + self.second[y if self.by_x else x].astype(f32))
        self.narrow().start()

    def narrow_sum(self):
        self.narrow().wait()
        total = self.pair(self.y, self.x) + self.second[self.y if self.by_x else self.x].astype(f32)
        return (total + self.third[...].astype(f32)).astype(bf16)


def scatter_scratch(rows, columns, first=True):
    return ([VMEM((2, 2, rows, columns), bf16)] if first else []) + [
        VMEM((2, rows, columns), bf16),
        VMEM((rows, columns), bf16),
        pltpu.SemaphoreType.DMA((3,)),
        pltpu.SemaphoreType.DMA((3,)),
    ]


class LineScatter:
    def __init__(self, bases, out, half, first, rest, kept, second, send, recv):
        self.bases, self.out = bases, out
        self.half, self.first, self.rest, self.kept, self.second = half, first, rest, kept, second
        self.send, self.recv = send, recv
        self.dp, self.z = bases[0].dp, bases[0].z
        self.low = lax.rem(self.z, 2)
        self.high = lax.div(self.z, 2)

    def near(self):
        peer = (self.dp, self.z + 1 - 2 * self.low)
        return remote(self.half.at[1 - self.low], self.first, self.send.at[0], self.recv.at[0], peer)

    def far(self):
        peer = (self.dp, self.z + 2 - 4 * self.high)
        return remote(self.rest, self.second, self.send.at[1], self.recv.at[1], peer)

    def start(self):
        q = self.kept.shape[0] // 2
        totals = [base.narrow_sum() for base in self.bases]
        for low in range(2):
            for high in range(2):
                for n in range(2):
                    block = 2 * high + low
                    self.half[low, pl.ds((2 * high + n) * q, q), :] = totals[n][block * q : (block + 1) * q]
        self.near().start()

    def near_to_far(self):
        self.near().wait()
        size = self.kept.shape[0]
        mine = pl.ds(pl.multiple_of(self.high * size, size), size)
        other = pl.ds(pl.multiple_of((1 - self.high) * size, size), size)
        self.rest[...] = (self.half[self.low, other, :].astype(f32) + self.first[other, :].astype(f32)).astype(bf16)
        self.far().start()
        self.kept[...] = self.half[self.low, mine, :].astype(f32) + self.first[mine, :].astype(f32)

    def finish(self):
        self.far().wait()
        total = self.kept[...] + self.second[...].astype(f32)
        q = total.shape[0] // 2
        for n in range(2):
            self.out[:, self.bases[n].columns] = total[n * q : (n + 1) * q]


def line_scratch(rows, columns):
    return [
        VMEM((2, rows, columns), bf16),
        VMEM((rows, columns), bf16),
        VMEM((rows // 2, columns), bf16),
        VMEM((rows // 2, columns), f32),
        VMEM((rows // 2, columns), bf16),
        pltpu.SemaphoreType.DMA((2,)),
        pltpu.SemaphoreType.DMA((2,)),
    ]


def row(ref):
    return ref[...].reshape(1, ref.shape[0])


def own_columns(per, z, w_ref, qb_ref, vb_ref, own_w, own_b):
    start = z * (per * HEAD_DIM)
    base = pl.multiple_of(start // 128 * 128, 128)
    line = lax.broadcasted_iota(jnp.int32, (SLOT, SLOT), 0)
    lane = lax.broadcasted_iota(jnp.int32, (SLOT, SLOT), 1)
    move = ((line == lane + (start - base)) & (lane < per * HEAD_DIM)).astype(f32).astype(bf16)
    for n in range(3):
        part = w_ref[:, pl.ds(pl.multiple_of(n * D + base, 128), SLOT)]
        own_w[:, n * SLOT : (n + 1) * SLOT] = dot(part, move).astype(bf16)
    own_b[...] = jnp.zeros_like(own_b)
    for n, ref in ((0, qb_ref), (2, vb_ref)):
        part = jnp.concatenate(split3(jnp.broadcast_to(ref[pl.ds(base, SLOT)].reshape(1, SLOT), (8, SLOT))), axis=0)
        part = dot(part.astype(bf16), move)
        own_b[:, n * SLOT : (n + 1) * SLOT] = part[:8] + part[8:16] + part[16:]


def embed_kernel(local_rows, z_ref, tok_ref, tab_ref, up_w_ref, up_b_ref, gain_ref, shift_ref, qb_ref, vb_ref, w_ref,
                 own_w_ref, own_b_ref, *refs):
    embed_body(local_rows, z_ref, tok_ref, tab_ref, up_w_ref, up_b_ref, gain_ref, shift_ref, qb_ref, vb_ref, w_ref,
               own_b_ref, own_w_ref, 0, *refs)


def embed_body(
    local_rows,
    z_ref,
    tok_ref,
    tab_ref,
    up_w_ref,
    up_b_ref,
    gain_ref,
    shift_ref,
    qb_ref,
    vb_ref,
    w_ref,
    own_b_ref,
    own_w_ref,
    per,
    k_ref,
    vt_ref,
    own_ref,
    normed_ref,
    lhs_ref,
    sc_ref,
    qt_ref,
    h0_ref,
    rhs_ref,
    mean_ref,
    tab3,
    vcol,
):
    i = pl.program_id(0)
    dp_n, _, vp = tab_ref.shape
    blocks, _, rows = tok_ref.shape

    @pl.when(i == 0)
    def _():
        if per:
            own_columns(per, z_ref[0], w_ref, qb_ref, vb_ref, own_w_ref, own_b_ref)
        table = jnp.concatenate([tab_ref[j] for j in range(dp_n)], axis=1)
        squares = jnp.sum(table * table, axis=0, keepdims=True)
        lane = lax.broadcasted_iota(jnp.int32, squares.shape, 1)
        norms = jnp.where(lane % vp < local_rows, jnp.sqrt(squares + 1.0), 0.0)
        mean_ref[...] = jnp.broadcast_to(jnp.sum(norms, axis=1, keepdims=True) / (local_rows * dp_n), (8, 128))
        tab3[...] = jnp.concatenate(split3(table), axis=0).astype(bf16)
        segments = tok_ref[:, 17, :]
        steps = tok_ref[:, 18, :]
        sub = lax.broadcasted_iota(jnp.int32, (8, 1), 0)
        time = jnp.zeros((8, 1), f32)
        for s in range(DOCS):
            own = jnp.max(jnp.where(segments == float(s), steps, 0.0), axis=(0, 1), keepdims=True)
            time = jnp.where(sub == s, own, time)
        lane = lax.broadcasted_iota(jnp.int32, (8, D), 1)
        half = D // 2
        index = jnp.where(lane < half, lane, lane - half).astype(f32)
        angle = time * jnp.exp(index * (-math.log(10000.0) / half))
        wave = jnp.where(lane < half, jnp.sin(angle), jnp.cos(angle)) + row(up_b_ref)
        parts = split3(wave)
        rhs_ref[...] = jnp.concatenate([up_w_ref[...].astype(f32), *parts, jnp.zeros((8, D), f32)], axis=0).astype(bf16)
        bias = jnp.concatenate([row(qb_ref), row(vb_ref), jnp.zeros((6, D), f32)], axis=0)
        vcol[...] = jnp.transpose(bias)

    span = lhs_ref.shape[0]
    tok = jnp.concatenate([tok_ref[i * span + n] for n in range(span)], axis=1)
    ids = tok[16:17, :]
    picked3 = dot(tab3[...], id_matrix(dp_n * vp, ids))
    picked = picked3[:16] + picked3[16:32] + picked3[32:48]
    mean = mean_ref[0:1, 0:1]
    alpha_bar = 1.0 - jnp.sqrt(tok[18:19, :] / TSTEPS + 0.0001)
    signal = jnp.sqrt(alpha_bar)
    noise_scale = jnp.sqrt(1.0 - alpha_bar)
    mixed = signal * (picked / mean) + noise_scale * tok[:16]
    seg = onehot8(tok[17:18, :])
    lhs = jnp.concatenate([mixed, seg, seg, seg, jnp.zeros((8, span * rows), f32)], axis=0).astype(bf16)
    scales = jnp.concatenate([picked, signal, noise_scale, jnp.zeros((6, span * rows), f32)], axis=0)
    for n in range(span):
        lhs_ref[n] = lhs[:, n * rows : (n + 1) * rows]
        sc_ref[n] = scales[:, n * rows : (n + 1) * rows]
    hidden0 = dot(lhs, rhs_ref[...], TN)
    unit, _ = norm_parts(hidden0)
    normed = (unit * row(gain_ref) + row(shift_ref)).astype(bf16)
    normed_ref[...] = normed
    k_ref[...] = dot(normed, w_ref[:, D : 2 * D]).astype(bf16)
    vt_ref[...] = (dot(w_ref[:, 2 * D :], normed, TT) + vcol[:, 1:2]).astype(bf16)
    own = dot(normed, own_w_ref[...]) + own_b_ref[0:1, :]
    own_ref[:, :SLOT] = (own[:, :SLOT] * SCALE).astype(bf16)
    own_ref[:, SLOT:] = own[:, SLOT:].astype(bf16)

    for n in range(span):

        @pl.when(i * span + n == z_ref[0])
        def _():
            h0_ref[...] = hidden0[n * rows : (n + 1) * rows]

    @pl.when(i == lax.div(z_ref[0], span))
    def _():
        place = pl.ds(pl.multiple_of(lax.rem(z_ref[0], span) * rows, rows), rows)
        q = (dot(w_ref[:, :D], normed_ref[place, :], TT) + vcol[:, 0:1]).astype(bf16)
        qt_ref[...] = (q.astype(f32) * SCALE).astype(bf16)


def embed(z, tok, tab, up_w, vectors, w, local_rows, own_w, own_b):
    blocks, _, rows = tok.shape
    group = blocks * rows
    vocab = tab.shape[0] * tab.shape[2]
    operands = (tok, tab, up_w, *vectors, w, own_w, own_b)
    spec = pltpu.PrefetchScalarGridSpec(
        num_scalar_prefetch=1,
        grid=(blocks,),
        in_specs=[whole(x.shape) for x in operands],
        out_specs=[
            pl.BlockSpec((rows, D), lambda i, z: (i, 0)),
            pl.BlockSpec((D, rows), lambda i, z: (0, i)),
            pl.BlockSpec((rows, 3 * SLOT), lambda i, z: (i, 0)),
            pl.BlockSpec((rows, D), lambda i, z: (i, 0)),
            pl.BlockSpec((1, 48, rows), lambda i, z: (i, 0, 0)),
            pl.BlockSpec((1, 24, rows), lambda i, z: (i, 0, 0)),
            whole((D, rows)),
            whole((rows, D)),
            whole((48, D)),
            whole((8, 128)),
        ],
        scratch_shapes=[VMEM((48, vocab), bf16), VMEM((D, 8), f32)],
    )
    return pl.pallas_call(
        functools.partial(embed_kernel, local_rows),
        grid_spec=spec,
        out_shape=[
            jax.ShapeDtypeStruct((group, D), bf16),
            jax.ShapeDtypeStruct((D, group), bf16),
            jax.ShapeDtypeStruct((group, 3 * SLOT), bf16),
            jax.ShapeDtypeStruct((group, D), bf16),
            jax.ShapeDtypeStruct((blocks, 48, rows), bf16),
            jax.ShapeDtypeStruct((blocks, 24, rows), f32),
            jax.ShapeDtypeStruct((D, rows), bf16),
            jax.ShapeDtypeStruct((rows, D), f32),
            jax.ShapeDtypeStruct((48, D), bf16),
            jax.ShapeDtypeStruct((8, 128), f32),
        ],
        compiler_params=params(),
        name="embed",
    )(z, *operands)


ROOT = math.sqrt(2.0 / math.pi)


def attend(p, tok_ref, mine_ref, k_ref, vt_ref, qt_ref, att, lse, kext, qext):
    blocks, _, rows = tok_ref.shape

    @pl.when(p == 0)
    def _():
        for b in range(blocks):
            seg = jnp.concatenate([onehot8(tok_ref[b, 17:18, :]), jnp.zeros((120, rows), f32)], axis=0)
            kext[b * rows : (b + 1) * rows, :] = jnp.transpose(seg).astype(bf16)
        seg = onehot8(mine_ref[17:18, :])
        sub = lax.broadcasted_iota(jnp.int32, seg.shape, 0)
        barred = jnp.where(sub < DOCS, -BIG * (1.0 - seg), 0.0)
        qext[...] = jnp.concatenate([barred, jnp.zeros((120, rows), f32)], axis=0).astype(bf16)

    k = k_ref[...]
    keys = jnp.concatenate([k, kext[...]], axis=1)
    zeros = jnp.zeros((HEAD_DIM, rows), bf16)
    ones = jnp.ones((HEAD_DIM, blocks * rows), bf16)
    largest = jnp.max(jnp.abs(k), axis=0, keepdims=True).astype(f32)
    bound = jnp.max(dot(jnp.broadcast_to(largest, (8, PAIR)).astype(bf16), jnp.abs(qt_ref[...])))

    def heads(shifted):
        results = []
        for h in range(2):
            q = qt_ref[h * HEAD_DIM : (h + 1) * HEAD_DIM, :]
            v = vt_ref[h * HEAD_DIM : (h + 1) * HEAD_DIM, :]
            queries = jnp.concatenate([q, zeros, qext[...]] if h == 0 else [zeros, q, qext[...]], axis=0)
            scores = dot(keys, queries)
            if shifted:
                top = jnp.max(scores, axis=0, keepdims=True)
                scores = scores - top
            total = dot(jnp.concatenate([v, ones], axis=0), jnp.exp(scores).astype(bf16))
            results.append(total[:HEAD_DIM] / total[HEAD_DIM:])
            log_sum = jnp.log(total[HEAD_DIM : HEAD_DIM + 1])
            lse[pl.ds(2 * p + h, 1), :] = log_sum + top if shifted else log_sum
        att[pl.ds(pl.multiple_of(p * PAIR, PAIR), PAIR), :] = jnp.concatenate(results, axis=0)

    safe = bound < SAFE
    pl.when(safe)(lambda: heads(False))
    pl.when(jnp.logical_not(safe))(lambda: heads(True))


def front_kernel(
    local_rows,
    per,
    z_ref,
    tok_ref,
    tab_ref,
    up_w_ref,
    up_b_ref,
    gain_ref,
    shift_ref,
    qb_ref,
    vb_ref,
    w_ref,
    own_ref,
    normed_ref,
    lhs_ref,
    sc_ref,
    h0_ref,
    rhs_ref,
    mean_ref,
    own_w_ref,
    att,
    lse,
    keys,
    values,
    queries,
    tab3,
    vcol,
    own_b,
    kext,
    qext,
):
    i = pl.program_id(0)
    blocks, _, rows = tok_ref.shape

    span = lhs_ref.shape[0]
    steps = blocks // span

    @pl.when(i < steps)
    def _():
        place = pl.ds(pl.multiple_of(i * span * rows, rows), span * rows)
        embed_body(
            local_rows, z_ref, tok_ref, tab_ref, up_w_ref, up_b_ref, gain_ref, shift_ref, qb_ref, vb_ref, w_ref, own_b,
            own_w_ref, per, keys.at[place, :], values.at[:, place], own_ref, normed_ref, lhs_ref, sc_ref, queries,
            h0_ref, rhs_ref, mean_ref, tab3, vcol,
        )

    @pl.when(i >= steps)
    def _():
        p = i - steps
        pair = pl.ds(pl.multiple_of(p * PAIR, PAIR), PAIR)
        mine = tok_ref.at[z_ref[0]]
        attend(p, tok_ref, mine, keys.at[:, pair], values.at[pair, :], queries.at[pair, :], att, lse, kext, qext)


def front(z, tok, tab, up_w, vectors, w, local_rows, per):
    blocks, _, rows = tok.shape
    group = blocks * rows
    span = 2
    last = blocks // span - 1
    vocab = tab.shape[0] * tab.shape[2]
    operands = (tok, tab, up_w, *vectors, w)
    spec = pltpu.PrefetchScalarGridSpec(
        num_scalar_prefetch=1,
        grid=(last + 1 + HEADS // 2,),
        in_specs=[whole(x.shape) for x in operands],
        out_specs=[
            pl.BlockSpec((span * rows, 3 * SLOT), lambda i, z: (jnp.minimum(i, last), 0)),
            pl.BlockSpec((span * rows, D), lambda i, z: (jnp.minimum(i, last), 0)),
            pl.BlockSpec((span, 48, rows), lambda i, z: (jnp.minimum(i, last), 0, 0)),
            pl.BlockSpec((span, 24, rows), lambda i, z: (jnp.minimum(i, last), 0, 0)),
            whole((rows, D)),
            whole((48, D)),
            whole((8, 128)),
            whole((D, 3 * SLOT)),
            whole((D, rows)),
            whole((16, rows)),
        ],
        scratch_shapes=[
            VMEM((group, D), bf16),
            VMEM((D, group), bf16),
            VMEM((D, rows), bf16),
            VMEM((48, vocab), bf16),
            VMEM((D, 8), f32),
            VMEM((8, 3 * SLOT), f32),
            VMEM((group, PAIR), bf16),
            VMEM((PAIR, rows), bf16),
        ],
    )
    return pl.pallas_call(
        functools.partial(front_kernel, local_rows, per),
        grid_spec=spec,
        out_shape=[
            jax.ShapeDtypeStruct((group, 3 * SLOT), bf16),
            jax.ShapeDtypeStruct((group, D), bf16),
            jax.ShapeDtypeStruct((blocks, 48, rows), bf16),
            jax.ShapeDtypeStruct((blocks, 24, rows), f32),
            jax.ShapeDtypeStruct((rows, D), f32),
            jax.ShapeDtypeStruct((48, D), bf16),
            jax.ShapeDtypeStruct((8, 128), f32),
            jax.ShapeDtypeStruct((D, 3 * SLOT), bf16),
            jax.ShapeDtypeStruct((D, rows), f32),
            jax.ShapeDtypeStruct((16, rows), f32),
        ],
        compiler_params=params(),
        name="front",
    )(z, *operands)


def gelu_parts(x):
    square = x * x
    t = jnp.tanh(x * (ROOT + (ROOT * 0.044715) * square))
    half = 0.5 + 0.5 * t
    active = x * half
    slope = half + active * (1.0 - t) * (ROOT + (3.0 * ROOT * 0.044715) * square)
    return active.astype(bf16), slope


def layer_kernel(
    per,
    tok_ref,
    mine_ref,
    k_ref,
    vt_ref,
    qt_ref,
    h0_ref,
    cot_ref,
    vec_ref,
    b1_ref,
    wo_ref,
    w1_ref,
    w2_ref,
    out_ref,
    h1g_ref,
    msg_ref,
    dwo_ref,
    dw1_ref,
    dw2_ref,
    small_ref,
    kext,
    qext,
    att,
    lse,
    wo,
    wo_slots,
    w1,
    w2,
    sems,
):
    p = pl.program_id(0)
    last = pl.num_programs(0) - 1
    blocks, _, rows = tok_ref.shape
    copies = [
        pltpu.make_async_copy(wo_ref, wo, sems.at[0]),
        pltpu.make_async_copy(w1_ref, w1, sems.at[1]),
        pltpu.make_async_copy(w2_ref, w2, sems.at[2]),
    ]

    @pl.when(p == 0)
    def _():
        for c in copies:
            c.start()

    attend(p, tok_ref, mine_ref, k_ref, vt_ref, qt_ref, att, lse, kext, qext)

    @pl.when(p == last)
    def _():
        for c in copies:
            c.wait()
        attended = att[...].astype(bf16)
        hidden1 = h0_ref[...] + dot(attended, wo[...], TN) + vec_ref[0:1, :]
        unit, inverse = norm_parts(hidden1)
        normed2 = (unit * vec_ref[1:2, :] + vec_ref[2:3, :]).astype(bf16)
        cot = cot_ref[...]
        out_grad = cot.astype(bf16)
        block_out = hidden1 + vec_ref[3:4, :]
        norm_grad = jnp.zeros_like(hidden1)
        inner_sums = []
        for c in range(FF // D):
            cols = slice(c * D, (c + 1) * D)
            x = dot(normed2, w1[:, cols]) + b1_ref[c : c + 1, :]
            active, slope = gelu_parts(x)
            block_out = block_out + dot(active, w2[cols, :])
            inner_grad = (dot(out_grad, w2[cols, :], NT) * slope).astype(bf16)
            dw2_ref[cols, :] = dot(active, out_grad, TN).astype(bf16)
            dw1_ref[:, cols] = dot(normed2, inner_grad, TN).astype(bf16)
            norm_grad = norm_grad + dot(inner_grad, w1[:, cols], NT)
            inner_sums.append(column_sum(inner_grad.astype(f32)))
        out_ref[...] = block_out
        hidden1_grad = cot + norm_pull(norm_grad, unit, inverse, vec_ref[1:2, :])
        h1g_ref[...] = hidden1_grad
        branch = hidden1_grad.astype(bf16)
        dwo_ref[...] = dot(attended, branch).astype(bf16)
        small_ref[...] = jnp.concatenate(
            [
                column_sum(branch.astype(f32)),
                column_sum(norm_grad * unit),
                column_sum(norm_grad),
                column_sum(out_grad.astype(f32)),
                *inner_sums,
            ],
            axis=0,
        )
        seg = onehot8(mine_ref[17:18, :])
        back = dot(wo[...], branch, NT).astype(bf16).astype(f32)
        product = back * att[...]
        for j in range(blocks):
            heads = [h for h in range(per * j, per * (j + 1)) if h < HEADS]
            wo_slots[...] = jnp.zeros_like(wo_slots)
            size = len(heads) * HEAD_DIM
            rows_ext = [jnp.zeros((HEAD_DIM, rows), f32), jnp.where(
                lax.broadcasted_iota(jnp.int32, (8, rows), 0) < DOCS, -BIG * (1.0 - seg), 0.0
            )[:DOCS]]
            lse_parts = []
            delta_parts = []
            for n in range(3):
                h = per * j + n
                if n < per and h < HEADS:
                    delta = column_sum(product[h * HEAD_DIM : (h + 1) * HEAD_DIM])
                    lse_parts += split3(-lse[h : h + 1, :])
                    delta_parts += split3(-delta)
                else:
                    lse_parts += [jnp.zeros((1, rows), f32)] * 3
                    delta_parts += [jnp.zeros((1, rows), f32)] * 3
            used = DOCS + 18
            rows_ext = rows_ext + lse_parts + delta_parts + [jnp.zeros((HEAD_DIM - used, rows), f32)]
            ext = jnp.transpose(jnp.concatenate(rows_ext, axis=0))
            if size:
                wo_slots[:size, :] = wo[heads[0] * HEAD_DIM : heads[0] * HEAD_DIM + size, :]
            grads = dot(branch, wo_slots[...], NT)
            msg_ref[j, :, :PAIR] = grads[:, :PAIR].astype(bf16)
            msg_ref[j, :, PAIR:] = (grads[:, PAIR:] + ext).astype(bf16)


def layer(tok, mine, k, vt, qt, h0, cot, vec, b1, wo, w1, w2, per):
    blocks, _, rows = tok.shape
    group = blocks * rows
    any_spec = pl.BlockSpec(memory_space=pl.ANY)
    return pl.pallas_call(
        functools.partial(layer_kernel, per),
        grid=(HEADS // 2,),
        in_specs=[
            whole(tok.shape),
            whole(mine.shape),
            pl.BlockSpec((group, PAIR), lambda p: (0, p)),
            pl.BlockSpec((PAIR, group), lambda p: (p, 0)),
            pl.BlockSpec((PAIR, rows), lambda p: (p, 0)),
            whole(h0.shape),
            whole(cot.shape),
            whole(vec.shape),
            whole(b1.shape),
            any_spec,
            any_spec,
            any_spec,
        ],
        out_specs=[
            whole((rows, D)),
            whole((rows, D)),
            whole((blocks, rows, SLOT)),
            whole((D, D)),
            whole((D, FF)),
            whole((FF, D)),
            whole((8, D)),
        ],
        out_shape=[
            jax.ShapeDtypeStruct((rows, D), f32),
            jax.ShapeDtypeStruct((rows, D), f32),
            jax.ShapeDtypeStruct((blocks, rows, SLOT), bf16),
            jax.ShapeDtypeStruct((D, D), bf16),
            jax.ShapeDtypeStruct((D, FF), bf16),
            jax.ShapeDtypeStruct((FF, D), bf16),
            jax.ShapeDtypeStruct((8, D), f32),
        ],
        scratch_shapes=[
            VMEM((group, PAIR), bf16),
            VMEM((PAIR, rows), bf16),
            VMEM((D, rows), f32),
            VMEM((16, rows), f32),
            VMEM((D, D), bf16),
            VMEM((SLOT, D), bf16),
            VMEM((D, FF), bf16),
            VMEM((FF, D), bf16),
            pltpu.SemaphoreType.DMA((3,)),
        ],
        compiler_params=params(),
        name="layer",
    )(tok, mine, k, vt, qt, h0, cot, vec, b1, wo, w1, w2)


def back_prepare(tok_ref, own_ref, kt, vt):
    blocks, _, rows = tok_ref.shape
    for b in range(blocks):
        place = slice(b * rows, (b + 1) * rows)
        seg = onehot8(tok_ref[b, 17:18, :])
        seg = jnp.concatenate([seg, jnp.zeros((HEAD_DIM - 8, rows), f32)], axis=0)
        sub = lax.broadcasted_iota(jnp.int32, seg.shape, 0)
        k_ext = jnp.where((sub >= DOCS) & (sub < DOCS + 9), 1.0, jnp.where(sub < DOCS, seg, 0.0))
        v_ext = jnp.where((sub >= DOCS + 9) & (sub < DOCS + 18), 1.0, 0.0)
        kt_b = jnp.transpose(own_ref[place, SLOT : 2 * SLOT].astype(f32))
        vt_b = jnp.transpose(own_ref[place, 2 * SLOT :].astype(f32))
        kt[:, place] = jnp.concatenate([kt_b[:EXT], k_ext], axis=0).astype(bf16)
        vt[:, place] = jnp.concatenate([vt_b[:EXT], v_ext], axis=0).astype(bf16)


def back_block(per, q, msg, keys, kt, vt, dkt, dvt):
    lane = lax.broadcasted_iota(jnp.int32, q.shape, 1)
    m = msg.astype(f32)
    queries = jnp.where(lane < EXT, q.astype(f32), m)
    q_t = jnp.transpose(q.astype(f32)).astype(bf16)
    m_t = jnp.transpose(m).astype(bf16)
    dq = jnp.zeros(q.shape, f32)

    def products(h):
        mine = (lane >= h * HEAD_DIM) & (lane < (h + 1) * HEAD_DIM)
        low = EXT + DOCS + 3 * h
        barred = (lane >= EXT) & (lane < EXT + DOCS)
        use_q = mine | barred | ((lane >= low) & (lane < low + 3))
        use_m = mine | ((lane >= low + 9) & (lane < low + 12))
        scores = dot(jnp.where(use_q, queries, 0.0).astype(bf16), kt[...])
        return mine, scores, dot(jnp.where(use_m, m, 0.0).astype(bf16), vt[...])

    coming = products(0)
    for h in range(per):
        mine, scores, prob_grad = coming
        if h + 1 < per:
            coming = products(h + 1)
        head = slice(h * HEAD_DIM, (h + 1) * HEAD_DIM)
        probs = jnp.exp(scores)
        score_grad = (probs * prob_grad).astype(bf16)
        dvt[head, :] += dot(m_t[head], probs.astype(bf16))
        dkt[head, :] += dot(q_t[head], score_grad)
        dq = dq + jnp.where(mine, dot(score_grad, keys), 0.0)
    return (dq * SCALE).astype(bf16)


def back_kernel(per, tok_ref, own_ref, msg_ref, grad_ref, kt, vt, dkt, dvt):
    blocks, _, rows = tok_ref.shape
    back_prepare(tok_ref, own_ref, kt, vt)
    dkt[...] = jnp.zeros_like(dkt)
    dvt[...] = jnp.zeros_like(dvt)

    def step(b, carry):
        place = pl.ds(pl.multiple_of(b * rows, rows), rows)
        keys = own_ref[:, SLOT : 2 * SLOT]
        grad_ref[place, :SLOT] = back_block(per, own_ref[place, :SLOT], msg_ref[b], keys, kt, vt, dkt, dvt)
        return carry

    lax.fori_loop(0, blocks, step, 0)
    for b in range(blocks):
        place = slice(b * rows, (b + 1) * rows)
        grad_ref[place, SLOT : 2 * SLOT] = jnp.transpose(dkt[:, place]).astype(bf16)
        grad_ref[place, 2 * SLOT :] = jnp.transpose(dvt[:, place]).astype(bf16)


def back(tok, own, msg, per):
    group = own.shape[0]
    return pl.pallas_call(
        functools.partial(back_kernel, per),
        in_specs=[pl.BlockSpec(memory_space=VMEM)] * 3,
        out_specs=pl.BlockSpec(memory_space=VMEM),
        out_shape=jax.ShapeDtypeStruct(own.shape, bf16),
        scratch_shapes=[
            VMEM((SLOT, group), bf16),
            VMEM((SLOT, group), bf16),
            VMEM((SLOT, group), f32),
            VMEM((SLOT, group), f32),
        ],
        compiler_params=params(),
        name="attention_back",
    )(tok, own, msg)

def final_kernel(
    z_ref, tok_ref, grad_ref, normed_ref, lhs_ref, sc_ref, rhs_ref, h1g_ref, up_w_ref, vec_ref, own_w_ref, mean_ref,
    dw_ref, noise_ref, table_ref, small_ref, acc,
):
    i = pl.program_id(0)
    last = pl.num_programs(0) - 1
    vocab = table_ref.shape[1]
    mean = mean_ref[0:1, 0:1]

    @pl.when(i == 0)
    def _():
        acc[...] = jnp.zeros_like(acc)
        small_ref[...] = jnp.zeros_like(small_ref)
        table_ref[...] = jnp.zeros_like(table_ref)

    grad = grad_ref[...]
    hidden0 = dot(lhs_ref[0], rhs_ref[...], TN)
    unit, inverse = norm_parts(hidden0)
    norm_grad = dot(grad, own_w_ref[...], NT)
    acc[...] += dot(normed_ref[...], grad, TN)
    own = (z_ref[0] == i).astype(f32)
    h0_grad = (norm_pull(norm_grad, unit, inverse, vec_ref[1:2, :]) + own * h1g_ref[...]).astype(bf16)
    mixed_grad = dot(up_w_ref[...], h0_grad, NT)
    sc = sc_ref[0]
    noise_ref[0] = sc[17:18] * mixed_grad
    embedded_grad = sc[16:17] * mixed_grad
    picked = sc[:16]
    norm_term = -jnp.sum(embedded_grad * picked, axis=(0, 1), keepdims=True) / (mean * mean)
    ids = tok_ref[i][16:17, :]
    table3 = dot(jnp.concatenate(split3(embedded_grad / mean), axis=0).astype(bf16), id_matrix(vocab, ids), NT)
    table_ref[...] += table3[:16] + table3[16:32] + table3[32:48]
    gradf = grad.astype(f32)
    small_ref[...] += jnp.concatenate(
        [
            dot(lhs_ref[0, :16, :], h0_grad),
            column_sum(h0_grad.astype(f32)),
            column_sum(norm_grad * unit),
            column_sum(norm_grad),
            column_sum(gradf),
            jnp.broadcast_to(norm_term, (1, D)),
            jnp.zeros((3, D), f32),
        ],
        axis=0,
    )

    @pl.when(i == last)
    def _():
        dw_ref[...] = acc[...].astype(bf16)


def final(z, tok, grad, normed, lhs, sc, rhs, h1g, up_w, vec, own_w, mean, vocab):
    blocks, _, rows = tok.shape
    spec = pltpu.PrefetchScalarGridSpec(
        num_scalar_prefetch=1,
        grid=(blocks,),
        in_specs=[
            whole(tok.shape),
            pl.BlockSpec((rows, 3 * SLOT), lambda i, z: (i, 0)),
            pl.BlockSpec((rows, D), lambda i, z: (i, 0)),
            pl.BlockSpec((1, 48, rows), lambda i, z: (i, 0, 0)),
            pl.BlockSpec((1, 24, rows), lambda i, z: (i, 0, 0)),
            whole(rhs.shape),
            whole(h1g.shape),
            whole(up_w.shape),
            whole(vec.shape),
            whole(own_w.shape),
            whole(mean.shape),
        ],
        out_specs=[
            whole((D, 3 * SLOT)),
            pl.BlockSpec((1, 16, rows), lambda i, z: (i, 0, 0)),
            whole((16, vocab)),
            whole((24, D)),
        ],
        scratch_shapes=[VMEM((D, 3 * SLOT), f32)],
    )
    return pl.pallas_call(
        final_kernel,
        grid_spec=spec,
        out_shape=[
            jax.ShapeDtypeStruct((D, 3 * SLOT), bf16),
            jax.ShapeDtypeStruct((blocks, 16, rows), f32),
            jax.ShapeDtypeStruct((16, vocab), f32),
            jax.ShapeDtypeStruct((24, D), f32),
        ],
        compiler_params=params(),
        name="embed_back",
    )(z, tok, grad, normed, lhs, sc, rhs, h1g, up_w, vec, own_w, mean)


UNITS = (
    (1, 0, 768, True),
    (1, 768, 768, False),
    (1, 1536, 768, True),
    (1, 2304, 768, False),
    (0, 0, 384, True),
    (0, 384, 384, False),
    (2, 0, 384, True),
    (2, 384, 384, False),
    (3, 0, 384, True),
    (3, 384, 384, False),
)
UNIT_ROWS = (384, 96, 96, 96)
CORE, WIDE, NARROW, NEAR, FAR, DONE = range(6)
PLAN = {
    "chunk0": [(CORE, 0)],
    "chunk1": [(CORE, 1), (WIDE, 0)],
    "chunk2": [(CORE, 2), (WIDE, 1)],
    "chunk3": [(CORE, 3), (WIDE, 2)],
    "sent": [(CORE, 6), (CORE, 7), (WIDE, 3), (NARROW, 0), (WIDE, 4), (WIDE, 5)],
    "prep": [(WIDE, 6), (WIDE, 7), (NARROW, 1)],
    "q0": [],
    "q1": [(NARROW, 2), (NARROW, 3)],
    "q2": [(NARROW, 4), (NARROW, 6)],
    "q3": [(NARROW, 5), (NARROW, 7), (NEAR, 0)],
    "kv": [(NEAR, 1), (FAR, 0)],
    "dw": [(CORE, 8), (CORE, 9), (NEAR, 2), (NEAR, 3)],
    "e0": [(WIDE, 8), (WIDE, 9), (FAR, 1)],
    "e1": [(FAR, 2), (FAR, 3)],
    "e2": [(NARROW, 8), (NARROW, 9)],
    "e3": [(DONE, 0), (DONE, 1)],
    "end": [(DONE, 2), (DONE, 3)],
}


def mega_kernel(
    per,
    plan,
    tok_ref,
    lse_ref,
    gain1_ref,
    out_b_ref,
    gain2_ref,
    shift2_ref,
    outer_b_ref,
    b1_ref,
    lhs_ref,
    sc_ref,
    rhs_ref,
    mean_ref,
    up_w_ref,
    att_hbm,
    h0_hbm,
    cot_hbm,
    wo_hbm,
    w1_hbm,
    w2_hbm,
    own_hbm,
    normed_hbm,
    own_w_hbm,
    out_hbm,
    dwo_out,
    dw1_out,
    dw2_out,
    dw_out,
    small_out,
    table_out,
    noise_out,
    dw2,
    dw1,
    dwo,
    dwq,
    h1g,
    msg_out,
    msgs,
    small1,
    msg_send,
    msg_recv,
    first2,
    chunk_send,
    chunk_recv,
    send_parts,
    parts,
    mine,
    lines,
    sums,
    dw_parts,
    noise_mine,
    noise_parts,
    sends,
    recvs,
    *scratch,
):
    blocks, _, rows = tok_ref.shape
    dp = lax.axis_index("dp")
    z = lax.axis_index("blk")
    dp_n, blk_n = parts.shape[0], lines.shape[0]
    group = blocks * rows
    half = D // 2
    nd, nz = dp_n - 1, blk_n - 1
    grads = (dw2, dw1, dwo, dwq)
    outs = (dw2_out, dw1_out, dwo_out)
    scratch = list(scratch)
    units = []
    lines_of = []
    core, x, y = lax.rem(dp, 2), lax.rem(lax.div(dp, 2), 2), lax.div(dp, 4)
    sibling = (dp + 1 - 2 * core, z)

    def chunk_copy(c):
        at = (c // 2, c % 2)
        return remote(dw2.at[at + (1 - core,)], first2.at[at], chunk_send.at[c], chunk_recv.at[c], sibling)

    for which, first, size, by_x in UNITS:
        buffer = first2 if which == 0 else scratch.pop(0)
        rest = [scratch.pop(0) for _ in range(4)]
        chunks = [functools.partial(chunk_copy, c) for c in range(4)] if which == 0 else None
        units.append(Scatter(grads[which], pl.ds(first, size), by_x, buffer, *rest, chunks=chunks))
        if which != 3 and not by_x:
            lines_of.append(LineScatter(units[-2:], outs[which], *[scratch.pop(0) for _ in range(7)]))

    def run(slot):
        for kind, n in plan[slot]:
            if kind == CORE:
                units[n].start()
            elif kind == WIDE:
                units[n].core_to_wide()
            elif kind == NARROW:
                units[n].wide_to_narrow()
            elif kind == NEAR:
                lines_of[n].start()
            elif kind == FAR:
                lines_of[n].near_to_far()
            else:
                lines_of[n].finish()

    def z_peer(k):
        low, high = lax.rem(z, 2), lax.div(z, 2)
        return (low + (k % 2) * (1 - 2 * low)) + 2 * (high + (k // 2) * (1 - 2 * high))

    def message(k):
        return remote(msg_out.at[z_peer(k)], msgs.at[k], msg_send.at[k], msg_recv.at[k], (dp, z_peer(k)))

    dp_to = [(lax.rem(dp + k, dp_n), z) for k in range(1, dp_n)]
    z_to = [(dp, lax.rem(z + k, blk_n)) for k in range(1, blk_n)]

    greet(dp_to + z_to)

    def dense(att_v, h0_v, cot_v, wo, w1, w2, wo_slots, sems):
        pairs = [(wo_hbm, wo), (att_hbm, att_v), (h0_hbm, h0_v), (cot_hbm, cot_v)]
        for c in range(FF // D):
            part = pl.ds(c * D, D)
            pairs += [(w1_hbm.at[:, part], w1.at[:, part]), (w2_hbm.at[part], w2.at[part])]
        moves = [pltpu.make_async_copy(src, dst, sems.at[n]) for n, (src, dst) in enumerate(pairs)]
        for c in moves:
            c.start()
        for c in moves[:3]:
            c.wait()
        attended = att_v[...].astype(bf16)
        hidden1 = h0_v[...] + dot(attended, wo[...], TN) + row(out_b_ref)
        unit, inverse = norm_parts(hidden1)
        normed2 = (unit * row(gain2_ref) + row(shift2_ref)).astype(bf16)
        moves[3].wait()
        cot = cot_v[...]
        out_grad = cot.astype(bf16)
        h0_v[...] = hidden1 + row(outer_b_ref)
        h1g[...] = jnp.zeros_like(h1g)
        inner_sums = []
        for c in range(FF // D):
            cols = slice(c * D, (c + 1) * D)
            moves[4 + 2 * c].wait()
            moves[5 + 2 * c].wait()
            active, slope = gelu_parts(dot(normed2, w1[:, cols]) + b1_ref[pl.ds(c * D, D)].reshape(1, D))
            h0_v[...] += dot(active, w2[cols, :])
            inner_grad = (dot(out_grad, w2[cols, :], NT) * slope).astype(bf16)
            if c == 0:
                met(dp_to + z_to)
            part = dot(active, out_grad, TN).astype(bf16)
            dw2[c // 2, c % 2, 0] = part[: D // 2]
            dw2[c // 2, c % 2, 1] = part[D // 2 :]
            chunk_copy(c).start()
            part = dot(normed2, inner_grad, TN).astype(bf16)
            for k in range(8):
                dw1[k // 4, k // 2 % 2, k % 2, :, cols] = part[k * 96 : (k + 1) * 96]
            h1g[...] += dot(inner_grad, w1[:, cols], NT)
            inner_sums.append(column_sum(inner_grad.astype(f32)))
            run(("chunk0", "chunk1", "chunk2", "chunk3")[c])
        norm_grad = h1g[...]
        write = pltpu.make_async_copy(h0_v, out_hbm, sems.at[0])
        write.start()
        hidden1_grad = cot + norm_pull(norm_grad, unit, inverse, row(gain2_ref))
        h1g[...] = hidden1_grad
        branch = hidden1_grad.astype(bf16)
        seg = onehot8(tok_ref[z, 17:18, :])
        sub = lax.broadcasted_iota(jnp.int32, (8, rows), 0)
        barred = jnp.where(sub < DOCS, -BIG * (1.0 - seg), 0.0)[:DOCS]
        product = dot(wo[...], branch, NT).astype(bf16).astype(f32) * att_v[...]
        wo_slots[...] = jnp.zeros_like(wo_slots)
        size = per * HEAD_DIM
        exts = []
        for j in range(blocks):
            lse_parts = []
            delta_parts = []
            for h in range(per * j, per * (j + 1)):
                delta = column_sum(product[h * HEAD_DIM : (h + 1) * HEAD_DIM])
                lse_parts += split3(-lse_ref[h : h + 1, :])
                delta_parts += split3(-delta)
            rest = jnp.zeros((HEAD_DIM - DOCS - 6 * per, rows), f32)
            ext = [jnp.zeros((HEAD_DIM, rows), f32), barred] + lse_parts + delta_parts + [rest]
            ext = jnp.transpose(jnp.concatenate(ext, axis=0))
            exts.append(ext)
            wo_slots[j * SLOT : j * SLOT + size, :] = wo[j * size : (j + 1) * size, :]
        branch_grads = dot(branch, wo_slots[...], NT)
        for j in range(blocks):
            part = branch_grads[:, j * SLOT : (j + 1) * SLOT]
            msg_out[j, :, :PAIR] = part[:, :PAIR].astype(bf16)
            msg_out[j, :, PAIR:] = (part[:, PAIR:] + exts[j]).astype(bf16)
        message(1).start()
        message(2).start()
        part = dot(attended, branch).astype(bf16)
        for k in range(8):
            dwo[k // 4, k // 2 % 2, k % 2] = part[k * 96 : (k + 1) * 96]
        small1[...] = jnp.concatenate(
            [
                column_sum(branch.astype(f32)),
                column_sum(norm_grad * unit),
                column_sum(norm_grad),
                column_sum(out_grad.astype(f32)),
                *inner_sums,
            ],
            axis=0,
        )
        run("sent")
        write.wait()

    pl.run_scoped(
        dense,
        VMEM((D, rows), f32),
        VMEM((rows, D), f32),
        VMEM((rows, D), f32),
        VMEM((D, D), bf16),
        VMEM((D, FF), bf16),
        VMEM((FF, D), bf16),
        VMEM((blocks * SLOT, D), bf16),
        pltpu.SemaphoreType.DMA((12,)),
    )

    def backward(grad, own, kt, vt, dkt, dvt, sem):
        load = pltpu.make_async_copy(own_hbm, own, sem)
        load.start()
        dkt[...] = jnp.zeros_like(dkt)
        dvt[...] = jnp.zeros_like(dvt)
        msgs[0] = msg_out[z]
        load.wait()
        back_prepare(tok_ref, own, kt, vt)
        run("prep")

        def body(b, carry):
            low, high = lax.rem(z, 2), lax.div(z, 2)
            b_low, b_high = lax.rem(b, 2), lax.div(b, 2)
            other = (low + b_low * (1 - 2 * low)) + 2 * (high + b_high * (1 - 2 * high))
            for k in range(blocks):
                if k or plan["q0"]:

                    @pl.when(b == k)
                    def _():
                        if k == 1:
                            message(3).start()
                        if k:
                            message(k).wait()
                        run(("q0", "q1", "q2", "q3")[k])

            place = pl.ds(pl.multiple_of(other * rows, rows), rows)
            keys = own[:, SLOT : 2 * SLOT]
            grad[place, :SLOT] = back_block(per, own[place, :SLOT], msgs[b], keys, kt, vt, dkt, dvt)
            return carry

        lax.fori_loop(0, blocks, body, 0)
        for b in range(blocks):
            place = slice(b * rows, (b + 1) * rows)
            grad[place, SLOT : 2 * SLOT] = jnp.transpose(dkt[:, place]).astype(bf16)
            grad[place, 2 * SLOT :] = jnp.transpose(dvt[:, place]).astype(bf16)

    def noise_copy(i):
        k = lax.rem(i - z + blk_n, blk_n) - 1
        k = jnp.maximum(k, 0)
        n = 2 * nd + nz + k
        return remote(noise_mine.at[i], noise_parts.at[z], sends.at[n], recvs.at[n], (dp, i))

    def embedding(grad, normed, own_w, sems):
        loads = [
            pltpu.make_async_copy(normed_hbm, normed, sems.at[0]),
            pltpu.make_async_copy(own_w_hbm, own_w, sems.at[1]),
        ]
        for c in loads:
            c.start()
        run("kv")
        for c in loads:
            c.wait()
        part = dot(normed[...], grad[...], TN).astype(bf16)
        for k in range(8):
            dwq[k // 4, k // 2 % 2, k % 2] = part[k * 96 : (k + 1) * 96]
        run("dw")
        mean = mean_ref[0:1, 0:1]
        small2 = jnp.zeros((24, D), f32)
        vocab = dp_n * 128
        table = jnp.zeros((16, vocab), f32)
        for first in range(0, blocks, 2):
            two = (first, first + 1)
            g = grad[first * rows : (first + 2) * rows, :]
            lhs = jnp.concatenate([lhs_ref[i] for i in two], axis=1)
            hidden0 = dot(lhs, rhs_ref[...], TN)
            unit, inverse = norm_parts(hidden0)
            norm_grad = dot(g, own_w[...], NT)
            later = jnp.concatenate([(z == i).astype(f32) * h1g[...] for i in two], axis=0)
            h0_grad = (norm_pull(norm_grad, unit, inverse, row(gain1_ref)) + later).astype(bf16)
            run(("e0", "e2")[first // 2])
            mixed_grad = dot(up_w_ref[...], h0_grad, NT)
            sc = jnp.concatenate([sc_ref[i] for i in two], axis=1)
            for n, i in enumerate(two):
                noise_mine[i] = (sc[17:18] * mixed_grad)[:, n * rows : (n + 1) * rows].astype(bf16)
                pl.when(z != i)(noise_copy(i).start)
            embedded_grad = sc[16:17] * mixed_grad
            norm_term = -jnp.sum(embedded_grad * sc[:16], axis=(0, 1), keepdims=True) / (mean * mean)
            table3 = dot(
                jnp.concatenate(split3(embedded_grad / mean), axis=0).astype(bf16),
                id_matrix(vocab, jnp.concatenate([tok_ref[i][16:17, :] for i in two], axis=1)),
                NT,
            )
            table = table + (table3[:16] + table3[16:32] + table3[32:48])
            small2 = small2 + jnp.concatenate(
                [
                    dot(lhs[:16, :], h0_grad),
                    column_sum(h0_grad.astype(f32)),
                    column_sum(norm_grad * unit),
                    column_sum(norm_grad),
                    jnp.broadcast_to(norm_term, (1, D)),
                    *[(z == j).astype(f32) * column_sum(g.astype(f32)) for j in range(blocks)],
                ],
                axis=0,
            )
            run(("e1", "e3")[first // 2])
        flat = jnp.concatenate([small1[...], small2], axis=0)
        for k in range(dp_n):
            n = k % 4
            send_parts[k, :, :half] = flat[8 * n : 8 * n + 8, (k // 4) * half : (k // 4 + 1) * half]
            send_parts[k, :, half : half + 128] = table[:8, k * 128 : (k + 1) * 128]
            send_parts[k, :, half + 128 :] = table[8:, k * 128 : (k + 1) * 128]

    def rest(grad):
        pl.run_scoped(
            functools.partial(backward, grad),
            VMEM((group, 3 * SLOT), bf16),
            VMEM((SLOT, group), bf16),
            VMEM((SLOT, group), bf16),
            VMEM((SLOT, group), f32),
            VMEM((SLOT, group), f32),
            pltpu.SemaphoreType.DMA,
        )
        pl.run_scoped(
            functools.partial(embedding, grad),
            VMEM((group, D), bf16),
            VMEM((D, 3 * SLOT), bf16),
            pltpu.SemaphoreType.DMA((2,)),
        )

    pl.run_scoped(rest, VMEM((group, 3 * SLOT), bf16))

    def spread(src, dst, peers, first):
        return [remote(src(p), dst, sends.at[first + k], recvs.at[first + k], p) for k, p in enumerate(peers)]

    one = spread(lambda p: send_parts.at[p[0]], parts.at[dp], dp_to, 0)
    four = spread(lambda p: noise_mine.at[p[1]], noise_parts.at[z], z_to, 2 * nd + nz)
    for c in one:
        c.start()
    parts[dp] = send_parts[dp]
    noise_parts[z] = noise_mine[z]
    dw_parts[...] = jnp.zeros_like(dw_parts)
    for u in units[8:]:
        total = u.narrow_sum()
        q = total.shape[0] // blk_n
        for k in range(blk_n):
            dw_parts[k, :q, u.columns] = total[k * q : (k + 1) * q]
    five = spread(lambda p: dw_parts.at[p[1]], dw_out.at[z], z_to, 2 * nd + 2 * nz)
    for c in five:
        c.start()
    dw_out[z] = dw_parts[z]
    for c in one:
        c.wait()
    total = parts[0]
    for k in range(1, dp_n):
        total = total + parts[k]
    mine[...] = total
    lines[z] = total
    two = spread(lambda p: mine, lines.at[z], z_to, nd)
    for c in two:
        c.start()
    for c in four:
        c.wait()
    total = noise_parts[0].astype(f32)
    for k in range(1, blk_n):
        total = total + noise_parts[k].astype(f32)
    noise_out[...] = total
    for c in two:
        c.wait()
    total = lines[0]
    for k in range(1, blk_n):
        total = total + lines[k]
    table_out[...] = total[:, half:]
    sums[...] = total[:, :half]
    small_out[dp] = total[:, :half]
    three = spread(lambda p: sums, small_out.at[dp], dp_to, nd + nz)
    for c in three:
        c.start()
    run("end")
    for c in three + five:
        c.wait()


def mega(small, big, dp_n, per):
    tok, att, lse, h0, cot, vectors, lhs, sc, rhs, mean, up_w = small
    blk_n, _, rows = tok.shape
    group = blk_n * rows
    share = D // (dp_n * blk_n)
    vmem = pl.BlockSpec(memory_space=VMEM)
    hbm = pl.BlockSpec(memory_space=pl.ANY)
    count = 2 * (dp_n - 1) + 3 * (blk_n - 1)
    half = D // 2
    scratch = []
    for which, _, size, by_x in UNITS:
        scratch += scatter_scratch(UNIT_ROWS[which], size, which != 0)
        if which != 3 and not by_x:
            scratch += line_scratch(UNIT_ROWS[which], size)
    in_vmem = (tok, lse, *vectors, lhs, sc, rhs, mean, up_w)
    in_hbm = (att, h0, cot) + tuple(big)
    return pl.pallas_call(
        functools.partial(mega_kernel, per, PLAN),
        in_specs=[vmem] * len(in_vmem) + [hbm] * len(in_hbm),
        out_specs=[hbm] + [vmem] * 7,
        out_shape=[
            jax.ShapeDtypeStruct((rows, D), f32),
            jax.ShapeDtypeStruct((share, D), f32),
            jax.ShapeDtypeStruct((share, FF), f32),
            jax.ShapeDtypeStruct((4 * share, D), f32),
            jax.ShapeDtypeStruct((blk_n, 32, 3 * SLOT), bf16),
            jax.ShapeDtypeStruct((dp_n, 8, half), f32),
            jax.ShapeDtypeStruct((8, 256), f32),
            jax.ShapeDtypeStruct((16, rows), f32),
        ],
        scratch_shapes=[
            VMEM((2, 2, 2, 384, D), bf16),
            VMEM((2, 2, 2, 96, FF), bf16),
            VMEM((2, 2, 2, 96, D), bf16),
            VMEM((2, 2, 2, 96, 3 * SLOT), bf16),
            VMEM((rows, D), f32),
            VMEM((blk_n, rows, SLOT), bf16),
            VMEM((blk_n, rows, SLOT), bf16),
            VMEM((8, D), f32),
            pltpu.SemaphoreType.DMA((blk_n,)),
            pltpu.SemaphoreType.DMA((blk_n,)),
            VMEM((2, 2, 384, D), bf16),
            pltpu.SemaphoreType.DMA((4,)),
            pltpu.SemaphoreType.DMA((4,)),
            VMEM((dp_n, 8, half + 256), f32),
            VMEM((dp_n, 8, half + 256), f32),
            VMEM((8, half + 256), f32),
            VMEM((blk_n, 8, half + 256), f32),
            VMEM((8, half), f32),
            VMEM((blk_n, 32, 3 * SLOT), bf16),
            VMEM((blk_n, 16, rows), bf16),
            VMEM((blk_n, 16, rows), bf16),
            pltpu.SemaphoreType.DMA((count,)),
            pltpu.SemaphoreType.DMA((count,)),
            *scratch,
        ],
        compiler_params=pltpu.CompilerParams(
            vmem_limit_bytes=63 * MIB, collective_id=1, has_side_effects=True
        ),
        name="layer_and_sums",
    )(*in_vmem, *in_hbm)


def finish_kernel(
    per, dwo_ref, dw1_ref, dw2_ref, dw_ref, flat_ref, table_sum_ref, noise_ref, mean_ref, table_ref, block_hbm,
    block_out, noise_out, table_out, up_w_out, up_b_out, gain1_out, shift1_out, qkv_out, qb_out, vb_out, dwo_out,
    out_b_out, gain2_out, shift2_out, dw1_out, b1_out, dw2_out, b2_out, mean_out, buffer, sems,
):
    load = pltpu.make_async_copy(block_hbm, buffer, sems.at[0])
    store = pltpu.make_async_copy(buffer, block_out, sems.at[1])
    load.start()
    blk_n = dw_ref.shape[0]
    vocab = table_ref.shape[1] * flat_ref.shape[0]
    load.wait()
    store.start()
    width = per * HEAD_DIM
    share = dwo_ref.shape[0]
    flat = [jnp.concatenate([flat_ref[n], flat_ref[4 + n]], axis=1) for n in range(4)]
    noise_out[...] = noise_ref[...]
    dwo_out[...] = dwo_ref[...]
    dw1_out[...] = dw1_ref[...]
    dw2_out[...] = dw2_ref[...]
    out_b_out[...] = flat[0][0]
    gain2_out[...] = flat[0][1]
    shift2_out[...] = flat[0][2]
    b2_out[...] = flat[0][3]
    for n in range(4):
        b1_out[pl.ds(n * D, D)] = flat[0][4 + n]
    up_w_out[:8, :] = flat[1]
    up_w_out[8:, :] = flat[2]
    up_b_out[...] = flat[3][0]
    gain1_out[...] = flat[3][1]
    shift1_out[...] = flat[3][2]
    for n in range(3):
        parts = [dw_ref[k].astype(f32)[:share, n * SLOT : n * SLOT + width] for k in range(blk_n)]
        qkv_out[:, n * D : (n + 1) * D] = jnp.concatenate(parts, axis=1)
    for n, out in ((0, qb_out), (2, vb_out)):
        parts = [flat[3][4 + k : 5 + k, n * SLOT : n * SLOT + width] for k in range(blk_n)]
        out[...] = jnp.concatenate(parts, axis=1)[0]
    table = table_ref[...]
    norms = jnp.sqrt(jnp.sum(table * table, axis=0, keepdims=True) + 1.0)
    total = jnp.concatenate([table_sum_ref[:, :128], table_sum_ref[:, 128:]], axis=0)
    table_out[...] = total[:, : table.shape[1]] + flat[3][3:4, :1] * table / (vocab * norms)
    mean_out[...] = mean_ref[0:1, 0:1]
    store.wait()


def finish(per, dwo, dw1, dw2, dw, flat, table_sum, noise, mean, table, block):
    vmem = pl.BlockSpec(memory_space=VMEM)
    hbm = pl.BlockSpec(memory_space=pl.ANY)
    vector = jax.ShapeDtypeStruct((D,), f32)
    share = dwo.shape[0]
    like = lambda x: jax.ShapeDtypeStruct(x.shape, x.dtype)
    shapes = [
        like(block), like(noise), like(table), jax.ShapeDtypeStruct((16, D), f32), vector, vector, vector,
        jax.ShapeDtypeStruct((share, 3 * D), f32), vector, vector, like(dwo), vector, vector, vector, like(dw1),
        jax.ShapeDtypeStruct((FF,), f32), like(dw2), vector, jax.ShapeDtypeStruct((1, 1), f32),
    ]
    return pl.pallas_call(
        functools.partial(finish_kernel, per),
        in_specs=[vmem] * 9 + [hbm],
        out_specs=[hbm] + [vmem] * 18,
        out_shape=shapes,
        scratch_shapes=[VMEM(block.shape, f32), pltpu.SemaphoreType.DMA((2,))],
        compiler_params=params(),
        name="finish",
    )(dwo, dw1, dw2, dw, flat, table_sum, noise, mean, table, block)


def shards(
    dp_n,
    blk_n,
    token_ids,
    segment_ids,
    timesteps,
    noise,
    table,
    up_weight,
    up_bias,
    norm1_gain,
    norm1_shift,
    qkv_weight,
    query_bias,
    value_bias,
    out_weight,
    out_bias,
    norm2_gain,
    norm2_shift,
    ffn_in_weight,
    ffn_in_bias,
    ffn_out_weight,
    ffn_out_bias,
    cotangent,
):
    rows = token_ids.shape[0]
    local_rows = table.shape[0]
    vp = -(-local_rows // 128) * 128
    per = -(-HEADS // blk_n)
    width = per * HEAD_DIM
    z = lax.axis_index("blk")
    z1 = z.reshape(1).astype(jnp.int32)
    vectors = (up_bias, norm1_gain, norm1_shift, query_bias, value_bias)

    if dp_n == 8 and blk_n == 4:
        tok, tab = gather(token_ids, segment_ids, timesteps, noise.T, table.T, dp_n, blk_n)
        own, normed, lhs, sc, h0, rhs, mean, own_w, att, lse = front(
            z1, tok, tab, up_weight, vectors, qkv_weight, local_rows, per
        )
        vectors = (norm1_gain, out_bias, norm2_gain, norm2_shift, ffn_out_bias, ffn_in_bias)
        block_out, dwo, dw1, dw2, dw, flat, table_sum, noise_sum = mega(
            (tok, att, lse, h0, cotangent, vectors, lhs, sc, rhs, mean, up_weight),
            (out_weight, ffn_in_weight, ffn_out_weight, own, normed, own_w),
            dp_n,
            per,
        )
        outs = list(finish(per, dwo, dw1, dw2, dw, flat, table_sum, noise_sum, mean, table.T, block_out))
        outs[1] = outs[1].T
        outs[2] = outs[2].T
        outs[-1] = outs[-1].reshape(())
        return tuple(outs)

    slots = (token_ids // local_rows) * vp + token_ids % local_rows
    scalars = jnp.stack([slots, segment_ids, timesteps]).astype(f32)
    mine = jnp.concatenate([noise.T, scalars, jnp.zeros((5, rows), f32)], axis=0)
    tok = lax.all_gather(mine, "blk")
    tab = lax.all_gather(jnp.pad(table.T, ((0, 0), (0, vp - local_rows))), "dp")
    padded = blk_n * width
    split = jnp.pad(qkv_weight.reshape(D, 3, D), ((0, 0), (0, 0), (0, padded - D)))
    own_w = lax.dynamic_slice(split, (0, 0, z * width), (D, 3, width))
    own_w = jnp.pad(own_w, ((0, 0), (0, 0), (0, SLOT - width))).reshape(D, 3 * SLOT)
    bias = jnp.pad(jnp.stack([query_bias, jnp.zeros((D,), f32), value_bias]), ((0, 0), (0, padded - D)))
    own_b = lax.dynamic_slice(bias, (0, z * width), (3, width))
    own_b = jnp.pad(own_b, ((0, 0), (0, SLOT - width))).reshape(1, 3 * SLOT)
    k, vt, own, normed, lhs, sc, qt, h0, rhs, mean = embed(
        z1, tok, tab, up_weight, vectors, qkv_weight, local_rows, own_w, own_b
    )
    vec1 = jnp.stack([up_bias, norm1_gain, norm1_shift])
    vec2 = jnp.stack([out_bias, norm2_gain, norm2_shift, ffn_out_bias])
    b1 = ffn_in_bias.reshape(FF // D, D)
    share = D // (dp_n * blk_n)
    block_out, h1g, msg, dwo, dw1, dw2, small1 = layer(
        tok, mine, k, vt, qt, h0, cotangent, vec2, b1, out_weight, ffn_in_weight, ffn_out_weight, per
    )
    msg = lax.all_to_all(msg, "blk", 0, 0)
    grad = back(tok, own, msg, per)
    dw, noise_part, table_part, small2 = final(
        z1, tok, grad, normed, lhs, sc, rhs, h1g, up_weight, vec1, own_w, mean, dp_n * vp
    )
    noise_grad = lax.psum_scatter(noise_part, "blk", scatter_dimension=0, tiled=False).T
    own_sums = small2[19].reshape(3, SLOT)[:, :width]
    own_sums = lax.dynamic_update_slice(jnp.zeros((3, padded), f32), own_sums, (0, z * width))[:, :D]
    small2, table_total, small1, own_sums = lax.psum((small2, table_part, small1, own_sums), ("dp", "blk"))
    scatter = functools.partial(lax.psum_scatter, axis_name=("dp", "blk"), scatter_dimension=0, tiled=True)
    dwo, dw1, dw2 = scatter(dwo), scatter(dw1), scatter(dw2)
    dw = lax.psum_scatter(dw, "dp", scatter_dimension=0, tiled=True)
    dw = lax.all_to_all(dw.reshape(blk_n, share, 3 * SLOT), "blk", 0, 0)
    dw = dw.reshape(blk_n, share, 3, SLOT)[..., :width].transpose(1, 2, 0, 3).reshape(share, 3, padded)[..., :D]
    table_grad = lax.dynamic_slice(table_total, (0, lax.axis_index("dp") * vp), (16, local_rows)).T
    norms = jnp.sqrt(jnp.sum(table * table, axis=-1, keepdims=True) + 1.0)
    table_grad = table_grad + small2[20, 0] * table / (dp_n * local_rows * norms)
    return (
        block_out,
        noise_grad,
        table_grad,
        small2[:16],
        small2[16],
        small2[17],
        small2[18],
        dw.reshape(share, 3 * D).astype(f32),
        own_sums[0],
        own_sums[2],
        dwo.astype(f32),
        small1[0],
        small1[1],
        small1[2],
        dw1.astype(f32),
        small1[4:8].reshape(FF),
        dw2.astype(f32),
        small1[3],
        mean[0, 0],
    )


def solution(mesh):
    rows = P(("dp", "blk"))
    wide = P(("dp", "blk"), None)
    in_specs = (rows, rows, rows, wide, P("dp", None)) + (P(),) * 15 + (wide,)
    out_specs = (
        (wide, wide, P("dp", None))
        + (P(),) * 4
        + (wide, P(), P(), wide, P(), P(), P(), wide, P(), wide, P(), P())
    )
    body = functools.partial(shards, mesh.shape["dp"], mesh.shape["blk"])
    return jax.shard_map(body, mesh=mesh, in_specs=in_specs, out_specs=out_specs, check_vma=False)
```
